128 devices in a mesh: dp: 4 (over x), fsdp: 32 (over y, z, core).
Axes of the slice: x: 4, y: 4, z: 4, core: 2. Of those that a mesh axis runs over, the one named last changes fastest.
Arguments:
- tokens: bfloat16 [16384, 1536], P(('dp', 'fsdp')), may hold values from -6 to 6
- cotangent: bfloat16 [16384, 1536], P(('dp', 'fsdp')), may hold values from -6 to 6
- lengths: int32 [128], P(('dp', 'fsdp')), may hold values from 1 to 128, as said below
- attn_weights: float32 [5, 1536, 1536], P(None, ('dp', 'fsdp'))
- attn_rows: float32 [5, 1536], P(None, ('dp', 'fsdp')), may hold values from 49.152 to 1638.4
- attn_cols: float32 [5, 1536], replicated, may hold values from 49.152 to 1638.4
- ffn_weights: float32 [2, 1536, 4096], P(None, ('dp', 'fsdp')), may hold values from -0.15625 to 0.15625
- ffn_rows: float32 [2, 1536], P(None, ('dp', 'fsdp')), may hold values from 327.68 to 2457.6
- ffn_cols: float32 [2, 4096], replicated, may hold values from 327.68 to 2457.6
- down_weight: float32 [4096, 1536], P(('dp', 'fsdp')), may hold values from -0.09375 to 0.09375
- down_rows: float32 [4096], P(('dp', 'fsdp')), may hold values from 1638.4 to 9830.4
- down_cols: float32 [1536], replicated, may hold values from 1638.4 to 9830.4
- small_params: float32 [40088], replicated
- small_moments: float32 [40088], replicated, may hold values from 81.92 to 8192
Outputs:
- block_out: bfloat16 [16384, 1536], P(('dp', 'fsdp'))
- input_grad: float32 [16384, 1536], P(('dp', 'fsdp'))
- attn_grad: float32 [5, 1536, 1536], P(None, ('dp', 'fsdp'))
- attn_new: float32 [5, 1536, 1536], P(None, ('dp', 'fsdp'))
- attn_copy: bfloat16 [5, 1536, 1536], P(None, ('dp', 'fsdp'))
- attn_rows_new: float32 [5, 1536], P(None, ('dp', 'fsdp'))
- attn_cols_new: float32 [5, 1536], replicated
- ffn_grad: float32 [2, 1536, 4096], P(None, ('dp', 'fsdp'))
- ffn_new: float32 [2, 1536, 4096], P(None, ('dp', 'fsdp'))
- ffn_copy: bfloat16 [2, 1536, 4096], P(None, ('dp', 'fsdp'))
- ffn_rows_new: float32 [2, 1536], P(None, ('dp', 'fsdp'))
- ffn_cols_new: float32 [2, 4096], replicated
- down_grad: float32 [4096, 1536], P(('dp', 'fsdp'))
- down_new: float32 [4096, 1536], P(('dp', 'fsdp'))
- down_copy: bfloat16 [4096, 1536], P(('dp', 'fsdp'))
- down_rows_new: float32 [4096], P(('dp', 'fsdp'))
- down_cols_new: float32 [1536], replicated
- small_grad: float32 [40088], replicated
- small_new: float32 [40088], replicated
- small_moments_new: float32 [40088], replicated
The draws below stay inside these ranges and needn't reach their ends.
Inputs may be any that keep to these rules, and one draw needn't show every extreme that they name: Each sequence's first lengths entry of its 128 slots are real tokens and the rest padding; some sequence fills all 128 slots.
All inputs are finite; a program needn't handle non-finite values.
Results may differ from the reference program's by a relative error of at most 0.015.
The reference program's roundings to bfloat16 on the way count: a program that leaves them out, or rounds other values in their place, can miss the bound.
Values may be sent and summed in bfloat16 or wider, within the bound.
No kernel may reach another device: no remote copies, remote signals or barrier semaphores. Data moves between devices by JAX's collectives and lax.ppermute only.
A program may use at most 384 MiB of HBM per device.

```python
import math
import jax
import jax.numpy as jnp
from jax import lax

D = 1536
H = 24
HD = 64
FF = 4096
TOK_DEV = 128
TOKENS = 16384
SMALL = 40088
N_DP = 4
N_FSDP = 32


def draw_lengths(key, part):
    key = jax.random.fold_in(key, 5)
    devices = N_DP * N_FSDP
    slot_ids = jnp.arange(devices, dtype=jnp.int32)
    outer_part = slot_ids // N_FSDP
    inner_part = slot_ids % N_FSDP
    ramp_value = TOK_DEV * (N_FSDP - 1 + 2 * inner_part) * (N_DP - 1 + 2 * outer_part) // (8 * (N_FSDP - 1) * (N_DP - 1))
    jitter = jax.random.randint(key, (devices,), 0, TOK_DEV // 8 + 1, dtype=jnp.int32)
    lengths = jnp.clip(ramp_value - jitter, 1, TOK_DEV)
    return jnp.where(slot_ids == devices - 1, TOK_DEV, lengths).astype(jnp.int32)


def draw_attn_weights(key, part):
    key = jax.random.fold_in(key, 7)
    raw_draw = jax.random.truncated_normal(key, -4.0, 4.0, (5, D, D), jnp.float32)
    factors = jnp.array([1.0, 1.0, 1.0, 1.0, 8.0], jnp.float32)
    return raw_draw * factors[:, None, None] * D ** (-0.5)


def rising_gain(key, steepness, noise_low, noise_high):
    row_ids = jnp.arange(D, dtype=jnp.int32)
    block_rows = D // N_DP
    outer_part = (row_ids // block_rows).astype(jnp.float32) / max(N_DP - 1, 1)
    inner_part = (row_ids % block_rows).astype(jnp.float32) / max(block_rows - 1, 1)
    noise_factor = jax.random.uniform(key, (D,), jnp.float32, noise_low, noise_high)
    return 0.5 * (1.0 + steepness * inner_part) * (1.0 + steepness * outer_part) * noise_factor


def draw_small_params(key, part):
    key = jax.random.fold_in(key, 9)
    keys_list = jax.random.split(key, 7)
    head_order = jax.random.permutation(keys_list[4], H)
    rank_share = head_order.astype(jnp.float32) / max(H - 1, 1)
    wobble = jax.random.uniform(keys_list[5], (H,), jnp.float32, -0.3, 0.3)
    gain_one = rising_gain(keys_list[0], 0.73, 0.85, 1.15)
    gain_two = rising_gain(keys_list[1], 0.73, 0.85, 1.15)
    query_gain = jax.random.uniform(keys_list[2], (HD,), jnp.float32, 0.8, 1.4)
    key_gain = jax.random.uniform(keys_list[3], (HD,), jnp.float32, 0.8, 1.4)
    forget_bias = 2.5 + 4.5 * rank_share + wobble
    forget_weight = jax.random.truncated_normal(keys_list[6], -4.0, 4.0, (D * H,), jnp.float32) * D ** (-0.5)
    return jnp.concatenate([gain_one, gain_two, query_gain, key_gain, forget_bias, forget_weight])


def block_levels(rng, shape, cuts, smallest, largest):
    gain, own = 1.0, jax.random.fold_in(rng, 6)
    for axis_at, blocks in cuts:
        draws = jnp.exp(jax.random.uniform(jax.random.fold_in(own, axis_at), (blocks,), jnp.float32, smallest / len(cuts), largest / len(cuts)))
        gain = gain * jnp.repeat(draws, shape[axis_at] // blocks).reshape([-1 if axis == axis_at else 1 for axis in range(len(shape))])
    return gain


def normal_values(key, shape, scale, bound, shards=(), held_as=jnp.bfloat16):
    drawn = jax.random.normal(key, shape, jnp.float32) * scale
    if len(shards) > 0:
        drawn = block_levels(key, shape, shards, -0.22, 0.18) * drawn
    return jnp.clip(drawn, min=-bound, max=bound).astype(held_as)


def setup_inputs(seed: int = 0) -> dict:
    key_of = jax.random.split(jax.random.key(seed), 15)
    return {
        "tokens": normal_values(key_of[0], (TOKENS, D), 1.0, 6.0, ((0, 128),)),
        "cotangent": normal_values(key_of[1], (TOKENS, D), 1.0, 6.0, ((0, 128),)),
        "lengths": draw_lengths(jax.random.fold_in(key_of[14], 71), 0),
        "attn_weights": draw_attn_weights(jax.random.fold_in(key_of[14], 71), 0),
        "attn_rows": jnp.clip(jnp.exp(math.log(1638.4) - 3.506558 * jax.random.uniform(key_of[4], (5, D), jnp.float32) ** block_levels(key_of[4], (5, D), ((1, 128),), -0.2, 0.2)), 49.152, 1638.4),
        "attn_cols": jnp.clip(jnp.exp(jax.random.uniform(key_of[5], (5, D), jnp.float32, math.log(49.152), math.log(1638.4))), 49.152, 1638.4),
        "ffn_weights": normal_values(key_of[6], (2, D, FF), D ** -0.5, 0.15625, ((1, 128),), jnp.float32),
        "ffn_rows": jnp.clip(jnp.exp(math.log(2457.6) - 2.014903 * jax.random.uniform(key_of[7], (2, D), jnp.float32) ** block_levels(key_of[7], (2, D), ((1, 128),), -0.2, 0.2)), 327.68, 2457.6),
        "ffn_cols": jnp.clip(jnp.exp(jax.random.uniform(key_of[8], (2, FF), jnp.float32, math.log(327.68), math.log(2457.6))), 327.68, 2457.6),
        "down_weight": normal_values(key_of[9], (FF, D), FF ** -0.5, 0.09375, ((0, 128),), jnp.float32),
        "down_rows": jnp.clip(jnp.exp(math.log(9830.4) - 1.7917595 * jax.random.uniform(key_of[10], (FF,), jnp.float32) ** block_levels(key_of[10], (FF,), ((0, 128),), -0.2, 0.2)), 1638.4, 9830.4),
        "down_cols": jnp.clip(jnp.exp(jax.random.uniform(key_of[11], (D,), jnp.float32, math.log(1638.4), math.log(9830.4))), 1638.4, 9830.4),
        "small_params": draw_small_params(jax.random.fold_in(key_of[14], 71), 0),
        "small_moments": jnp.clip(jnp.exp(jax.random.uniform(key_of[13], (SMALL,), jnp.float32, math.log(81.92), math.log(8192.0))), 81.92, 8192.0),
    }


@jax.custom_vjp
def low(v):
    return lax.optimization_barrier(v.astype(jnp.bfloat16)).astype(jnp.float32)

@jax.custom_vjp
def low_back(v):
    return v

def low_keep(v):
    return (low(v), None)

def low_pass(kept, grad):
    return (grad,)

def back_keep(v):
    return (v, None)

def back_low(kept, grad):
    return (low(grad),)
low.defvjp(low_keep, low_pass)
low_back.defvjp(back_keep, back_low)
BETA = 0.5
CLIP = 0.1
RATE = 3.0
EPS_NORM = 1e-06
EPS_STAT = 1e-30
NEG_FILL = -1e+30

def matmul(left_side, right_side):
    return jnp.dot(left_side, right_side, precision=lax.Precision.HIGHEST)

def rms_norm(values):
    return values * lax.rsqrt(lax.optimization_barrier(jnp.mean(values * values, axis=-1, keepdims=True)) + EPS_NORM)

def split_small(vector):
    widths = [D, D, HD, HD, H]
    pieces = []
    offset = 0
    for piece_width in widths:
        pieces.append(vector[offset:offset + piece_width])
        offset = offset + piece_width
    pieces.append(vector[offset:].reshape(D, H))
    return pieces

def attend_packed(bundle):
    query_heads, key_heads, value_heads, log_forget, valid_keys = bundle
    length = query_heads.shape[0]
    score_scale = query_heads.shape[-1] ** (-0.5)
    cumulative = jnp.cumsum(log_forget, axis=0)
    raw_scores = jnp.einsum('thd,shd->hts', query_heads, key_heads, precision=lax.Precision.HIGHEST) * score_scale
    raw_scores = raw_scores + cumulative.T[:, :, None] - cumulative.T[:, None, :]
    scores = low_back(raw_scores)
    positions = jnp.arange(length, dtype=jnp.int32)
    allowed = (positions[None, :] <= positions[:, None]) & valid_keys[None, :]
    scores = jnp.where(allowed[None], scores, NEG_FILL)
    highest = lax.optimization_barrier(jnp.max(scores, axis=-1, keepdims=True))
    weights = jnp.exp(scores - highest)
    probabilities = weights / lax.optimization_barrier(jnp.sum(weights, axis=-1, keepdims=True))
    return jnp.einsum('hts,shd->thd', low(probabilities), value_heads, precision=lax.Precision.HIGHEST)

def block_forward(inputs, attn_weights, ffn_weights, down_weight, small_params, valid_rows):
    gain_one, gain_two, query_gain, key_gain, forget_bias, forget_weight = split_small(small_params)
    rows_total = inputs.shape[0]
    sequences = rows_total // TOK_DEV
    hidden_one = low(rms_norm(inputs) * gain_one)
    matrices = [low(attn_weights[matrix_id]) for matrix_id in range(5)]
    query_raw = low_back(matmul(hidden_one, matrices[0]))
    key_raw = low_back(matmul(hidden_one, matrices[1]))
    value_heads = low(low_back(matmul(hidden_one, matrices[2]))).reshape(rows_total, H, HD)
    gate_raw = low_back(matmul(hidden_one, matrices[3]))
    forget_raw = low_back(matmul(hidden_one, low(forget_weight)))
    log_forget = -jnp.log1p(jnp.exp(-(forget_raw + forget_bias)))
    query_heads = low(rms_norm(query_raw.reshape(rows_total, H, HD)) * query_gain)
    key_heads = low(rms_norm(key_raw.reshape(rows_total, H, HD)) * key_gain)

    def to_blocks(array_in):
        return array_in.reshape((sequences, TOK_DEV) + array_in.shape[1:])
    attended = lax.map(jax.checkpoint(attend_packed), (to_blocks(query_heads), to_blocks(key_heads), to_blocks(value_heads), to_blocks(log_forget), to_blocks(valid_rows)))
    attended = low_back(attended.reshape(rows_total, D))
    gated_out = low(attended * lax.logistic(gate_raw))
    mixed_sum = inputs + low_back(matmul(gated_out, matrices[4]))
    hidden_two = low(rms_norm(mixed_sum) * gain_two)
    gate_part = low_back(matmul(hidden_two, low(ffn_weights[0])))
    up_part = low_back(matmul(hidden_two, low(ffn_weights[1])))
    activated = low(gate_part * lax.logistic(gate_part) * up_part)
    return mixed_sum + low_back(matmul(activated, low(down_weight)))

def factored(weight, grad_value, rows_old, cols_old):
    squares = grad_value * grad_value
    rows_new = BETA * rows_old + (1.0 - BETA) * (lax.optimization_barrier(jnp.mean(squares, axis=1)) + EPS_STAT)
    cols_new = BETA * cols_old + (1.0 - BETA) * (lax.optimization_barrier(jnp.mean(squares, axis=0)) + EPS_STAT)
    second = rows_new[:, None] * cols_new[None, :] / jnp.mean(rows_new)
    update = grad_value * lax.rsqrt(second)
    clip_ratio = jnp.sqrt(jnp.mean(update * update)) / CLIP
    update = update / jnp.maximum(1.0, clip_ratio)
    spread = jnp.sqrt(jnp.mean(weight * weight) + EPS_NORM)
    return (weight - RATE * spread * update, rows_new, cols_new)

def plain_update(param_part, grad_part, moment_part):
    moment_new = BETA * moment_part + (1.0 - BETA) * (grad_part * grad_part + EPS_STAT)
    update = grad_part * lax.rsqrt(moment_new)
    clip_ratio = jnp.sqrt(jnp.mean(update * update)) / CLIP
    update = update / jnp.maximum(1.0, clip_ratio)
    spread = jnp.sqrt(jnp.mean(param_part * param_part) + EPS_NORM)
    return (param_part - RATE * spread * update, moment_new)

def small_update(params_all, grads_all, moments_all):
    widths = [D, D, HD, HD, H, D * H]
    new_parts = []
    moment_parts = []
    offset = 0
    for piece_width in widths:
        fresh, moment_new = plain_update(params_all[offset:offset + piece_width], grads_all[offset:offset + piece_width], moments_all[offset:offset + piece_width])
        new_parts.append(fresh)
        moment_parts.append(moment_new)
        offset = offset + piece_width
    return (jnp.concatenate(new_parts), jnp.concatenate(moment_parts))

def reference(tokens, cotangent, lengths, attn_weights, attn_rows, attn_cols, ffn_weights, ffn_rows, ffn_cols, down_weight, down_rows, down_cols, small_params, small_moments):
    inputs = tokens.astype(jnp.float32)
    slot_ids = jnp.arange(TOKENS, dtype=jnp.int32)
    valid_rows = slot_ids % TOK_DEV < lengths[slot_ids // TOK_DEV]

    def forward(inputs_in, attn_in, ffn_in, down_in, small_in):
        return block_forward(inputs_in, attn_in, ffn_in, down_in, small_in, valid_rows)
    outputs, pullback = jax.vjp(forward, inputs, attn_weights, ffn_weights, down_weight, small_params)
    seed_grad = cotangent.astype(jnp.float32) * valid_rows[:, None].astype(jnp.float32)
    input_grad, attn_grad, ffn_grad, down_grad, small_grad = pullback(seed_grad)
    attn_results = [factored(attn_weights[matrix_id], attn_grad[matrix_id], attn_rows[matrix_id], attn_cols[matrix_id]) for matrix_id in range(5)]
    ffn_results = [factored(ffn_weights[matrix_id], ffn_grad[matrix_id], ffn_rows[matrix_id], ffn_cols[matrix_id]) for matrix_id in range(2)]
    down_new, down_rows_new, down_cols_new = factored(down_weight, down_grad, down_rows, down_cols)
    attn_new = jnp.stack([member[0] for member in attn_results])
    ffn_new = jnp.stack([member[0] for member in ffn_results])
    small_new, small_moments_new = small_update(small_params, small_grad, small_moments)
    return (outputs.astype(jnp.bfloat16), input_grad, attn_grad, attn_new, attn_new.astype(jnp.bfloat16), jnp.stack([member[1] for member in attn_results]), jnp.stack([member[2] for member in attn_results]), ffn_grad, ffn_new, ffn_new.astype(jnp.bfloat16), jnp.stack([member[1] for member in ffn_results]), jnp.stack([member[2] for member in ffn_results]), down_grad, down_new, down_new.astype(jnp.bfloat16), down_rows_new, down_cols_new, small_grad, small_new, small_moments_new)
```

```python
import jax
import jax.numpy as jnp
from jax import lax
from jax.sharding import Mesh
from jax.sharding import PartitionSpec as P

D = 1536
H = 24
HD = 64
FF = 4096
SEQ = 128
HALF = D // 2
HEADS = H // 2
GROUP = 8
PLANE = 16
CHIPS = 64
DEVICES = 128
FF_PART = FF // GROUP

BETA = 0.5
CLIP = 0.1
RATE = 3.0
EPS_NORM = 1e-06
EPS_STAT = 1e-30
NEG_FILL = -1e30
LOW = jnp.bfloat16
WIDE = jnp.float32

ALL = ("x", "y", "z", "c")
XYZ = ("x", "y", "z")
XY = ("x", "y")
ZC = ("z", "c")


def dot_plain(left_side, right_side):
    return jnp.dot(left_side, right_side, preferred_element_type=WIDE)


def dot_right_t(left_side, right_side):
    return lax.dot_general(
        left_side, right_side, (((1,), (1,)), ((), ())), preferred_element_type=WIDE
    )


def dot_left_t(left_side, right_side):
    return lax.dot_general(
        left_side, right_side, (((0,), (0,)), ((), ())), preferred_element_type=WIDE
    )


def inverse_rms(values):
    return lax.rsqrt(jnp.mean(values * values, axis=-1, keepdims=True) + EPS_NORM)


def norm_back(normed, inverse, grad_out):
    return inverse * (grad_out - normed * jnp.mean(grad_out * normed, axis=-1, keepdims=True))


def split_small(vector):
    widths = [D, D, HD, HD, H]
    pieces = []
    offset = 0
    for piece_width in widths:
        pieces.append(vector[offset : offset + piece_width])
        offset = offset + piece_width
    pieces.append(vector[offset:].reshape(D, H))
    return pieces


def plain_update(param_part, grad_part, moment_part):
    moment_new = BETA * moment_part + (1.0 - BETA) * (grad_part * grad_part + EPS_STAT)
    update = grad_part * lax.rsqrt(moment_new)
    clip_ratio = jnp.sqrt(jnp.mean(update * update)) / CLIP
    update = update / jnp.maximum(1.0, clip_ratio)
    spread = jnp.sqrt(jnp.mean(param_part * param_part) + EPS_NORM)
    return (param_part - RATE * spread * update, moment_new)


def small_update(params_all, grads_all, moments_all):
    widths = [D, D, HD, HD, H, D * H]
    new_parts = []
    moment_parts = []
    offset = 0
    for piece_width in widths:
        fresh, moment_new = plain_update(
            params_all[offset : offset + piece_width],
            grads_all[offset : offset + piece_width],
            moments_all[offset : offset + piece_width],
        )
        new_parts.append(fresh)
        moment_parts.append(moment_new)
        offset = offset + piece_width
    return (jnp.concatenate(new_parts), jnp.concatenate(moment_parts))


def local_stats(weight, grad_value, rows_old):
    squares = grad_value * grad_value
    rows_new = BETA * rows_old + (1.0 - BETA) * (jnp.mean(squares, axis=2) + EPS_STAT)
    return (
        rows_new,
        jnp.sum(squares, axis=1),
        jnp.sum(rows_new, axis=1),
        jnp.sum(weight * weight, axis=(1, 2)),
        jnp.sum(squares / rows_new[:, :, None], axis=1),
    )


def factor_update(grad_value, rows_new, cols_old, column_sum, row_sum, all_rows):
    cols_new = BETA * cols_old + (1.0 - BETA) * (column_sum / all_rows + EPS_STAT)
    row_mean = row_sum / all_rows
    second = rows_new[:, :, None] * cols_new[:, None, :] / row_mean[:, None, None]
    return (cols_new, row_mean, grad_value * lax.rsqrt(second))


def apply_step(weight, update, mean_square, weight_sum, entries):
    clip_ratio = jnp.sqrt(mean_square) / CLIP
    clipped = update / jnp.maximum(1.0, clip_ratio)[:, None, None]
    spread = jnp.sqrt(weight_sum / entries + EPS_NORM)
    return weight - RATE * spread[:, None, None] * clipped


def swap_core(value):
    return lax.ppermute(value, "c", [(0, 1), (1, 0)])


def reduce_core(part, core):
    keep = lax.dynamic_index_in_dim(part, core, 0, keepdims=False)
    send = lax.dynamic_index_in_dim(part, 1 - core, 0, keepdims=False)
    return keep + swap_core(send)


def gather_group(value):
    return lax.all_gather(value, ZC, axis=0, tiled=True)


def scatter_group(part):
    return lax.psum_scatter(
        part.astype(LOW).reshape(GROUP, SEQ, D), ZC, scatter_dimension=0, tiled=False
    ).astype(WIDE)


def sum_everywhere(vectors):
    sizes = [vector.size for vector in vectors]
    flat = jnp.concatenate([vector.reshape(-1) for vector in vectors])
    width = -(-flat.size // (DEVICES * 128)) * 128
    flat = jnp.pad(flat, (0, DEVICES * width - flat.size)).reshape(DEVICES, width // 128, 128)
    mine = jnp.sum(lax.all_to_all(flat, ALL, 0, 0, tiled=True), axis=0)
    spread = jnp.broadcast_to(mine[None], flat.shape)
    whole = lax.all_to_all(spread, ALL, 0, 0, tiled=True).reshape(-1)
    parts = []
    offset = 0
    for vector, size in zip(vectors, sizes):
        parts.append(whole[offset : offset + size].reshape(vector.shape))
        offset = offset + size
    return parts


def shards(
    tokens,
    cotangent,
    lengths,
    attn_weights,
    attn_rows,
    attn_cols,
    ffn_weights,
    ffn_rows,
    ffn_cols,
    down_weight,
    down_rows,
    down_cols,
    small_params,
    small_moments,
):
    core = lax.axis_index("c")
    inputs = tokens.astype(WIDE)
    slot_ids = jnp.arange(SEQ, dtype=jnp.int32)
    valid_rows = slot_ids < lengths[0]
    lengths_pair = lax.all_gather(lengths.astype(WIDE), "c", axis=0, tiled=True)
    valid_keys = slot_ids[None, :].astype(WIDE) < lengths_pair[:, None]
    gain_one, gain_two, query_gain, key_gain, forget_bias, forget_weight = split_small(small_params)
    forget_low = lax.dynamic_slice_in_dim(forget_weight, core * HEADS, HEADS, axis=1).astype(LOW)
    bias_mine = lax.dynamic_slice_in_dim(forget_bias, core * HEADS, HEADS, axis=0)

    attn_low = jnp.moveaxis(attn_weights.astype(LOW).reshape(5, 12, 2, HALF), 2, 0)
    attn_low = jnp.moveaxis(attn_low, 1, 2).reshape(2, 12, 5 * HALF)
    attn_pair = lax.all_to_all(attn_low, "c", 0, 0, tiled=True).reshape(24, 5 * HALF)
    attn_full = lax.all_gather(attn_pair, XYZ, axis=0, tiled=True)
    proj_full = attn_full[:, : 4 * HALF]
    out_rows = lax.all_to_all(attn_full[:, 4 * HALF :], "c", 0, 1, tiled=True)

    pair_low = ffn_weights.astype(LOW).reshape(2, 12, PLANE, GROUP, 32)
    pair_low = pair_low.transpose(3, 0, 1, 2, 4).reshape(GROUP, 2, 12, FF_PART)
    pair_low = lax.all_to_all(pair_low, ZC, 0, 0, tiled=True)
    pair_low = jnp.moveaxis(pair_low, 0, 1).reshape(2 * 96, FF_PART)
    down_low = jnp.moveaxis(down_weight.astype(LOW).reshape(32, 3, 512), 1, 0).reshape(96, 512)
    ffn_full = lax.all_gather(jnp.concatenate([pair_low, down_low]), XY, axis=0, tiled=False)
    gate_full = ffn_full[:, :96].reshape(D, FF_PART)
    up_full = ffn_full[:, 96:192].reshape(D, FF_PART)
    down_full = jnp.moveaxis(ffn_full[:, 192:].reshape(PLANE, 3, 32, 512), 1, 2).reshape(FF_PART, D)

    inverse_one = inverse_rms(inputs)
    normed_one = inputs * inverse_one
    hidden_own = (normed_one * gain_one).astype(LOW)
    hidden_one = lax.all_gather(hidden_own, "c", axis=0, tiled=True)
    seed_grad = cotangent.astype(WIDE) * valid_rows[:, None].astype(WIDE)
    seed_low = gather_group(seed_grad.astype(LOW))

    raw = dot_plain(hidden_one, proj_full)
    query_raw = raw[:, :HALF].reshape(2, SEQ, HEADS, HD)
    key_raw = raw[:, HALF : 2 * HALF].reshape(2, SEQ, HEADS, HD)
    value_low = raw[:, 2 * HALF : 3 * HALF].astype(LOW).reshape(2, SEQ, HEADS, HD)
    gate_raw = raw[:, 3 * HALF :]
    forget_arg = dot_plain(hidden_one, forget_low) + bias_mine
    log_forget = -jnp.log1p(jnp.exp(-forget_arg))
    query_inverse = inverse_rms(query_raw)
    key_inverse = inverse_rms(key_raw)
    query_normed = query_raw * query_inverse
    key_normed = key_raw * key_inverse
    query_low = (query_normed * query_gain).astype(LOW)
    key_low = (key_normed * key_gain).astype(LOW)
    score_scale = HD ** (-0.5)
    cumulative = jnp.cumsum(log_forget.reshape(2, SEQ, HEADS), axis=1).transpose(0, 2, 1)
    allowed = (slot_ids[None, :] <= slot_ids[:, None])[None] & valid_keys[:, None, :]
    scores = (
        jnp.einsum("bthd,bshd->bhts", query_low, key_low, preferred_element_type=WIDE) * score_scale
    )
    scores = scores + cumulative[:, :, :, None] - cumulative[:, :, None, :]
    scores = jnp.where(allowed[:, None], scores, NEG_FILL)
    weights = jnp.exp(scores - jnp.max(scores, axis=-1, keepdims=True))
    probabilities = weights / jnp.sum(weights, axis=-1, keepdims=True)
    prob_low = probabilities.astype(LOW)
    attended = jnp.einsum(
        "bhts,bshd->bthd", prob_low, value_low, preferred_element_type=WIDE
    ).reshape(2 * SEQ, HALF)
    gate_value = lax.logistic(gate_raw)
    gated_out = (attended * gate_value).astype(LOW)
    mixed_sum = inputs + reduce_core(dot_plain(gated_out, out_rows).reshape(2, SEQ, D), core)
    inverse_two = inverse_rms(mixed_sum)
    normed_two = mixed_sum * inverse_two
    hidden_two = gather_group((normed_two * gain_two).astype(LOW))

    gate_part = dot_plain(hidden_two, gate_full)
    up_part = dot_plain(hidden_two, up_full)
    gate_sig = lax.logistic(gate_part)
    activated = (gate_part * gate_sig * up_part).astype(LOW)
    activated_grad = dot_right_t(seed_low, down_full)
    silu_grad = activated_grad * up_part
    gate_part_grad = (
        silu_grad * gate_sig + silu_grad * gate_part * gate_sig * (1.0 - gate_sig)
    ).astype(LOW)
    up_part_grad = (activated_grad * (gate_part * gate_sig)).astype(LOW)
    hidden_two_grad = scatter_group(
        dot_right_t(gate_part_grad, gate_full) + dot_right_t(up_part_grad, up_full)
    )
    block_out = (mixed_sum + scatter_group(dot_plain(activated, down_full))).astype(LOW)
    gate_terms = dot_left_t(hidden_two, gate_part_grad).astype(LOW).reshape(PLANE, 96, 512)
    up_terms = dot_left_t(hidden_two, up_part_grad).astype(LOW).reshape(PLANE, 96, 512)
    down_terms = dot_left_t(activated, seed_low).astype(LOW).reshape(PLANE, 32, 3, 512)
    down_terms = jnp.moveaxis(down_terms, 2, 1).reshape(PLANE, 96, 512)
    ffn_sum = lax.psum_scatter(
        jnp.concatenate([gate_terms, up_terms, down_terms], axis=1),
        XY,
        scatter_dimension=0,
        tiled=False,
    )
    down_grad = jnp.moveaxis(ffn_sum[192:].reshape(3, 32, 512), 0, 1).reshape(32, D).astype(WIDE)
    pair_back = jnp.moveaxis(ffn_sum[:192].reshape(2, GROUP, 12, FF_PART), 1, 0)
    pair_back = lax.all_to_all(pair_back, ZC, 0, 0, tiled=True).reshape(GROUP, 2, 12, PLANE, 32)
    ffn_grad = pair_back.transpose(1, 2, 3, 0, 4).reshape(2, 12, FF).astype(WIDE)

    gain_two_grad = jnp.sum(normed_two * hidden_two_grad, axis=0)
    mixed_grad = seed_grad + norm_back(normed_two, inverse_two, hidden_two_grad * gain_two)
    mixed_low = lax.all_gather(mixed_grad.astype(LOW), "c", axis=0, tiled=True)
    gated_grad = dot_right_t(mixed_low, out_rows)
    attended_grad = (gated_grad * gate_value).astype(LOW).reshape(2, SEQ, HEADS, HD)
    gate_raw_grad = (gated_grad * attended * gate_value * (1.0 - gate_value)).astype(LOW)
    prob_grad = jnp.einsum(
        "bthd,bshd->bhts", attended_grad, value_low, preferred_element_type=WIDE
    )
    row_delta = jnp.sum(probabilities * prob_grad, axis=-1, keepdims=True)
    score_grad = (probabilities * (prob_grad - row_delta)).astype(LOW)
    value_grad = (
        jnp.einsum("bhts,bthd->bshd", prob_low, attended_grad, preferred_element_type=WIDE)
        .astype(LOW)
        .reshape(2 * SEQ, HALF)
    )
    query_low_grad = (
        jnp.einsum("bhts,bshd->bthd", score_grad, key_low, preferred_element_type=WIDE)
        * score_scale
    )
    key_low_grad = (
        jnp.einsum("bhts,bthd->bshd", score_grad, query_low, preferred_element_type=WIDE)
        * score_scale
    )
    score_rows = jnp.sum(score_grad, axis=3, dtype=WIDE)
    score_cols = jnp.sum(score_grad, axis=2, dtype=WIDE)
    log_forget_grad = lax.cumsum(score_rows - score_cols, axis=2, reverse=True)
    log_forget_grad = log_forget_grad.transpose(0, 2, 1).reshape(2 * SEQ, HEADS)
    forget_arg_grad = log_forget_grad * (1.0 - lax.logistic(forget_arg))
    forget_low_grad = forget_arg_grad.astype(LOW)
    query_gain_grad = jnp.sum(query_normed * query_low_grad, axis=(0, 1, 2))
    key_gain_grad = jnp.sum(key_normed * key_low_grad, axis=(0, 1, 2))
    query_raw_grad = norm_back(query_normed, query_inverse, query_low_grad * query_gain)
    key_raw_grad = norm_back(key_normed, key_inverse, key_low_grad * key_gain)
    raw_grad = jnp.concatenate(
        [
            query_raw_grad.astype(LOW).reshape(2 * SEQ, HALF),
            key_raw_grad.astype(LOW).reshape(2 * SEQ, HALF),
            value_grad,
            gate_raw_grad,
        ],
        axis=1,
    )
    gated_full = lax.all_gather(gated_out, "c", axis=1, tiled=True)
    mixed_half = lax.dynamic_slice_in_dim(mixed_low, core * HALF, HALF, axis=1)
    attn_terms = jnp.concatenate(
        [
            dot_left_t(hidden_one, raw_grad).astype(LOW),
            dot_left_t(gated_full, mixed_half).astype(LOW),
        ],
        axis=1,
    )
    attn_sum = lax.psum_scatter(
        attn_terms.reshape(CHIPS, 24, 5 * HALF), XYZ, scatter_dimension=0, tiled=False
    )
    attn_back = lax.all_to_all(attn_sum.reshape(2, 12, 5 * HALF), "c", 0, 0, tiled=True)
    attn_grad = attn_back.reshape(2, 12, 5, HALF).transpose(2, 1, 0, 3).reshape(5, 12, D)
    attn_grad = attn_grad.astype(WIDE)

    hidden_one_grad = reduce_core(
        (dot_right_t(raw_grad, proj_full) + dot_right_t(forget_low_grad, forget_low)).reshape(
            2, SEQ, D
        ),
        core,
    )
    gain_one_grad = jnp.sum(normed_one * hidden_one_grad, axis=0)
    input_grad = mixed_grad + norm_back(normed_one, inverse_one, hidden_one_grad * gain_one)

    forget_bias_grad = lax.dynamic_update_slice_in_dim(
        jnp.zeros((H,), WIDE), jnp.sum(forget_arg_grad, axis=0), core * HEADS, axis=0
    )
    forget_w_grad = lax.dynamic_update_slice_in_dim(
        jnp.zeros((D, H), WIDE), dot_left_t(hidden_one, forget_low_grad), core * HEADS, axis=1
    )
    small_local = jnp.concatenate(
        [
            gain_one_grad,
            gain_two_grad,
            query_gain_grad,
            key_gain_grad,
            forget_bias_grad,
            forget_w_grad.reshape(-1),
        ]
    )
    members = [
        (attn_weights, attn_grad, attn_rows, attn_cols, D),
        (ffn_weights, ffn_grad, ffn_rows, ffn_cols, D),
        (down_weight[None], down_grad[None], down_rows[None], down_cols[None], FF),
    ]
    stats = [local_stats(member[0], member[1], member[2]) for member in members]
    sums_all = sum_everywhere(
        [stat for member_stats in stats for stat in member_stats[1:]] + [small_local]
    )
    small_total = sums_all[12]
    results = []
    for member_id in range(3):
        weight, grad_value, _, cols_old, all_rows = members[member_id]
        column_sum, row_sum, weight_sum, scaled = sums_all[4 * member_id : 4 * member_id + 4]
        rows_new = stats[member_id][0]
        cols_new, row_mean, update = factor_update(
            grad_value, rows_new, cols_old, column_sum, row_sum, all_rows
        )
        entries = all_rows * weight.shape[2]
        mean_square = row_mean * jnp.sum(scaled / cols_new, axis=1) / entries
        fresh = apply_step(weight, update, mean_square, weight_sum, entries)
        results.append((fresh, rows_new, cols_new))
    small_new, small_moments_new = small_update(small_params, small_total, small_moments)
    attn_new = results[0][0]
    ffn_new = results[1][0]
    down_new = results[2][0][0]
    return (
        block_out,
        input_grad,
        attn_grad,
        attn_new,
        attn_new.astype(LOW),
        results[0][1],
        results[0][2],
        ffn_grad,
        ffn_new,
        ffn_new.astype(LOW),
        results[1][1],
        results[1][2],
        down_grad,
        down_new,
        down_new.astype(LOW),
        results[2][1][0],
        results[2][2][0],
        small_total,
        small_new,
        small_moments_new,
    )


def solution(mesh):
    chips = Mesh(mesh.devices.reshape(4, 4, 4, 2), ALL)
    rows_first = P(ALL, None)
    rows_second = P(None, ALL, None)
    stat_rows = P(None, ALL)
    flat = P(ALL)
    whole = P()
    return jax.shard_map(
        shards,
        mesh=chips,
        in_specs=(
            rows_first,
            rows_first,
            flat,
            rows_second,
            stat_rows,
            whole,
            rows_second,
            stat_rows,
            whole,
            rows_first,
            flat,
            whole,
            whole,
            whole,
        ),
        out_specs=(
            rows_first,
            rows_first,
            rows_second,
            rows_second,
            rows_second,
            stat_rows,
            whole,
            rows_second,
            rows_second,
            rows_second,
            stat_rows,
            whole,
            rows_first,
            rows_first,
            rows_first,
            flat,
            whole,
            whole,
            whole,
            whole,
        ),
        check_vma=False,
    )
```

```python
import jax
import jax.numpy as jnp
from jax import lax
from jax.sharding import Mesh
from jax.sharding import PartitionSpec as P

D = 1536
H = 24
HD = 64
FF = 4096
SEQ = 128
HALF = D // 2
HEADS = H // 2
GROUP = 8
PLANE = 16
CHIPS = 64
DEVICES = 128
FF_PART = FF // GROUP

BETA = 0.5
CLIP = 0.1
RATE = 3.0
EPS_NORM = 1e-06
EPS_STAT = 1e-30
NEG_FILL = -1e30
LOW = jnp.bfloat16
WIDE = jnp.float32

ALL = ("x", "y", "z", "c")
XYZ = ("x", "y", "z")
XY = ("x", "y")
ZC = ("z", "c")


def dot_plain(left_side, right_side):
    return jnp.dot(left_side, right_side, preferred_element_type=WIDE)


def dot_right_t(left_side, right_side):
    return lax.dot_general(
        left_side, right_side, (((1,), (1,)), ((), ())), preferred_element_type=WIDE
    )


def dot_left_t(left_side, right_side):
    return lax.dot_general(
        left_side, right_side, (((0,), (0,)), ((), ())), preferred_element_type=WIDE
    )


def inverse_rms(values):
    return lax.rsqrt(jnp.mean(values * values, axis=-1, keepdims=True) + EPS_NORM)


def norm_back(normed, inverse, grad_out):
    return inverse * (grad_out - normed * jnp.mean(grad_out * normed, axis=-1, keepdims=True))


def split_small(vector):
    widths = [D, D, HD, HD, H]
    pieces = []
    offset = 0
    for piece_width in widths:
        pieces.append(vector[offset : offset + piece_width])
        offset = offset + piece_width
    pieces.append(vector[offset:].reshape(D, H))
    return pieces


def plain_update(param_part, grad_part, moment_part):
    moment_new = BETA * moment_part + (1.0 - BETA) * (grad_part * grad_part + EPS_STAT)
    update = grad_part * lax.rsqrt(moment_new)
    clip_ratio = jnp.sqrt(jnp.mean(update * update)) / CLIP
    update = update / jnp.maximum(1.0, clip_ratio)
    spread = jnp.sqrt(jnp.mean(param_part * param_part) + EPS_NORM)
    return (param_part - RATE * spread * update, moment_new)


def small_update(params_all, grads_all, moments_all):
    widths = [D, D, HD, HD, H, D * H]
    new_parts = []
    moment_parts = []
    offset = 0
    for piece_width in widths:
        fresh, moment_new = plain_update(
            params_all[offset : offset + piece_width],
            grads_all[offset : offset + piece_width],
            moments_all[offset : offset + piece_width],
        )
        new_parts.append(fresh)
        moment_parts.append(moment_new)
        offset = offset + piece_width
    return (jnp.concatenate(new_parts), jnp.concatenate(moment_parts))


def local_stats(weight, grad_value, rows_old):
    squares = grad_value * grad_value
    rows_new = BETA * rows_old + (1.0 - BETA) * (jnp.mean(squares, axis=2) + EPS_STAT)
    return (
        rows_new,
        jnp.sum(squares, axis=1),
        jnp.sum(rows_new, axis=1),
        jnp.sum(weight * weight, axis=(1, 2)),
        jnp.sum(squares / rows_new[:, :, None], axis=1),
    )


def factor_update(grad_value, rows_new, cols_old, column_sum, row_sum, all_rows):
    cols_new = BETA * cols_old + (1.0 - BETA) * (column_sum / all_rows + EPS_STAT)
    row_mean = row_sum / all_rows
    second = rows_new[:, :, None] * cols_new[:, None, :] / row_mean[:, None, None]
    return (cols_new, row_mean, grad_value * lax.rsqrt(second))


def apply_step(weight, update, mean_square, weight_sum, entries):
    clip_ratio = jnp.sqrt(mean_square) / CLIP
    clipped = update / jnp.maximum(1.0, clip_ratio)[:, None, None]
    spread = jnp.sqrt(weight_sum / entries + EPS_NORM)
    return weight - RATE * spread[:, None, None] * clipped


def swap_core(value):
    return lax.ppermute(value, "c", [(0, 1), (1, 0)])


def reduce_core(part, core):
    keep = lax.dynamic_index_in_dim(part, core, 0, keepdims=False)
    send = lax.dynamic_index_in_dim(part, 1 - core, 0, keepdims=False)
    return keep + swap_core(send)


def hop(value, axis, step):
    return lax.ppermute(value, axis, [(i, (i + step) % 4) for i in range(4)])


def core_hop(value, axis):
    pairs = []
    for i in range(4):
        pairs.append((2 * i, 2 * ((i + 1) % 4)))
        pairs.append((2 * i + 1, 2 * ((i + 3) % 4) + 1))
    return lax.ppermute(value, (axis, "c"), pairs)


def gather_group(value):
    rows = value.shape[0] // 2
    before = hop(value, "z", 1)
    after = hop(value, "z", -1)
    far = jnp.concatenate([hop(before[:rows], "z", 1), hop(after[rows:], "z", -1)])
    mine = jnp.concatenate([value, after, far, before])
    return jnp.concatenate([mine, swap_core(mine)])


def scatter_group(part):
    part = part.astype(LOW).reshape(2, 4, SEQ, D)
    part = part[0].astype(WIDE) + swap_core(part[1]).astype(WIDE)
    far = part[2].astype(LOW)
    rows = SEQ // 2
    from_before = hop(far[:rows], "z", 1).astype(WIDE)
    from_after = hop(far[rows:], "z", -1).astype(WIDE)
    to_after = jnp.concatenate([part[1][:rows] + from_before, part[1][rows:]]).astype(LOW)
    to_before = jnp.concatenate([part[3][:rows], part[3][rows:] + from_after]).astype(LOW)
    return part[0] + hop(to_after, "z", 1).astype(WIDE) + hop(to_before, "z", -1).astype(WIDE)


def ring_scatter(blocks, axes):
    way = 1 - 2 * lax.axis_index("c")
    for axis in axes:
        dim = XYZ.index(axis)
        here = lax.axis_index(axis)
        arrived = None
        for step in (1, 2, 3, 4):
            block = lax.dynamic_slice_in_dim(blocks, (here - way * step) % 4, 1, axis=dim)
            if arrived is not None:
                block = (block.astype(WIDE) + arrived.astype(WIDE)).astype(LOW)
            if step < 4:
                arrived = core_hop(block, axis)
        blocks = block
    return blocks


def sum_everywhere(vectors):
    sizes = [vector.size for vector in vectors]
    flat = jnp.concatenate([vector.reshape(-1) for vector in vectors])
    width = -(-flat.size // (DEVICES * 128)) * 128
    flat = jnp.pad(flat, (0, DEVICES * width - flat.size)).reshape(DEVICES, width // 128, 128)
    mine = jnp.sum(lax.all_to_all(flat, ALL, 0, 0, tiled=True), axis=0)
    spread = jnp.broadcast_to(mine[None], flat.shape)
    whole = lax.all_to_all(spread, ALL, 0, 0, tiled=True).reshape(-1)
    parts = []
    offset = 0
    for vector, size in zip(vectors, sizes):
        parts.append(whole[offset : offset + size].reshape(vector.shape))
        offset = offset + size
    return parts


def shards(
    tokens,
    cotangent,
    lengths,
    attn_weights,
    attn_rows,
    attn_cols,
    ffn_weights,
    ffn_rows,
    ffn_cols,
    down_weight,
    down_rows,
    down_cols,
    small_params,
    small_moments,
):
    core = lax.axis_index("c")
    inputs = tokens.astype(WIDE)
    slot_ids = jnp.arange(SEQ, dtype=jnp.int32)
    valid_rows = slot_ids < lengths[0]
    lengths_pair = lax.all_gather(lengths.astype(WIDE), "c", axis=0, tiled=True)
    valid_keys = slot_ids[None, :].astype(WIDE) < lengths_pair[:, None]
    gain_one, gain_two, query_gain, key_gain, forget_bias, forget_weight = split_small(small_params)
    forget_low = lax.dynamic_slice_in_dim(forget_weight, core * HEADS, HEADS, axis=1).astype(LOW)
    bias_mine = lax.dynamic_slice_in_dim(forget_bias, core * HEADS, HEADS, axis=0)

    attn_low = jnp.moveaxis(attn_weights.astype(LOW).reshape(5, 12, 2, HALF), 2, 0)
    attn_low = jnp.moveaxis(attn_low, 1, 2).reshape(2, 12, 5 * HALF)
    attn_pair = lax.all_to_all(attn_low, "c", 0, 0, tiled=True).reshape(24, 5 * HALF)
    attn_full = lax.all_gather(attn_pair, XYZ, axis=0, tiled=True)
    proj_full = attn_full[:, : 4 * HALF]
    out_rows = lax.all_to_all(attn_full[:, 4 * HALF :], "c", 0, 1, tiled=True)

    pair_low = ffn_weights.astype(LOW).reshape(2, 12, PLANE, GROUP, 32)
    pair_low = pair_low.transpose(3, 0, 1, 2, 4).reshape(GROUP, 2, 12, FF_PART)
    pair_low = lax.all_to_all(pair_low, ZC, 0, 0, tiled=True)
    pair_low = jnp.moveaxis(pair_low, 0, 1).reshape(2 * 96, FF_PART)
    down_low = jnp.moveaxis(down_weight.astype(LOW).reshape(32, 3, 512), 1, 0).reshape(96, 512)
    ffn_full = lax.all_gather(jnp.concatenate([pair_low, down_low]), XY, axis=0, tiled=False)
    gate_full = ffn_full[:, :96].reshape(D, FF_PART)
    up_full = ffn_full[:, 96:192].reshape(D, FF_PART)
    down_full = jnp.moveaxis(ffn_full[:, 192:].reshape(PLANE, 3, 32, 512), 1, 2).reshape(FF_PART, D)

    inverse_one = inverse_rms(inputs)
    normed_one = inputs * inverse_one
    hidden_own = (normed_one * gain_one).astype(LOW)
    hidden_one = lax.all_gather(hidden_own, "c", axis=0, tiled=True)
    seed_grad = cotangent.astype(WIDE) * valid_rows[:, None].astype(WIDE)
    seed_low = gather_group(seed_grad.astype(LOW))

    raw = dot_plain(hidden_one, proj_full)
    query_raw = raw[:, :HALF].reshape(2, SEQ, HEADS, HD)
    key_raw = raw[:, HALF : 2 * HALF].reshape(2, SEQ, HEADS, HD)
    value_low = raw[:, 2 * HALF : 3 * HALF].astype(LOW).reshape(2, SEQ, HEADS, HD)
    gate_raw = raw[:, 3 * HALF :]
    forget_arg = dot_plain(hidden_one, forget_low) + bias_mine
    log_forget = -jnp.log1p(jnp.exp(-forget_arg))
    query_inverse = inverse_rms(query_raw)
    key_inverse = inverse_rms(key_raw)
    query_normed = query_raw * query_inverse
    key_normed = key_raw * key_inverse
    query_low = (query_normed * query_gain).astype(LOW)
    key_low = (key_normed * key_gain).astype(LOW)
    score_scale = HD ** (-0.5)
    cumulative = jnp.cumsum(log_forget.reshape(2, SEQ, HEADS), axis=1).transpose(0, 2, 1)
    allowed = (slot_ids[None, :] <= slot_ids[:, None])[None] & valid_keys[:, None, :]
    scores = (
        jnp.einsum("bthd,bshd->bhts", query_low, key_low, preferred_element_type=WIDE) * score_scale
    )
    scores = scores + cumulative[:, :, :, None] - cumulative[:, :, None, :]
    scores = jnp.where(allowed[:, None], scores, NEG_FILL)
    weights = jnp.exp(scores - jnp.max(scores, axis=-1, keepdims=True))
    probabilities = weights / jnp.sum(weights, axis=-1, keepdims=True)
    prob_low = probabilities.astype(LOW)
    attended = jnp.einsum(
        "bhts,bshd->bthd", prob_low, value_low, preferred_element_type=WIDE
    ).reshape(2 * SEQ, HALF)
    gate_value = lax.logistic(gate_raw)
    gated_out = (attended * gate_value).astype(LOW)
    mixed_sum = inputs + reduce_core(dot_plain(gated_out, out_rows).reshape(2, SEQ, D), core)
    inverse_two = inverse_rms(mixed_sum)
    normed_two = mixed_sum * inverse_two
    hidden_two = gather_group((normed_two * gain_two).astype(LOW))

    gate_part = dot_plain(hidden_two, gate_full)
    up_part = dot_plain(hidden_two, up_full)
    gate_sig = lax.logistic(gate_part)
    activated = (gate_part * gate_sig * up_part).astype(LOW)
    activated_grad = dot_right_t(seed_low, down_full)
    silu_grad = activated_grad * up_part
    gate_part_grad = (
        silu_grad * gate_sig + silu_grad * gate_part * gate_sig * (1.0 - gate_sig)
    ).astype(LOW)
    up_part_grad = (activated_grad * (gate_part * gate_sig)).astype(LOW)
    hidden_two_grad = scatter_group(
        dot_right_t(gate_part_grad, gate_full) + dot_right_t(up_part_grad, up_full)
    )
    block_out = (mixed_sum + scatter_group(dot_plain(activated, down_full))).astype(LOW)
    gate_terms = dot_left_t(hidden_two, gate_part_grad).astype(LOW).reshape(PLANE, 96, 512)
    up_terms = dot_left_t(hidden_two, up_part_grad).astype(LOW).reshape(PLANE, 96, 512)
    down_terms = dot_left_t(activated, seed_low).astype(LOW).reshape(PLANE, 32, 3, 512)
    down_terms = jnp.moveaxis(down_terms, 2, 1).reshape(PLANE, 96, 512)
    first_terms = jnp.concatenate([gate_terms, up_terms[:, :48]], axis=1)
    second_terms = jnp.concatenate([up_terms[:, 48:], down_terms], axis=1)
    ffn_sum = jnp.concatenate(
        [
            ring_scatter(first_terms.reshape(4, 4, 144, 512), ("x", "y")).reshape(144, 512),
            ring_scatter(second_terms.reshape(4, 4, 144, 512), ("y", "x")).reshape(144, 512),
        ]
    )
    down_grad = jnp.moveaxis(ffn_sum[192:].reshape(3, 32, 512), 0, 1).reshape(32, D).astype(WIDE)
    pair_back = jnp.moveaxis(ffn_sum[:192].reshape(2, GROUP, 12, FF_PART), 1, 0)
    pair_back = lax.all_to_all(pair_back, ZC, 0, 0, tiled=True).reshape(GROUP, 2, 12, PLANE, 32)
    ffn_grad = pair_back.transpose(1, 2, 3, 0, 4).reshape(2, 12, FF).astype(WIDE)

    gain_two_grad = jnp.sum(normed_two * hidden_two_grad, axis=0)
    mixed_grad = seed_grad + norm_back(normed_two, inverse_two, hidden_two_grad * gain_two)
    mixed_low = lax.all_gather(mixed_grad.astype(LOW), "c", axis=0, tiled=True)
    gated_grad = dot_right_t(mixed_low, out_rows)
    attended_grad = (gated_grad * gate_value).astype(LOW).reshape(2, SEQ, HEADS, HD)
    gate_raw_grad = (gated_grad * attended * gate_value * (1.0 - gate_value)).astype(LOW)
    prob_grad = jnp.einsum(
        "bthd,bshd->bhts", attended_grad, value_low, preferred_element_type=WIDE
    )
    row_delta = jnp.sum(probabilities * prob_grad, axis=-1, keepdims=True)
    score_grad = (probabilities * (prob_grad - row_delta)).astype(LOW)
    value_grad = (
        jnp.einsum("bhts,bthd->bshd", prob_low, attended_grad, preferred_element_type=WIDE)
        .astype(LOW)
        .reshape(2 * SEQ, HALF)
    )
    query_low_grad = (
        jnp.einsum("bhts,bshd->bthd", score_grad, key_low, preferred_element_type=WIDE)
        * score_scale
    )
    key_low_grad = (
        jnp.einsum("bhts,bthd->bshd", score_grad, query_low, preferred_element_type=WIDE)
        * score_scale
    )
    score_rows = jnp.sum(score_grad, axis=3, dtype=WIDE)
    score_cols = jnp.sum(score_grad, axis=2, dtype=WIDE)
    log_forget_grad = lax.cumsum(score_rows - score_cols, axis=2, reverse=True)
    log_forget_grad = log_forget_grad.transpose(0, 2, 1).reshape(2 * SEQ, HEADS)
    forget_arg_grad = log_forget_grad * (1.0 - lax.logistic(forget_arg))
    forget_low_grad = forget_arg_grad.astype(LOW)
    query_gain_grad = jnp.sum(query_normed * query_low_grad, axis=(0, 1, 2))
    key_gain_grad = jnp.sum(key_normed * key_low_grad, axis=(0, 1, 2))
    query_raw_grad = norm_back(query_normed, query_inverse, query_low_grad * query_gain)
    key_raw_grad = norm_back(key_normed, key_inverse, key_low_grad * key_gain)
    raw_grad = jnp.concatenate(
        [
            query_raw_grad.astype(LOW).reshape(2 * SEQ, HALF),
            key_raw_grad.astype(LOW).reshape(2 * SEQ, HALF),
            value_grad,
            gate_raw_grad,
        ],
        axis=1,
    )
    gated_full = lax.all_gather(gated_out, "c", axis=1, tiled=True)
    mixed_half = lax.dynamic_slice_in_dim(mixed_low, core * HALF, HALF, axis=1)
    out_terms = dot_left_t(gated_full, mixed_half).astype(LOW)
    gate_raw_terms = dot_left_t(hidden_one, gate_raw_grad).astype(LOW)
    value_terms = dot_left_t(hidden_one, value_grad).astype(LOW)
    pair_terms = dot_left_t(hidden_one, raw_grad[:, : 2 * HALF]).astype(LOW)
    chips = (4, 4, 4, 24)
    out_sum = ring_scatter(out_terms.reshape(*chips, HALF), ("x", "y", "z"))
    gate_sum = ring_scatter(gate_raw_terms.reshape(*chips, HALF), ("y", "z", "x"))
    value_sum = ring_scatter(value_terms.reshape(*chips, HALF), ("z", "x", "y"))
    pair_sums = [
        ring_scatter(pair_terms[:, 512 * k : 512 * (k + 1)].reshape(*chips, 512), order)
        for k, order in enumerate((("x", "y", "z"), ("y", "z", "x"), ("z", "x", "y")))
    ]
    attn_sum = jnp.concatenate([*pair_sums, value_sum, gate_sum, out_sum], axis=4)
    attn_back = lax.all_to_all(attn_sum.reshape(2, 12, 5 * HALF), "c", 0, 0, tiled=True)
    attn_grad = attn_back.reshape(2, 12, 5, HALF).transpose(2, 1, 0, 3).reshape(5, 12, D)
    attn_grad = attn_grad.astype(WIDE)

    hidden_one_grad = reduce_core(
        (dot_right_t(raw_grad, proj_full) + dot_right_t(forget_low_grad, forget_low)).reshape(
            2, SEQ, D
        ),
        core,
    )
    gain_one_grad = jnp.sum(normed_one * hidden_one_grad, axis=0)
    input_grad = mixed_grad + norm_back(normed_one, inverse_one, hidden_one_grad * gain_one)

    forget_bias_grad = lax.dynamic_update_slice_in_dim(
        jnp.zeros((H,), WIDE), jnp.sum(forget_arg_grad, axis=0), core * HEADS, axis=0
    )
    forget_w_grad = lax.dynamic_update_slice_in_dim(
        jnp.zeros((D, H), WIDE), dot_left_t(hidden_one, forget_low_grad), core * HEADS, axis=1
    )
    small_local = jnp.concatenate(
        [
            gain_one_grad,
            gain_two_grad,
            query_gain_grad,
            key_gain_grad,
            forget_bias_grad,
            forget_w_grad.reshape(-1),
        ]
    )
    members = [
        (attn_weights, attn_grad, attn_rows, attn_cols, D),
        (ffn_weights, ffn_grad, ffn_rows, ffn_cols, D),
        (down_weight[None], down_grad[None], down_rows[None], down_cols[None], FF),
    ]
    stats = [local_stats(member[0], member[1], member[2]) for member in members]
    sums_all = sum_everywhere(
        [stat for member_stats in stats for stat in member_stats[1:]] + [small_local]
    )
    small_total = sums_all[12]
    results = []
    for member_id in range(3):
        weight, grad_value, _, cols_old, all_rows = members[member_id]
        column_sum, row_sum, weight_sum, scaled = sums_all[4 * member_id : 4 * member_id + 4]
        rows_new = stats[member_id][0]
        cols_new, row_mean, update = factor_update(
            grad_value, rows_new, cols_old, column_sum, row_sum, all_rows
        )
        entries = all_rows * weight.shape[2]
        mean_square = row_mean * jnp.sum(scaled / cols_new, axis=1) / entries
        fresh = apply_step(weight, update, mean_square, weight_sum, entries)
        results.append((fresh, rows_new, cols_new))
    small_new, small_moments_new = small_update(small_params, small_total, small_moments)
    attn_new = results[0][0]
    ffn_new = results[1][0]
    down_new = results[2][0][0]
    return (
        block_out,
        input_grad,
        attn_grad,
        attn_new,
        attn_new.astype(LOW),
        results[0][1],
        results[0][2],
        ffn_grad,
        ffn_new,
        ffn_new.astype(LOW),
        results[1][1],
        results[1][2],
        down_grad,
        down_new,
        down_new.astype(LOW),
        results[2][1][0],
        results[2][2][0],
        small_total,
        small_new,
        small_moments_new,
    )


def solution(mesh):
    chips = Mesh(mesh.devices.reshape(4, 4, 4, 2), ALL)
    rows_first = P(ALL, None)
    rows_second = P(None, ALL, None)
    stat_rows = P(None, ALL)
    flat = P(ALL)
    whole = P()
    return jax.shard_map(
        shards,
        mesh=chips,
        in_specs=(
            rows_first,
            rows_first,
            flat,
            rows_second,
            stat_rows,
            whole,
            rows_second,
            stat_rows,
            whole,
            rows_first,
            flat,
            whole,
            whole,
            whole,
        ),
        out_specs=(
            rows_first,
            rows_first,
            rows_second,
            rows_second,
            rows_second,
            stat_rows,
            whole,
            rows_second,
            rows_second,
            rows_second,
            stat_rows,
            whole,
            rows_first,
            rows_first,
            rows_first,
            flat,
            whole,
            whole,
            whole,
            whole,
        ),
        check_vma=False,
    )
```

```python
import jax
import jax.numpy as jnp
from jax import lax
from jax.experimental import pallas as pl
from jax.experimental.pallas import tpu as pltpu
from jax.sharding import Mesh
from jax.sharding import PartitionSpec as P

D = 1536
H = 24
HD = 64
FF = 4096
SEQ = 128
HALF = D // 2
HEADS = H // 2
GROUP = 8
PLANE = 16
CHIPS = 64
DEVICES = 128
FF_PART = FF // GROUP

BETA = 0.5
CLIP = 0.1
RATE = 3.0
EPS_NORM = 1e-06
EPS_STAT = 1e-30
NEG_FILL = -1e30
LOW = jnp.bfloat16
WIDE = jnp.float32

ALL = ("x", "y", "z", "c")
XYZ = ("x", "y", "z")
XY = ("x", "y")
ZC = ("z", "c")


def dot_plain(left_side, right_side):
    return jnp.dot(left_side, right_side, preferred_element_type=WIDE)


def dot_right_t(left_side, right_side):
    return lax.dot_general(
        left_side, right_side, (((1,), (1,)), ((), ())), preferred_element_type=WIDE
    )


def dot_left_t(left_side, right_side):
    return lax.dot_general(
        left_side, right_side, (((0,), (0,)), ((), ())), preferred_element_type=WIDE
    )


def inverse_rms(values):
    return lax.rsqrt(jnp.mean(values * values, axis=-1, keepdims=True) + EPS_NORM)


def norm_back(normed, inverse, grad_out):
    return inverse * (grad_out - normed * jnp.mean(grad_out * normed, axis=-1, keepdims=True))


def split_small(vector):
    widths = [D, D, HD, HD, H]
    pieces = []
    offset = 0
    for piece_width in widths:
        pieces.append(vector[offset : offset + piece_width])
        offset = offset + piece_width
    pieces.append(vector[offset:].reshape(D, H))
    return pieces


def plain_update(param_part, grad_part, moment_part):
    moment_new = BETA * moment_part + (1.0 - BETA) * (grad_part * grad_part + EPS_STAT)
    update = grad_part * lax.rsqrt(moment_new)
    clip_ratio = jnp.sqrt(jnp.mean(update * update)) / CLIP
    update = update / jnp.maximum(1.0, clip_ratio)
    spread = jnp.sqrt(jnp.mean(param_part * param_part) + EPS_NORM)
    return (param_part - RATE * spread * update, moment_new)


def small_update(params_all, grads_all, moments_all):
    widths = [D, D, HD, HD, H, D * H]
    new_parts = []
    moment_parts = []
    offset = 0
    for piece_width in widths:
        fresh, moment_new = plain_update(
            params_all[offset : offset + piece_width],
            grads_all[offset : offset + piece_width],
            moments_all[offset : offset + piece_width],
        )
        new_parts.append(fresh)
        moment_parts.append(moment_new)
        offset = offset + piece_width
    return (jnp.concatenate(new_parts), jnp.concatenate(moment_parts))


def local_stats(weight, grad_value, rows_old):
    squares = grad_value * grad_value
    rows_new = BETA * rows_old + (1.0 - BETA) * (jnp.mean(squares, axis=2) + EPS_STAT)
    return (
        rows_new,
        jnp.sum(squares, axis=1),
        jnp.sum(rows_new, axis=1),
        jnp.sum(weight * weight, axis=(1, 2)),
        jnp.sum(squares / rows_new[:, :, None], axis=1),
    )


def factor_update(grad_value, rows_new, cols_old, column_sum, row_sum, all_rows):
    cols_new = BETA * cols_old + (1.0 - BETA) * (column_sum / all_rows + EPS_STAT)
    row_mean = row_sum / all_rows
    second = rows_new[:, :, None] * cols_new[:, None, :] / row_mean[:, None, None]
    return (cols_new, row_mean, grad_value * lax.rsqrt(second))


def apply_step(weight, update, mean_square, weight_sum, entries):
    clip_ratio = jnp.sqrt(mean_square) / CLIP
    clipped = update / jnp.maximum(1.0, clip_ratio)[:, None, None]
    spread = jnp.sqrt(weight_sum / entries + EPS_NORM)
    return weight - RATE * spread[:, None, None] * clipped


def fence(*values):
    return lax.optimization_barrier(values)


def swap_core(value):
    return lax.ppermute(value, "c", [(0, 1), (1, 0)])


def reduce_core(part, core):
    keep = lax.dynamic_index_in_dim(part, core, 0, keepdims=False)
    send = lax.dynamic_index_in_dim(part, 1 - core, 0, keepdims=False)
    return keep + swap_core(send)


def hop(value, axis, step):
    return lax.ppermute(value, axis, [(i, (i + step) % 4) for i in range(4)])


def gather_group(value):
    rows = value.shape[0] // 2
    before = hop(value, "z", 1)
    after = hop(value, "z", -1)
    other = swap_core(value)
    before, after, other = fence(before, after, other)
    near = jnp.concatenate([before, after])
    far_one = hop(before[:rows], "z", 1)
    far_two = hop(after[rows:], "z", -1)
    near_other = swap_core(near)
    far_one, far_two, near_other = fence(far_one, far_two, near_other)
    far = jnp.concatenate([far_one, far_two])
    return jnp.concatenate([value, near, far, other, near_other, swap_core(far)])


def far_halves(part):
    rows = SEQ // 2
    far = part[3].astype(LOW)
    return (hop(far[:rows], "z", 1), hop(far[rows:], "z", -1))


def near_blocks(part, halves):
    rows = SEQ // 2
    to_after = jnp.concatenate([part[2][:rows] + halves[0].astype(WIDE), part[2][rows:]])
    to_before = jnp.concatenate([part[1][:rows], part[1][rows:] + halves[1].astype(WIDE)])
    return (hop(to_after.astype(LOW), "z", 1), hop(to_before.astype(LOW), "z", -1))


def direct_sum(blocks, axis, dim):
    here = lax.axis_index(axis)
    total = lax.dynamic_index_in_dim(blocks, here, dim, keepdims=False).astype(WIDE)
    for step in (1, 2, 3):
        block = lax.dynamic_index_in_dim(blocks, (here + step) % 4, dim, keepdims=False)
        total = total + hop(block, axis, step).astype(WIDE)
    return total


def direct_exchange(blocks, axis):
    here = lax.axis_index(axis)
    pieces = [lax.dynamic_index_in_dim(blocks, here, 0, keepdims=False)]
    for step in (1, 2, 3):
        block = lax.dynamic_index_in_dim(blocks, (here + step) % 4, 0, keepdims=False)
        pieces.append(hop(block, axis, step))
    return pieces


def head_stat(values, lane_low):
    low = jnp.sum(jnp.where(lane_low, values, 0.0), axis=-1, keepdims=True) * (1.0 / HD)
    high = jnp.sum(jnp.where(lane_low, 0.0, values), axis=-1, keepdims=True) * (1.0 / HD)
    return jnp.where(lane_low, low, high)


def head_normed(values, lane_low):
    inverse = lax.rsqrt(head_stat(values * values, lane_low) + EPS_NORM)
    return (values * inverse, inverse)


def attend_kernel(
    raw_ref, cols_ref, rows_ref, length_ref, gains_ref, gated_ref, attended_ref, prob_ref
):
    lane = lax.broadcasted_iota(jnp.int32, (SEQ, SEQ), 1)
    lane_low = lane < HD
    slot = lax.broadcasted_iota(jnp.int32, (SEQ, SEQ), 0)
    allowed = (lane <= slot) & (lane.astype(WIDE) < length_ref[0])
    for pair in range(HEADS // 2):
        at = pair * SEQ
        query, _ = head_normed(raw_ref[:, at : at + SEQ], lane_low)
        key, _ = head_normed(raw_ref[:, HALF + at : HALF + at + SEQ], lane_low)
        query = (query * gains_ref[0:1]).astype(LOW)
        key = (key * gains_ref[1:2]).astype(LOW)
        value = raw_ref[:, 2 * HALF + at : 2 * HALF + at + SEQ].astype(LOW)
        outs = []
        for side in range(2):
            head = 2 * pair + side
            mine = lane_low if side == 0 else jnp.logical_not(lane_low)
            score = dot_right_t(jnp.where(mine, query, jnp.zeros_like(query)), key)
            score = score * (HD**-0.5) + cols_ref[:, head : head + 1] - rows_ref[0, head : head + 1]
            score = jnp.where(allowed, score, NEG_FILL)
            weight = jnp.exp(score - jnp.max(score, axis=-1, keepdims=True))
            prob = weight / jnp.sum(weight, axis=-1, keepdims=True)
            prob_ref[0, head] = prob
            outs.append(dot_plain(prob.astype(LOW), value))
        attended = jnp.where(lane_low, outs[0], outs[1])
        attended_ref[:, at : at + SEQ] = attended
        gate = lax.logistic(raw_ref[:, 3 * HALF + at : 3 * HALF + at + SEQ])
        gated_ref[:, at : at + SEQ] = (attended * gate).astype(LOW)


def attend(raw, cols, rows, lengths, gains):
    return pl.pallas_call(
        attend_kernel,
        grid=(2,),
        in_specs=[
            pl.BlockSpec((SEQ, 4 * HALF), lambda i: (i, 0)),
            pl.BlockSpec((SEQ, SEQ), lambda i: (i, 0)),
            pl.BlockSpec((1, 16, SEQ), lambda i: (i, 0, 0)),
            pl.BlockSpec((1, 1, SEQ), lambda i: (i, 0, 0)),
            pl.BlockSpec((8, SEQ), lambda i: (0, 0)),
        ],
        out_specs=[
            pl.BlockSpec((SEQ, HALF), lambda i: (i, 0)),
            pl.BlockSpec((SEQ, HALF), lambda i: (i, 0)),
            pl.BlockSpec((1, HEADS, SEQ, SEQ), lambda i: (i, 0, 0, 0)),
        ],
        out_shape=[
            jax.ShapeDtypeStruct((2 * SEQ, HALF), LOW),
            jax.ShapeDtypeStruct((2 * SEQ, HALF), WIDE),
            jax.ShapeDtypeStruct((2, HEADS, SEQ, SEQ), WIDE),
        ],
        compiler_params=pltpu.CompilerParams(vmem_limit_bytes=40 * 1024 * 1024),
        cost_estimate=pl.CostEstimate(
            flops=24 * 4 * SEQ**3, bytes_accessed=6_000_000, transcendentals=24 * SEQ * SEQ
        ),
        name="attend",
    )(raw, cols, rows, lengths, gains)


def attend_back_kernel(
    raw_ref, gated_grad_ref, attended_ref, prob_ref, gains_ref, grad_ref, forget_ref, gain_ref
):
    lane_low = lax.broadcasted_iota(jnp.int32, (SEQ, SEQ), 1) < HD
    ones = jnp.ones((8, SEQ), LOW)
    forget_ref[...] = jnp.zeros_like(forget_ref)

    @pl.when(pl.program_id(0) == 0)
    def _():
        gain_ref[...] = jnp.zeros_like(gain_ref)

    for pair in range(HEADS // 2):
        at = pair * SEQ
        query_normed, query_inverse = head_normed(raw_ref[:, at : at + SEQ], lane_low)
        key_normed, key_inverse = head_normed(raw_ref[:, HALF + at : HALF + at + SEQ], lane_low)
        query = (query_normed * gains_ref[0:1]).astype(LOW)
        key = (key_normed * gains_ref[1:2]).astype(LOW)
        value = raw_ref[:, 2 * HALF + at : 2 * HALF + at + SEQ].astype(LOW)
        gate = lax.logistic(raw_ref[:, 3 * HALF + at : 3 * HALF + at + SEQ])
        gated_grad = gated_grad_ref[:, at : at + SEQ]
        out_grad = (gated_grad * gate).astype(LOW)
        gate_grad = gated_grad * attended_ref[:, at : at + SEQ] * gate * (1.0 - gate)
        grad_ref[3, :, at : at + SEQ] = gate_grad.astype(LOW)
        query_parts = []
        key_parts = []
        value_parts = []
        for side in range(2):
            head = 2 * pair + side
            mine = lane_low if side == 0 else jnp.logical_not(lane_low)
            prob = prob_ref[0, head]
            prob_grad = dot_right_t(jnp.where(mine, out_grad, jnp.zeros_like(out_grad)), value)
            delta = jnp.sum(prob * prob_grad, axis=-1, keepdims=True)
            score_grad = (prob * (prob_grad - delta)).astype(LOW)
            value_parts.append(dot_left_t(prob.astype(LOW), out_grad))
            query_parts.append(dot_plain(score_grad, key))
            key_parts.append(dot_left_t(score_grad, query))
            sums = dot_right_t(ones, score_grad) - dot_plain(ones, score_grad)
            forget_ref[0, head : head + 1] = sums[0:1]
        value_grad = jnp.where(lane_low, value_parts[0], value_parts[1])
        grad_ref[2, :, at : at + SEQ] = value_grad.astype(LOW)
        query_grad = jnp.where(lane_low, query_parts[0], query_parts[1]) * (HD**-0.5)
        key_grad = jnp.where(lane_low, key_parts[0], key_parts[1]) * (HD**-0.5)
        for row, grad, normed, inverse in (
            (0, query_grad, query_normed, query_inverse),
            (1, key_grad, key_normed, key_inverse),
        ):
            product = grad * normed
            gain_ref[row : row + 1] += jnp.sum(product, axis=0, keepdims=True)
            mean = head_stat(product * gains_ref[row : row + 1], lane_low)
            back = inverse * (grad * gains_ref[row : row + 1] - normed * mean)
            grad_ref[row, :, at : at + SEQ] = back.astype(LOW)


def attend_back(raw, gated_grad, attended, prob, gains):
    return pl.pallas_call(
        attend_back_kernel,
        grid=(2,),
        in_specs=[
            pl.BlockSpec((SEQ, 4 * HALF), lambda i: (i, 0)),
            pl.BlockSpec((SEQ, HALF), lambda i: (i, 0)),
            pl.BlockSpec((SEQ, HALF), lambda i: (i, 0)),
            pl.BlockSpec((1, HEADS, SEQ, SEQ), lambda i: (i, 0, 0, 0)),
            pl.BlockSpec((8, SEQ), lambda i: (0, 0)),
        ],
        out_specs=[
            pl.BlockSpec((4, SEQ, HALF), lambda i: (0, i, 0)),
            pl.BlockSpec((1, 16, SEQ), lambda i: (i, 0, 0)),
            pl.BlockSpec((8, SEQ), lambda i: (0, 0)),
        ],
        out_shape=[
            jax.ShapeDtypeStruct((4, 2 * SEQ, HALF), LOW),
            jax.ShapeDtypeStruct((2, 16, SEQ), WIDE),
            jax.ShapeDtypeStruct((8, SEQ), WIDE),
        ],
        compiler_params=pltpu.CompilerParams(vmem_limit_bytes=40 * 1024 * 1024),
        cost_estimate=pl.CostEstimate(
            flops=24 * 10 * SEQ**3, bytes_accessed=8_000_000, transcendentals=2 * SEQ * HALF
        ),
        name="attend_back",
    )(raw, gated_grad, attended, prob, gains)


def padded(value, size):
    flat = value.reshape(-1)
    return jnp.pad(flat, (0, size - flat.size))


def spread_sum(flat):
    pieces = flat.reshape(DEVICES, -1, 128)
    return jnp.sum(lax.all_to_all(pieces, ALL, 0, 0, tiled=True), axis=0)


def spread_back(mine):
    whole = jnp.broadcast_to(mine[None], (DEVICES, *mine.shape))
    return lax.all_to_all(whole, ALL, 0, 0, tiled=True).reshape(-1)


def column_order():
    source = lax.broadcasted_iota(jnp.int32, (1024, 1024), 0)
    target = lax.broadcasted_iota(jnp.int32, (1024, 1024), 1)
    lane = source % 128
    return (target == (lane // 32) * 256 + (source // 128) * 32 + lane % 32).astype(LOW)


def shards(
    tokens,
    cotangent,
    lengths,
    attn_weights,
    attn_rows,
    attn_cols,
    ffn_weights,
    ffn_rows,
    ffn_cols,
    down_weight,
    down_rows,
    down_cols,
    small_params,
    small_moments,
):
    core = lax.axis_index("c")
    inputs = tokens.astype(WIDE)
    slot_ids = jnp.arange(SEQ, dtype=jnp.int32)
    valid_rows = slot_ids < lengths[0]
    lengths_pair = lax.all_gather(lengths.astype(WIDE), "c", axis=0, tiled=True)
    lengths_pair = jnp.broadcast_to(lengths_pair[:, None, None], (2, 1, SEQ))
    gain_one, gain_two, query_gain, key_gain, forget_bias, forget_weight = split_small(small_params)
    forget_low = lax.dynamic_slice_in_dim(forget_weight, core * HEADS, HEADS, axis=1).astype(LOW)
    bias_mine = lax.dynamic_slice_in_dim(forget_bias, core * HEADS, HEADS, axis=0)

    attn_low = jnp.moveaxis(attn_weights.astype(LOW).reshape(5, 12, 2, HALF), 2, 0)
    attn_low = jnp.moveaxis(attn_low, 1, 2).reshape(2, 12, 5 * HALF)
    attn_pair = lax.all_to_all(attn_low, "c", 0, 0, tiled=True).reshape(24, 5 * HALF)
    order = column_order()
    pair_low = ffn_weights.astype(LOW).reshape(24, 4, 1024).transpose(1, 0, 2).reshape(96, 1024)
    pair_low = dot_right_t(pair_low, order).astype(LOW).reshape(4, 2, 12, GROUP, 128)
    pair_low = pair_low.transpose(3, 1, 2, 0, 4).reshape(GROUP, 2, 12, FF_PART)
    pair_low = lax.all_to_all(pair_low, ZC, 0, 0, tiled=True)
    pair_low = jnp.moveaxis(pair_low, 0, 1).reshape(2 * 96, FF_PART)
    down_low = [down_weight[:, at : at + 512].astype(LOW) for at in (0, 512, 1024)]
    ffn_full = lax.all_gather(jnp.concatenate([pair_low, *down_low]), XY, axis=0, tiled=False)
    attn_full = lax.all_gather(attn_pair, XYZ, axis=0, tiled=True)
    inverse_one = inverse_rms(inputs)
    normed_one = inputs * inverse_one
    hidden_own = (normed_one * gain_one).astype(LOW)
    hidden_own, attn_pair = fence(hidden_own, attn_pair)
    hidden_one = lax.all_gather(hidden_own, "c", axis=0, tiled=True)
    hidden_before = hop(hidden_own, "z", 1)
    hidden_after = hop(hidden_own, "z", -1)
    hidden_far = [hop(hidden_before[:64], "z", 1), hop(hidden_after[64:], "z", -1)]
    hidden_deep = [hidden_before, jnp.concatenate(hidden_far), hidden_after]
    hidden_deep = [lax.all_gather(piece, "c", axis=0, tiled=True) for piece in hidden_deep]
    hidden_deep = jnp.concatenate([hidden_one, *hidden_deep])
    seed_grad = cotangent.astype(WIDE) * valid_rows[:, None].astype(WIDE)
    seed_low = gather_group(seed_grad.astype(LOW))

    forget_arg = dot_plain(hidden_one, forget_low) + bias_mine
    log_forget = -jnp.log1p(jnp.exp(-forget_arg))
    cumulative = jnp.cumsum(log_forget.reshape(2, SEQ, HEADS), axis=1)
    forget_cols = jnp.pad(cumulative.reshape(2 * SEQ, HEADS), ((0, 0), (0, SEQ - HEADS)))
    forget_rows = jnp.pad(cumulative.transpose(0, 2, 1), ((0, 0), (0, 16 - HEADS), (0, 0)))
    gains = jnp.stack([jnp.tile(query_gain, 2), jnp.tile(key_gain, 2)])
    gains = jnp.pad(gains, ((0, 6), (0, 0)))
    attn_full, seed_low, hidden_deep, forget_cols, forget_rows, gains, order = fence(
        attn_full, seed_low, hidden_deep, forget_cols, forget_rows, gains, order
    )
    proj_full = attn_full[:, : 4 * HALF]
    out_half = attn_full[:, 4 * HALF :].reshape(2, HALF, HALF)
    out_own = lax.dynamic_index_in_dim(out_half, core, 0, keepdims=False)
    out_got = swap_core(lax.dynamic_index_in_dim(out_half, 1 - core, 0, keepdims=False))
    out_rows = jnp.where(
        core == 0,
        jnp.concatenate([out_own, out_got], axis=1),
        jnp.concatenate([out_got, out_own], axis=1),
    )

    raw = dot_plain(hidden_one, proj_full)
    gated_out, attended, prob = attend(raw, forget_cols, forget_rows, lengths_pair, gains)
    mixed_sum = inputs + reduce_core(dot_plain(gated_out, out_rows).reshape(2, SEQ, D), core)
    inverse_two = inverse_rms(mixed_sum)
    normed_two = mixed_sum * inverse_two
    hidden_two = gather_group((normed_two * gain_two).astype(LOW))

    gated_full = lax.all_gather(gated_out, "c", axis=1, tiled=True)
    hidden_two, ffn_full, gated_full = fence(hidden_two, ffn_full, gated_full)
    gate_full = ffn_full[:, :96].reshape(D, FF_PART)
    up_full = ffn_full[:, 96:192].reshape(D, FF_PART)
    down_full = jnp.concatenate(
        [ffn_full[:, at : at + 32].reshape(FF_PART, 512) for at in (192, 224, 256)], axis=1
    )

    gate_part = dot_plain(hidden_two, gate_full)
    up_part = dot_plain(hidden_two, up_full)
    gate_sig = lax.logistic(gate_part)
    activated = (gate_part * gate_sig * up_part).astype(LOW)
    activated_grad = dot_right_t(seed_low, down_full)
    silu_grad = activated_grad * up_part
    gate_part_grad = (
        silu_grad * gate_sig + silu_grad * gate_part * gate_sig * (1.0 - gate_sig)
    ).astype(LOW)
    up_part_grad = (activated_grad * (gate_part * gate_sig)).astype(LOW)
    token_part = (
        dot_right_t(gate_part_grad, gate_full) + dot_right_t(up_part_grad, up_full)
    ).astype(LOW).reshape(2, 4, SEQ, D)
    token_part = token_part[0].astype(WIDE) + swap_core(token_part[1]).astype(WIDE)
    token_part, hidden_two, gate_part_grad, up_part_grad, activated = fence(
        token_part, hidden_two, gate_part_grad, up_part_grad, activated
    )
    down_terms = dot_left_t(activated, seed_low).astype(LOW).reshape(PLANE, 32, D)
    ffn_terms = jnp.concatenate(
        [
            dot_left_t(hidden_two, gate_part_grad).astype(LOW).reshape(PLANE, 96, 512),
            dot_left_t(hidden_two, up_part_grad).astype(LOW).reshape(PLANE, 96, 512),
            down_terms[:, :, :512],
            down_terms[:, :, 512:1024],
            down_terms[:, :, 1024:],
        ],
        axis=1,
    )
    half_one, half_two, ffn_terms = fence(*far_halves(token_part), ffn_terms)
    ffn_sum = fence(lax.psum_scatter(ffn_terms, XY, scatter_dimension=0, tiled=False))[0]
    near_one, near_two = near_blocks(token_part, (half_one, half_two))
    hidden_two_grad = token_part[0] + near_one.astype(WIDE) + near_two.astype(WIDE)
    hidden_two_grad, activated = fence(hidden_two_grad, activated)
    out_part = dot_plain(activated, down_full).astype(LOW).reshape(GROUP, SEQ, D)
    deep = lax.axis_index("z")
    places = jnp.array([0, 2, 3, 1], jnp.int32)
    out_part = jnp.stack(
        [
            lax.dynamic_index_in_dim(
                out_part,
                4 * ((place - core) % 2) + places[(place // 2 - deep) % 4],
                0,
                keepdims=False,
            )
            for place in range(GROUP)
        ]
    )
    ffn_sum, out_part = fence(ffn_sum, out_part)
    out_sum = lax.psum_scatter(out_part, ZC, scatter_dimension=0, tiled=False)

    gain_two_grad = jnp.sum(normed_two * hidden_two_grad, axis=0)
    mixed_grad = seed_grad + norm_back(normed_two, inverse_two, hidden_two_grad * gain_two)
    mixed_low = lax.all_gather(mixed_grad.astype(LOW), "c", axis=0, tiled=True)
    gated_grad = dot_right_t(mixed_low, out_rows)
    mixed_half = lax.dynamic_slice_in_dim(mixed_low, core * HALF, HALF, axis=1)
    out_terms = dot_left_t(gated_full, mixed_half).astype(LOW).reshape(4, 4, 96, HALF)
    gated_grad, out_terms = fence(gated_grad, out_terms)
    out_terms = direct_sum(out_terms, "x", 0).astype(LOW)
    raw_grad, forget_sums, gain_sums = attend_back(raw, gated_grad, attended, prob, gains)
    pieces = direct_exchange(raw_grad, "z")
    raw_flat = jnp.concatenate([raw_grad[matrix] for matrix in range(4)], axis=1)

    slots = lax.broadcasted_iota(jnp.int32, (SEQ, SEQ), 0)
    later = (slots >= lax.broadcasted_iota(jnp.int32, (SEQ, SEQ), 1)).astype(WIDE)
    log_forget_grad = jnp.einsum(
        "bhu,ut->bth",
        forget_sums[:, :HEADS],
        later,
        precision=lax.Precision.HIGHEST,
        preferred_element_type=WIDE,
    ).reshape(2 * SEQ, HEADS)
    forget_arg_grad = log_forget_grad * (1.0 - lax.logistic(forget_arg))
    forget_low_grad = forget_arg_grad.astype(LOW)
    query_gain_grad = gain_sums[0, :HD] + gain_sums[0, HD:]
    key_gain_grad = gain_sums[1, :HD] + gain_sums[1, HD:]
    token_part = (
        dot_right_t(raw_flat, proj_full) + dot_right_t(forget_low_grad, forget_low)
    ).reshape(2, SEQ, D)
    *pieces, out_terms, token_part, forget_low_grad, ffn_sum = fence(
        *pieces, out_terms, token_part, forget_low_grad, ffn_sum
    )

    terms = dot_left_t(hidden_deep, jnp.concatenate(pieces)).astype(LOW).reshape(4, 4, 96, HALF)
    out_terms = [out_terms[:, None, :, :384], out_terms[:, None, :, 384:]]
    second = jnp.concatenate([jnp.moveaxis(terms[..., 384:], 1, 0), *out_terms], axis=1)
    first, second = fence(terms[..., :384], second)
    first = direct_sum(first, "x", 0).astype(LOW)
    second = direct_sum(second, "y", 0).astype(LOW)
    hidden_one_grad = reduce_core(token_part, core)
    pair_back = jnp.moveaxis(ffn_sum[:192].reshape(2, GROUP, 12, FF_PART), 1, 0)
    pair_back = lax.all_to_all(pair_back, ZC, 0, 0, tiled=True)
    pair_back = pair_back.reshape(GROUP, 24, 4, 128).transpose(2, 1, 0, 3).reshape(96, 1024)
    pair_back = dot_plain(pair_back, order).reshape(4, 24, 1024)
    ffn_grad = pair_back.transpose(1, 0, 2).reshape(2, 12, FF)
    down_grad = [ffn_sum[at : at + 32].astype(WIDE) for at in (192, 224, 256)]
    down_grad = jnp.concatenate(down_grad, axis=1)

    gain_one_grad = jnp.sum(normed_one * hidden_one_grad, axis=0)
    input_grad = mixed_grad + norm_back(normed_one, inverse_one, hidden_one_grad * gain_one)
    forget_bias_grad = lax.dynamic_update_slice_in_dim(
        jnp.zeros((H,), WIDE), jnp.sum(forget_arg_grad, axis=0), core * HEADS, axis=0
    )
    blank = jnp.zeros_like(forget_low_grad)
    forget_wide = jnp.where(
        core == 0,
        jnp.concatenate([forget_low_grad, blank], axis=1),
        jnp.concatenate([blank, forget_low_grad], axis=1),
    )
    forget_w_grad = dot_left_t(forget_wide, hidden_one)
    members = [
        (attn_weights, None, attn_rows, attn_cols, D),
        (ffn_weights, ffn_grad, ffn_rows, ffn_cols, D),
        (down_weight[None], down_grad[None], down_rows[None], down_cols[None], FF),
    ]
    stats = [None] + [local_stats(*member[:3]) for member in members[1:]]
    scalars = [*stats[1][2:4], *stats[2][2:4], query_gain_grad, key_gain_grad, forget_bias_grad]
    flat = jnp.concatenate(
        [
            padded(stats[1][1], 8192),
            padded(stats[1][4], 8192),
            padded(stats[2][1], 2048),
            padded(stats[2][4], 2048),
            gain_one_grad,
            gain_two_grad,
            padded(jnp.concatenate(scalars), 1024),
            padded(forget_w_grad, 36864 + 4096),
        ]
    )
    first, second, hidden_one_grad, flat = fence(first, second, hidden_one_grad, flat)
    first = direct_sum(first, "y", 0)
    out_terms = direct_sum(second[4:].reshape(2, 4, 24, 384), "z", 1)
    second = direct_sum(second[:4], "x", 0)
    first, second, out_terms, flat = fence(first, second, out_terms, spread_sum(flat))
    attn_sum = jnp.concatenate([first, second], axis=1).astype(LOW).reshape(GROUP, 12, HALF)
    attn_back = lax.all_to_all(attn_sum, ZC, 0, 0, tiled=True).reshape(4, 2, 12, HALF)
    attn_back = attn_back.transpose(0, 2, 1, 3).reshape(4, 12, D).astype(WIDE)
    out_back = out_terms.transpose(1, 0, 2).reshape(2, 12, HALF)
    out_back = lax.all_to_all(out_back, "c", 0, 0, tiled=True)
    out_back = out_back.transpose(1, 0, 2).reshape(1, 12, D)
    attn_grad = jnp.concatenate([attn_back, out_back])
    members[0] = (attn_weights, attn_grad, attn_rows, attn_cols, D)
    stats[0] = local_stats(*members[0][:3])
    attn_flat = jnp.concatenate(
        [
            padded(jnp.concatenate([stats[0][1].reshape(-1), *stats[0][2:4]]), 8192),
            padded(stats[0][4], 8192),
        ]
    )
    attn_flat, flat, out_sum = fence(attn_flat, spread_back(flat), out_sum)
    block_out = (mixed_sum + out_sum.astype(WIDE)).astype(LOW)
    attn_flat = spread_back(spread_sum(attn_flat))
    scalars = flat[23552:24576]
    sums_all = [
        attn_flat[:7680].reshape(5, D),
        attn_flat[7680:7685],
        attn_flat[7685:7690],
        attn_flat[8192:15872].reshape(5, D),
        flat[:8192].reshape(2, FF),
        scalars[:2],
        scalars[2:4],
        flat[8192:16384].reshape(2, FF),
        flat[16384:17920].reshape(1, D),
        scalars[4:5],
        scalars[5:6],
        flat[18432:19968].reshape(1, D),
    ]
    small_total = jnp.concatenate(
        [flat[20480:23552], scalars[6 : 6 + 2 * HD + H], flat[24576 : 24576 + D * H].reshape(H, D).T.reshape(-1)]
    )
    results = []
    for member_id in range(3):
        weight, grad_value, _, cols_old, all_rows = members[member_id]
        column_sum, row_sum, weight_sum, scaled = sums_all[4 * member_id : 4 * member_id + 4]
        rows_new = stats[member_id][0]
        cols_new, row_mean, update = factor_update(
            grad_value, rows_new, cols_old, column_sum, row_sum, all_rows
        )
        entries = all_rows * weight.shape[2]
        mean_square = row_mean * jnp.sum(scaled / cols_new, axis=1) / entries
        fresh = apply_step(weight, update, mean_square, weight_sum, entries)
        results.append((fresh, rows_new, cols_new))
    small_new, small_moments_new = small_update(small_params, small_total, small_moments)
    attn_new = results[0][0]
    ffn_new = results[1][0]
    down_new = results[2][0][0]
    return (
        block_out,
        input_grad,
        attn_grad,
        attn_new,
        attn_new.astype(LOW),
        results[0][1],
        results[0][2],
        ffn_grad,
        ffn_new,
        ffn_new.astype(LOW),
        results[1][1],
        results[1][2],
        down_grad,
        down_new,
        down_new.astype(LOW),
        results[2][1][0],
        results[2][2][0],
        small_total,
        small_new,
        small_moments_new,
    )


def solution(mesh):
    chips = Mesh(mesh.devices.reshape(4, 4, 4, 2), ALL)
    rows_first = P(ALL, None)
    rows_second = P(None, ALL, None)
    stat_rows = P(None, ALL)
    flat = P(ALL)
    whole = P()
    return jax.shard_map(
        shards,
        mesh=chips,
        in_specs=(
            rows_first,
            rows_first,
            flat,
            rows_second,
            stat_rows,
            whole,
            rows_second,
            stat_rows,
            whole,
            rows_first,
            flat,
            whole,
            whole,
            whole,
        ),
        out_specs=(
            rows_first,
            rows_first,
            rows_second,
            rows_second,
            rows_second,
            stat_rows,
            whole,
            rows_second,
            rows_second,
            rows_second,
            stat_rows,
            whole,
            rows_first,
            rows_first,
            rows_first,
            flat,
            whole,
            whole,
            whole,
            whole,
        ),
        check_vma=False,
    )
```

```python
import jax
import jax.numpy as jnp
from jax import lax
from jax.experimental import pallas as pl
from jax.experimental.pallas import tpu as pltpu
from jax.sharding import Mesh
from jax.sharding import PartitionSpec as P

D = 1536
H = 24
HD = 64
FF = 4096
SEQ = 128
HALF = D // 2
HEADS = H // 2
GROUP = 8
PLANE = 16
CHIPS = 64
DEVICES = 128
FF_PART = FF // GROUP
OWN_HEADS = H // GROUP
FLAT_ROWS = 640
FLAT_ROW_SUMS = 120
FLAT_SMALL = 280
FLAT_FORGET = 306
FLAT_WEIGHTS = 594
FLAT_END = 602
OWN = 4 * OWN_HEADS * HD
RAW = OWN + 2 * SEQ
WIDE_HEADS = OWN_HEADS * 2 * HD

BETA = 0.5
CLIP = 0.1
RATE = 3.0
EPS_NORM = 1e-06
EPS_STAT = 1e-30
NEG_FILL = -1e30
LOW = jnp.bfloat16
WIDE = jnp.float32

ALL = ("x", "y", "z", "c")
XYZ = ("x", "y", "z")
XY = ("x", "y")
ZC = ("z", "c")


def dot_plain(left_side, right_side):
    return jnp.dot(left_side, right_side, preferred_element_type=WIDE)


def dot_right_t(left_side, right_side):
    return lax.dot_general(
        left_side, right_side, (((1,), (1,)), ((), ())), preferred_element_type=WIDE
    )


def dot_left_t(left_side, right_side):
    return lax.dot_general(
        left_side, right_side, (((0,), (0,)), ((), ())), preferred_element_type=WIDE
    )


def inverse_rms(values):
    return lax.rsqrt(jnp.mean(values * values, axis=-1, keepdims=True) + EPS_NORM)


def norm_back(normed, inverse, grad_out):
    return inverse * (grad_out - normed * jnp.mean(grad_out * normed, axis=-1, keepdims=True))


def split_small(vector):
    widths = [D, D, HD, HD, H]
    pieces = []
    offset = 0
    for piece_width in widths:
        pieces.append(vector[offset : offset + piece_width])
        offset = offset + piece_width
    pieces.append(vector[offset:].reshape(D, H))
    return pieces


SMALL_WIDTHS = (D, D, HD, HD, H, D * H)


def square_sum(weight):
    return jnp.sum(weight * weight, axis=(1, 2))


def fence(*values):
    return lax.optimization_barrier(values)


def swap_core(value):
    return lax.ppermute(value, "c", [(0, 1), (1, 0)])


def reduce_core(part, core):
    keep = lax.dynamic_index_in_dim(part, core, 0, keepdims=False)
    send = lax.dynamic_index_in_dim(part, 1 - core, 0, keepdims=False)
    return keep + swap_core(send)


def hop(value, axis, step):
    return lax.ppermute(value, axis, [(i, (i + step) % 4) for i in range(4)])


def assemble_kernel(
    place_ref, own, near, far_one, far_two, other, near_other, far_other, whole_ref
):
    deep = place_ref[0]
    core = place_ref[1]
    rows = own.shape[0]
    half = rows // 2

    def put(step, side, start, value):
        at = lax.rem(deep + step, 4)
        whole_ref[at, side, start : start + value.shape[0], :] = value

    put(0, core, 0, own[...])
    put(0, 1 - core, 0, other[...])
    put(3, core, 0, near[:rows])
    put(1, core, 0, near[rows:])
    put(3, 1 - core, 0, near_other[:rows])
    put(1, 1 - core, 0, near_other[rows:])
    put(2, core, 0, far_one[...])
    put(2, core, half, far_two[...])
    put(2, 1 - core, 0, far_other[...])


def assemble(*pieces):
    place = jnp.stack([lax.axis_index("z"), lax.axis_index("c")]).astype(jnp.int32)
    rows, columns = pieces[0].shape
    whole = pl.pallas_call(
        assemble_kernel,
        in_specs=[pl.BlockSpec(memory_space=pltpu.SMEM)]
        + [pl.BlockSpec(memory_space=pltpu.VMEM)] * len(pieces),
        out_shape=jax.ShapeDtypeStruct((4, 2, rows, columns), pieces[0].dtype),
        compiler_params=pltpu.CompilerParams(vmem_limit_bytes=40 * 1024 * 1024),
        name="assemble",
    )(place, *pieces)
    return whole.reshape(GROUP * rows, columns)


def gather_group(value, *others):
    rows = value.shape[0] // 2
    before = hop(value, "z", 1)
    after = hop(value, "z", -1)
    other = swap_core(value)
    before, after, other = fence(before, after, other)
    near = jnp.concatenate([before, after])
    far_one = hop(before[:rows], "z", 1)
    far_two = hop(after[rows:], "z", -1)
    near_other = swap_core(near)
    far_one, far_two, near_other, *others = fence(far_one, far_two, near_other, *others)
    far_other = swap_core(jnp.concatenate([far_one, far_two]))
    whole = assemble(value, near, far_one, far_two, other, near_other, far_other)
    return (whole, *others)


def far_halves(part):
    rows = SEQ // 2
    far = part[3].astype(LOW)
    return (hop(far[:rows], "z", 1), hop(far[rows:], "z", -1))


def near_blocks(part, halves):
    rows = SEQ // 2
    to_after = jnp.concatenate([part[2][:rows] + halves[0].astype(WIDE), part[2][rows:]])
    to_before = jnp.concatenate([part[1][:rows], part[1][rows:] + halves[1].astype(WIDE)])
    return (hop(to_after.astype(LOW), "z", 1), hop(to_before.astype(LOW), "z", -1))


def group_reduce_start(part, core, deep):
    got = swap_core(lax.dynamic_index_in_dim(part, 1 - core, 1, keepdims=False))
    part = lax.dynamic_index_in_dim(part, core, 1, keepdims=False)
    part = part.astype(WIDE) + got.astype(WIDE)
    return [
        lax.dynamic_index_in_dim(part, (deep + step) % 4, 0, keepdims=False)
        for step in (0, 3, 1, 2)
    ]


def direct_sum(blocks, axis, dim):
    here = lax.axis_index(axis)
    total = lax.dynamic_index_in_dim(blocks, here, dim, keepdims=False).astype(WIDE)
    for step in (1, 2, 3):
        block = lax.dynamic_index_in_dim(blocks, (here + step) % 4, dim, keepdims=False)
        total = total + hop(block, axis, step).astype(WIDE)
    return total


def split_far(blocks, axis):
    far = lax.dynamic_index_in_dim(blocks, (lax.axis_index(axis) + 2) % 4, 0, keepdims=False)
    half = far.shape[0] // 2
    return (hop(far[:half], axis, 1), hop(far[half:], axis, -1))


def split_near(blocks, axis, halves):
    here = lax.axis_index(axis)
    after = lax.dynamic_index_in_dim(blocks, (here + 1) % 4, 0, keepdims=False)
    before = lax.dynamic_index_in_dim(blocks, (here + 3) % 4, 0, keepdims=False)
    half = after.shape[0] // 2
    to_after = jnp.concatenate([after[:half] + halves[0], after[half:]])
    to_before = jnp.concatenate([before[:half], before[half:] + halves[1]])
    return (hop(to_after, axis, 1), hop(to_before, axis, -1))


def split_sum(blocks, axis, near):
    own = lax.dynamic_index_in_dim(blocks, lax.axis_index(axis), 0, keepdims=False)
    return (own.astype(WIDE) + near[0].astype(WIDE) + near[1].astype(WIDE)).astype(LOW)


def direct_exchange(blocks, axis):
    here = lax.axis_index(axis)
    pieces = [lax.dynamic_index_in_dim(blocks, here, 0, keepdims=False)]
    for step in (1, 2, 3):
        block = lax.dynamic_index_in_dim(blocks, (here + step) % 4, 0, keepdims=False)
        pieces.append(hop(block, axis, step))
    return pieces


def head_stat(values, lane_low):
    low = jnp.sum(jnp.where(lane_low, values, 0.0), axis=-1, keepdims=True) * (1.0 / HD)
    high = jnp.sum(jnp.where(lane_low, 0.0, values), axis=-1, keepdims=True) * (1.0 / HD)
    return jnp.where(lane_low, low, high)


def head_normed(values, lane_low):
    inverse = lax.rsqrt(head_stat(values * values, lane_low) + EPS_NORM)
    return (values * inverse, inverse)


def attend_kernel(
    raw_ref, bias_ref, length_ref, gains_ref, gated_ref, attended_ref, prob_ref
):
    lane = lax.broadcasted_iota(jnp.int32, (SEQ, SEQ), 1)
    lane_low = lane < HD
    slot = lax.broadcasted_iota(jnp.int32, (SEQ, SEQ), 0)
    allowed = (lane <= slot) & (lane.astype(WIDE) < length_ref[0])
    forget = raw_ref[:, RAW - SEQ :] + bias_ref[0:1]
    mine = (lane >= HD) & (lane < HD + OWN_HEADS)
    log_forget = -jnp.log1p(jnp.exp(jnp.where(mine, -forget, 0.0)))
    cols = lax.dot_general(
        (lane <= slot).astype(WIDE),
        log_forget,
        (((1,), (0,)), ((), ())),
        precision=lax.Precision.HIGHEST,
        preferred_element_type=WIDE,
    )
    rows = cols.T
    for head in range(OWN_HEADS):
        at = 2 * head * SEQ
        normed, _ = head_normed(raw_ref[:, at : at + SEQ], lane_low)
        scaled = normed * gains_ref[0:1]
        query = jnp.where(lane_low, scaled, 0.0).astype(LOW)
        key = pltpu.roll(scaled, HD, 1).astype(LOW)
        value_gate = raw_ref[:, at + SEQ : at + 2 * SEQ]
        score = dot_right_t(query, key) * (HD**-0.5)
        score = score + cols[:, HD + head : HD + head + 1]
        score = score - rows[HD + head : HD + head + 1]
        score = jnp.where(allowed, score, NEG_FILL)
        weight = jnp.exp(score - jnp.max(score, axis=-1, keepdims=True))
        prob = weight / jnp.sum(weight, axis=-1, keepdims=True)
        prob_ref[0, head] = prob
        attended = dot_plain(prob.astype(LOW), value_gate.astype(LOW))
        gate = lax.logistic(pltpu.roll(value_gate, HD, 1))
        attended_ref[:, head * SEQ : (head + 1) * SEQ] = attended
        gated = jnp.where(lane_low, attended * gate, 0.0)
        gated_ref[:, head * SEQ : (head + 1) * SEQ] = gated.astype(LOW)


def attend(raw, bias, lengths, gains):
    return pl.pallas_call(
        attend_kernel,
        grid=(GROUP,),
        in_specs=[
            pl.BlockSpec((SEQ, RAW), lambda i: (i, 0)),
            pl.BlockSpec((8, SEQ), lambda i: (0, 0)),
            pl.BlockSpec((1, 1, SEQ), lambda i: (i, 0, 0)),
            pl.BlockSpec((8, SEQ), lambda i: (0, 0)),
        ],
        out_specs=[
            pl.BlockSpec((SEQ, WIDE_HEADS), lambda i: (i, 0)),
            pl.BlockSpec((SEQ, WIDE_HEADS), lambda i: (i, 0)),
            pl.BlockSpec((1, OWN_HEADS, SEQ, SEQ), lambda i: (i, 0, 0, 0)),
        ],
        out_shape=[
            jax.ShapeDtypeStruct((GROUP * SEQ, WIDE_HEADS), LOW),
            jax.ShapeDtypeStruct((GROUP * SEQ, WIDE_HEADS), WIDE),
            jax.ShapeDtypeStruct((GROUP, OWN_HEADS, SEQ, SEQ), WIDE),
        ],
        compiler_params=pltpu.CompilerParams(vmem_limit_bytes=40 * 1024 * 1024),
        cost_estimate=pl.CostEstimate(
            flops=24 * 4 * SEQ**3, bytes_accessed=6_000_000, transcendentals=24 * SEQ * SEQ
        ),
        name="attend",
    )(raw, bias, lengths, gains)


def attend_back_kernel(
    raw_ref, gated_grad_ref, attended_ref, prob_ref, gains_ref, grad_ref, forget_ref, gain_ref
):
    lane_low = lax.broadcasted_iota(jnp.int32, (SEQ, SEQ), 1) < HD
    ones = jnp.ones((8, SEQ), LOW)
    gains = gains_ref[0:1]
    forget_ref[...] = jnp.zeros_like(forget_ref)

    @pl.when(pl.program_id(0) == 0)
    def _():
        gain_ref[...] = jnp.zeros_like(gain_ref)

    for head in range(OWN_HEADS):
        at = 2 * head * SEQ
        normed, inverse = head_normed(raw_ref[:, at : at + SEQ], lane_low)
        swapped = pltpu.roll(normed * gains, HD, 1).astype(LOW)
        value_gate = raw_ref[:, at + SEQ : at + 2 * SEQ]
        gate = lax.logistic(pltpu.roll(value_gate, HD, 1))
        gated_grad = gated_grad_ref[:, head * SEQ : (head + 1) * SEQ]
        gated_grad = jnp.where(lane_low, gated_grad, 0.0)
        out_grad = (gated_grad * gate).astype(LOW)
        attended = attended_ref[:, head * SEQ : (head + 1) * SEQ]
        gate_grad = gated_grad * attended * gate * (1.0 - gate)
        prob = prob_ref[0, head]
        prob_grad = dot_right_t(out_grad, value_gate.astype(LOW))
        delta = jnp.sum(prob * prob_grad, axis=-1, keepdims=True)
        score_grad = (prob * (prob_grad - delta)).astype(LOW)
        value_grad = dot_left_t(prob.astype(LOW), out_grad)
        value_gate_grad = jnp.where(lane_low, value_grad, pltpu.roll(gate_grad, HD, 1))
        grad_ref[:, at + SEQ : at + 2 * SEQ] = value_gate_grad.astype(LOW)
        sums = dot_right_t(ones, score_grad) - dot_plain(ones, score_grad)
        forget_ref[0, head : head + 1] = sums[0:1]
        grad = jnp.where(
            lane_low, dot_plain(score_grad, swapped), dot_left_t(score_grad, swapped)
        ) * (HD**-0.5)
        product = grad * normed
        gain_ref[0:1] += jnp.sum(product, axis=0, keepdims=True)
        mean = head_stat(product * gains, lane_low)
        grad_ref[:, at : at + SEQ] = (inverse * (grad * gains - normed * mean)).astype(LOW)


def attend_back(raw, gated_grad, attended, prob, gains):
    return pl.pallas_call(
        attend_back_kernel,
        grid=(GROUP,),
        in_specs=[
            pl.BlockSpec((SEQ, RAW), lambda i: (i, 0)),
            pl.BlockSpec((SEQ, WIDE_HEADS), lambda i: (i, 0)),
            pl.BlockSpec((SEQ, WIDE_HEADS), lambda i: (i, 0)),
            pl.BlockSpec((1, OWN_HEADS, SEQ, SEQ), lambda i: (i, 0, 0, 0)),
            pl.BlockSpec((8, SEQ), lambda i: (0, 0)),
        ],
        out_specs=[
            pl.BlockSpec((SEQ, OWN), lambda i: (i, 0)),
            pl.BlockSpec((1, 8, SEQ), lambda i: (i, 0, 0)),
            pl.BlockSpec((8, SEQ), lambda i: (0, 0)),
        ],
        out_shape=[
            jax.ShapeDtypeStruct((GROUP * SEQ, OWN), LOW),
            jax.ShapeDtypeStruct((GROUP, 8, SEQ), WIDE),
            jax.ShapeDtypeStruct((8, SEQ), WIDE),
        ],
        compiler_params=pltpu.CompilerParams(vmem_limit_bytes=40 * 1024 * 1024),
        cost_estimate=pl.CostEstimate(
            flops=24 * 10 * SEQ**3, bytes_accessed=8_000_000, transcendentals=2 * SEQ * HALF
        ),
        name="attend_back",
    )(raw, gated_grad, attended, prob, gains)


def half_tile(ref, matrix, head):
    tile = ref[matrix, :, SEQ * (head // 2) : SEQ * (head // 2) + SEQ]
    return (tile, pltpu.roll(tile, HD, 1))[:: 1 if head % 2 == 0 else -1]


def pack_kernel(length_ref, weight_ref, forget_ref, packed_ref):
    lane = lax.broadcasted_iota(jnp.int32, (12, SEQ), 1)
    lane_low = lane < HD
    forget = forget_ref[...]
    length = jnp.where(lane == SEQ - 1, length_ref[0], 0.0)
    for place in range(GROUP):
        for slot in range(OWN_HEADS):
            head = OWN_HEADS * place + slot
            for pair in range(2):
                left, _ = half_tile(weight_ref, 2 * pair, head)
                _, right = half_tile(weight_ref, 2 * pair + 1, head)
                at = (2 * slot + pair) * SEQ
                tile = jnp.where(lane_low, left, right)
                packed_ref[place, :, at : at + SEQ] = tile.astype(LOW)
        first, _ = half_tile(weight_ref, 4, OWN_HEADS * place)
        _, second = half_tile(weight_ref, 4, OWN_HEADS * place + 1)
        third, _ = half_tile(weight_ref, 4, OWN_HEADS * place + 2)
        packed_ref[place, :, OWN : OWN + SEQ] = jnp.where(lane_low, first, second).astype(LOW)
        rest = pltpu.roll(forget, (HD - OWN_HEADS * place) % SEQ, 1)
        rest = jnp.where(lane < HD + OWN_HEADS, rest, length)
        packed_ref[place, :, OWN + SEQ :] = jnp.where(lane_low, third, rest).astype(LOW)


def pack(length, weights, forget):
    return pl.pallas_call(
        pack_kernel,
        in_specs=[
            pl.BlockSpec(memory_space=pltpu.SMEM),
            pl.BlockSpec(memory_space=pltpu.VMEM),
            pl.BlockSpec(memory_space=pltpu.VMEM),
        ],
        out_shape=jax.ShapeDtypeStruct((GROUP, 12, RAW), LOW),
        compiler_params=pltpu.CompilerParams(vmem_limit_bytes=40 * 1024 * 1024),
        name="pack",
    )(length, weights, forget)


def spread_rows_kernel(blocks_ref, rows_ref):
    for head in range(OWN_HEADS):
        at = head * SEQ
        for pair in range(GROUP // 2):
            left = blocks_ref[2 * pair, head * HD : head * HD + HD, :]
            right = blocks_ref[2 * pair + 1, head * HD : head * HD + HD, :]
            both = jnp.concatenate([left, right], axis=1)
            rows_ref[at : at + HD, 384 * pair : 384 * pair + 384] = both
        rows_ref[at + HD : at + SEQ, :] = jnp.zeros((HD, D), LOW)


def collect_rows_kernel(rows_ref, blocks_ref):
    for head in range(OWN_HEADS):
        at = head * SEQ
        for pair in range(GROUP // 2):
            both = rows_ref[at : at + HD, 384 * pair : 384 * pair + 384].astype(LOW)
            blocks_ref[2 * pair, head * HD : head * HD + HD, :] = both[:, : 3 * HD]
            blocks_ref[2 * pair + 1, head * HD : head * HD + HD, :] = both[:, 3 * HD :]


def move_rows(kernel, value, shape):
    return pl.pallas_call(
        kernel,
        out_shape=jax.ShapeDtypeStruct(shape, LOW),
        compiler_params=pltpu.CompilerParams(vmem_limit_bytes=40 * 1024 * 1024),
        name="move_rows",
    )(value)


def unpack_kernel(packed_ref, grad_ref):
    lane_low = lax.broadcasted_iota(jnp.int32, (12, SEQ), 1) < HD

    def tile_of(place, at):
        tile = packed_ref[place, :, at : at + SEQ]
        return (tile, pltpu.roll(tile, HD, 1))

    for left in range(0, H, 2):
        places = [(head // OWN_HEADS, head % OWN_HEADS) for head in (left, left + 1)]
        at = SEQ * (left // 2)
        for pair in range(2):
            tiles = [tile_of(place, (2 * slot + pair) * SEQ) for place, slot in places]
            grad_ref[2 * pair, :, at : at + SEQ] = jnp.where(lane_low, tiles[0][0], tiles[1][1])
            grad_ref[2 * pair + 1, :, at : at + SEQ] = jnp.where(lane_low, tiles[0][1], tiles[1][0])
        picked = []
        for side, (place, slot) in enumerate(places):
            tile = tile_of(place, OWN + SEQ * (slot // 2))
            picked.append(tile[(slot % 2) ^ side])
        grad_ref[4, :, at : at + SEQ] = jnp.where(lane_low, picked[0], picked[1])


def tiles_of(columns):
    return [(tile, tile * SEQ) for tile in range(columns // SEQ)]


def row_stats(grad_ref, rows_old, columns):
    total = jnp.zeros((grad_ref.shape[0], SEQ), WIDE)
    for _, at in tiles_of(columns):
        part = grad_ref[:, at : at + SEQ]
        total = total + part * part
    mean = jnp.sum(total, axis=1, keepdims=True) * (1.0 / columns)
    return BETA * rows_old + (1.0 - BETA) * (mean + EPS_STAT)


def column_stats(grad_ref, rows_new, columns, flat_ref, plain_at, scaled_at):
    for tile, at in tiles_of(columns):
        part = grad_ref[:, at : at + SEQ]
        part = part * part
        plain = jnp.sum(part, axis=0, keepdims=True)
        scaled = jnp.sum(part / rows_new, axis=0, keepdims=True)
        flat_ref[plain_at + tile : plain_at + tile + 1] = plain
        flat_ref[scaled_at + tile : scaled_at + tile + 1] = scaled


def measure_kernel(
    sums_ref,
    packed_ref,
    pair_ref,
    ffn_ref,
    attn_rows_ref,
    ffn_rows_ref,
    down_rows_ref,
    small_ref,
    forget_ref,
    attn_grad_ref,
    ffn_grad_ref,
    down_grad_ref,
    attn_rows_new_ref,
    ffn_rows_new_ref,
    down_rows_new_ref,
    flat_ref,
):
    unpack_kernel(packed_ref, attn_grad_ref)
    for block in range(4):
        for matrix in range(2):
            row = 24 * block + 12 * matrix
            ffn_grad_ref[matrix, :, 1024 * block : 1024 * block + 1024] = pair_ref[row : row + 12]
    for part in range(3):
        rows = ffn_ref[192 + 32 * part : 224 + 32 * part]
        down_grad_ref[:, 512 * part : 512 * part + 512] = rows.astype(WIDE)
    flat_ref[FLAT_END:] = jnp.zeros((FLAT_ROWS - FLAT_END, SEQ), WIDE)
    for matrix in range(8):
        value = jnp.full((1, SEQ), sums_ref[matrix], WIDE)
        flat_ref[FLAT_WEIGHTS + matrix : FLAT_WEIGHTS + matrix + 1] = value
    flat_ref[FLAT_SMALL : FLAT_SMALL + 26] = small_ref[...]
    flat_ref[FLAT_FORGET : FLAT_FORGET + 288] = forget_ref[...]
    groups = (
        (attn_grad_ref, attn_rows_ref, attn_rows_new_ref, 5, D, 0, 60, 0),
        (ffn_grad_ref, ffn_rows_ref, ffn_rows_new_ref, 2, FF, 128, 192, 5),
        (down_grad_ref, down_rows_ref, down_rows_new_ref, 1, D, 256, 268, 7),
    )
    for grad_ref, old_ref, new_ref, count, columns, plain_at, scaled_at, first in groups:
        for matrix in range(count):
            mine = grad_ref if first == 7 else grad_ref.at[matrix]
            rows_new = row_stats(mine, old_ref[matrix], columns)
            new_ref[matrix] = rows_new
            at = matrix * (columns // SEQ)
            column_stats(mine, rows_new, columns, flat_ref, plain_at + at, scaled_at + at)
            value = jnp.broadcast_to(jnp.sum(rows_new, axis=0, keepdims=True), (1, SEQ))
            flat_ref[FLAT_ROW_SUMS + first + matrix : FLAT_ROW_SUMS + first + matrix + 1] = value


def measure(sums, packed, pair, ffn, attn_rows, ffn_rows, down_rows, small, forget):
    return pl.pallas_call(
        measure_kernel,
        in_specs=[pl.BlockSpec(memory_space=pltpu.SMEM)]
        + [pl.BlockSpec(memory_space=pltpu.VMEM)] * 8,
        out_shape=[
            jax.ShapeDtypeStruct((5, 12, D), WIDE),
            jax.ShapeDtypeStruct((2, 12, FF), WIDE),
            jax.ShapeDtypeStruct((32, D), WIDE),
            jax.ShapeDtypeStruct((5, 12, 1), WIDE),
            jax.ShapeDtypeStruct((2, 12, 1), WIDE),
            jax.ShapeDtypeStruct((1, 32, 1), WIDE),
            jax.ShapeDtypeStruct((FLAT_ROWS, SEQ), WIDE),
        ],
        compiler_params=pltpu.CompilerParams(vmem_limit_bytes=40 * 1024 * 1024),
        name="measure",
    )(sums, packed, pair, ffn, attn_rows, ffn_rows, down_rows, small, forget)


def square_total(values):
    return jnp.sum(jnp.sum(values * values, axis=0, keepdims=True), axis=1, keepdims=True)


def finish_kernel(
    flat_ref,
    attn_grad_ref,
    ffn_grad_ref,
    down_grad_ref,
    attn_ref,
    ffn_ref,
    down_ref,
    attn_rows_ref,
    ffn_rows_ref,
    down_rows_ref,
    attn_cols_ref,
    ffn_cols_ref,
    down_cols_ref,
    small_ref,
    moments_ref,
    attn_new_ref,
    ffn_new_ref,
    down_new_ref,
    attn_copy_ref,
    ffn_copy_ref,
    down_copy_ref,
    attn_cols_new_ref,
    ffn_cols_new_ref,
    down_cols_new_ref,
    small_new_ref,
    moments_new_ref,
):
    groups = (
        (attn_grad_ref, attn_ref, attn_rows_ref, attn_cols_ref)
        + (attn_new_ref, attn_copy_ref, attn_cols_new_ref, 5, D, D, 0, 60, 0),
        (ffn_grad_ref, ffn_ref, ffn_rows_ref, ffn_cols_ref)
        + (ffn_new_ref, ffn_copy_ref, ffn_cols_new_ref, 2, D, FF, 128, 192, 5),
        (down_grad_ref, down_ref, down_rows_ref, down_cols_ref)
        + (down_new_ref, down_copy_ref, down_cols_new_ref, 1, FF, D, 256, 268, 7),
    )
    for (
        grad_ref,
        old_ref,
        rows_ref,
        cols_ref,
        new_ref,
        copy_ref,
        cols_new_ref,
        count,
        all_rows,
        columns,
        plain_at,
        scaled_at,
        first,
    ) in groups:
        entries = all_rows * columns
        tiles = columns // SEQ
        for matrix in range(count):
            whole = first == 7
            grad = grad_ref if whole else grad_ref.at[matrix]
            old = old_ref if whole else old_ref.at[matrix]
            new = new_ref if whole else new_ref.at[matrix]
            copy = copy_ref if whole else copy_ref.at[matrix]
            at = matrix * tiles
            plain = flat_ref[plain_at + at : plain_at + at + tiles]
            scaled = flat_ref[scaled_at + at : scaled_at + at + tiles]
            cols_new = BETA * cols_ref[at : at + tiles] + (1.0 - BETA) * (
                plain * (1.0 / all_rows) + EPS_STAT
            )
            cols_new_ref[at : at + tiles] = cols_new
            row = FLAT_ROW_SUMS + first + matrix
            row_mean = flat_ref[row : row + 1] * (1.0 / all_rows)
            row = FLAT_WEIGHTS + first + matrix
            spread = jnp.sqrt(flat_ref[row : row + 1] * (1.0 / entries) + EPS_NORM)
            total = jnp.sum(scaled / cols_new, axis=0, keepdims=True)
            total = jnp.sum(total, axis=1, keepdims=True)
            mean_square = row_mean * total * (1.0 / entries)
            factor = RATE * spread / jnp.maximum(1.0, jnp.sqrt(mean_square) / CLIP)
            rows_scale = lax.rsqrt(rows_ref[matrix])
            cols_scale = lax.rsqrt(cols_new / row_mean) * factor
            for tile, place in tiles_of(columns):
                step = grad[:, place : place + SEQ] * rows_scale * cols_scale[tile : tile + 1]
                value = old[:, place : place + SEQ] - step
                new[:, place : place + SEQ] = value
                copy[:, place : place + SEQ] = value.astype(LOW)

    lane_low = lax.broadcasted_iota(jnp.int32, (1, SEQ), 1) < HD
    for start, rows, width, lanes in (
        (0, 12, D, None),
        (12, 12, D, None),
        (24, 1, HD, lane_low),
        (24, 1, HD, jnp.logical_not(lane_low)),
        (25, 1, H, None),
        (26, 288, D * H, None),
    ):
        param = small_ref[start : start + rows]
        grad = flat_ref[FLAT_SMALL + start : FLAT_SMALL + start + rows]
        fresh = BETA * moments_ref[start : start + rows] + (1.0 - BETA) * (grad * grad + EPS_STAT)
        update = grad * lax.rsqrt(fresh)
        if lanes is not None:
            update = jnp.where(lanes, update, 0.0)
        inside = param if lanes is None else jnp.where(lanes, param, 0.0)
        clip_ratio = jnp.sqrt(square_total(update) * (1.0 / width)) / CLIP
        spread = jnp.sqrt(square_total(inside) * (1.0 / width) + EPS_NORM)
        value = param - RATE * spread * (update / jnp.maximum(1.0, clip_ratio))
        if lanes is None:
            small_new_ref[start : start + rows] = value
        elif width == HD:
            held = small_new_ref[start : start + rows]
            small_new_ref[start : start + rows] = jnp.where(lanes, value, held)
        moments_new_ref[start : start + rows] = fresh


def finish(flat, grads, weights, rows, cols, small, moments):
    return pl.pallas_call(
        finish_kernel,
        in_specs=[pl.BlockSpec(memory_space=pltpu.VMEM)] * 15,
        out_shape=[
            jax.ShapeDtypeStruct((5, 12, D), WIDE),
            jax.ShapeDtypeStruct((2, 12, FF), WIDE),
            jax.ShapeDtypeStruct((32, D), WIDE),
            jax.ShapeDtypeStruct((5, 12, D), LOW),
            jax.ShapeDtypeStruct((2, 12, FF), LOW),
            jax.ShapeDtypeStruct((32, D), LOW),
            jax.ShapeDtypeStruct((60, SEQ), WIDE),
            jax.ShapeDtypeStruct((64, SEQ), WIDE),
            jax.ShapeDtypeStruct((12, SEQ), WIDE),
            jax.ShapeDtypeStruct((314, SEQ), WIDE),
            jax.ShapeDtypeStruct((314, SEQ), WIDE),
        ],
        compiler_params=pltpu.CompilerParams(vmem_limit_bytes=40 * 1024 * 1024),
        name="finish",
    )(flat, *grads, *weights, *rows, *cols, small, moments)


def small_rows(vector, fill):
    bias = vector[2 * D + 2 * HD : 2 * D + 2 * HD + H]
    bias = jnp.concatenate([bias, jnp.full((SEQ - H,), fill, WIDE)])
    return jnp.concatenate(
        [
            vector[: 2 * D].reshape(24, SEQ),
            vector[2 * D : 2 * D + 2 * HD].reshape(1, SEQ),
            bias.reshape(1, SEQ),
            vector[2 * D + 2 * HD + H :].reshape(288, SEQ),
        ]
    )


def small_vector(rows):
    return jnp.concatenate(
        [rows[:25].reshape(-1), rows[25, :H], rows[26:].reshape(-1)]
    )


def spread_sum(flat):
    pieces = flat.reshape(DEVICES, -1, SEQ)
    return jnp.sum(lax.all_to_all(pieces, ALL, 0, 0, tiled=True), axis=0)


def spread_back(mine):
    whole = jnp.broadcast_to(mine[None], (DEVICES, *mine.shape))
    return lax.all_to_all(whole, ALL, 0, 0, tiled=True).reshape(-1, SEQ)


def column_order():
    source = lax.broadcasted_iota(jnp.int32, (1024, 1024), 0)
    target = lax.broadcasted_iota(jnp.int32, (1024, 1024), 1)
    lane = source % 128
    return (target == (lane // 32) * 256 + (source // 128) * 32 + lane % 32).astype(LOW)


def shards(
    tokens,
    cotangent,
    lengths,
    attn_weights,
    attn_rows,
    attn_cols,
    ffn_weights,
    ffn_rows,
    ffn_cols,
    down_weight,
    down_rows,
    down_cols,
    small_params,
    small_moments,
):
    core = lax.axis_index("c")
    deep = lax.axis_index("z")
    inputs = tokens.astype(WIDE)
    slot_ids = jnp.arange(SEQ, dtype=jnp.int32)
    valid_rows = slot_ids < lengths[0]
    gain_one, gain_two, query_gain, key_gain, forget_bias, forget_weight = split_small(small_params)

    device = ((lax.axis_index("x") * 4 + lax.axis_index("y")) * 4 + deep) * 2 + core
    forget_rows = lax.dynamic_slice_in_dim(forget_weight, device * 12, 12, axis=0)
    forget_rows = jnp.pad(forget_rows, ((0, 0), (0, SEQ - H)))
    attn_low = pack(lengths.astype(WIDE), attn_weights, forget_rows)
    attn_low = lax.all_to_all(attn_low, ZC, 0, 0, tiled=True)
    lengths_group = attn_low[:, 0, RAW - 1].astype(WIDE)
    attn_low = attn_low.reshape(96, RAW)
    attn_full = lax.all_gather(attn_low, XY, axis=0, tiled=True)
    order = column_order()
    pair_low = ffn_weights.astype(LOW).reshape(24, 4, 1024).transpose(1, 0, 2).reshape(96, 1024)
    pair_low = dot_right_t(pair_low, order).astype(LOW).reshape(4, 2, 12, GROUP, 128)
    pair_low = pair_low.transpose(3, 2, 1, 0, 4).reshape(GROUP, 12, 2 * FF_PART)
    pair_low = lax.all_to_all(pair_low, ZC, 0, 0, tiled=True).reshape(96, 2 * FF_PART)
    down_low = jnp.concatenate(
        [down_weight[:, at : at + 512].astype(LOW) for at in (0, 512, 1024)], axis=0
    )
    seed_grad = cotangent.astype(WIDE) * valid_rows[:, None].astype(WIDE)
    seed_grad, pair_low, down_low = fence(seed_grad, pair_low, down_low)
    seed_low = lax.all_gather(seed_grad.astype(LOW), ZC, axis=0, tiled=True)
    ffn_full = lax.all_gather(
        jnp.concatenate([pair_low, down_low], axis=1), XY, axis=0, tiled=True
    )

    inverse_one = inverse_rms(inputs)
    normed_one = inputs * inverse_one
    attn_low, attn_weights, ffn_weights, down_weight, small_params = fence(
        attn_low, attn_weights, ffn_weights, down_weight, small_params
    )
    tokens_group = gather_group(tokens)[0]
    inputs_group = tokens_group.astype(WIDE)
    inverse_group = inverse_rms(inputs_group)
    hidden_one = (inputs_group * inverse_group * gain_one).astype(LOW)
    place = 2 * deep + core

    lengths_group = jnp.broadcast_to(lengths_group[:, None, None], (GROUP, 1, SEQ))
    forget_low = lax.dynamic_slice_in_dim(forget_weight, place * OWN_HEADS, OWN_HEADS, axis=1)
    forget_low = forget_low.astype(LOW)
    bias_mine = lax.dynamic_slice_in_dim(forget_bias, place * OWN_HEADS, OWN_HEADS, axis=0)
    bias_tile = jnp.pad(bias_mine[None], ((0, 7), (HD, HD - OWN_HEADS)))
    exact = {"precision": lax.Precision.HIGHEST, "preferred_element_type": WIDE}
    slots = lax.broadcasted_iota(jnp.int32, (SEQ, SEQ), 0)
    later = (slots >= lax.broadcasted_iota(jnp.int32, (SEQ, SEQ), 1)).astype(WIDE)
    gains = jnp.concatenate([query_gain, key_gain])[None]
    gains = jnp.pad(gains, ((0, 7), (0, 0)))
    param_rows = small_rows(small_params, 0.0)
    moment_rows = small_rows(small_moments, 1.0)
    old_rows = (attn_rows[:, :, None], ffn_rows[:, :, None], down_rows[None, :, None])
    old_cols = (
        attn_cols.reshape(60, SEQ),
        ffn_cols.reshape(64, SEQ),
        down_cols.reshape(12, SEQ),
    )
    weight_sums = jnp.concatenate(
        [square_sum(attn_weights), square_sum(ffn_weights), square_sum(down_weight[None])]
    )
    (
        attn_full,
        hidden_one,
        tokens_group,
        inverse_group,
        lengths_group,
        forget_low,
        bias_tile,
        gains,
        order,
        weight_sums,
        param_rows,
        moment_rows,
        old_rows,
        old_cols,
    ) = fence(
        attn_full,
        hidden_one,
        tokens_group,
        inverse_group,
        lengths_group,
        forget_low,
        bias_tile,
        gains,
        order,
        weight_sums,
        param_rows,
        moment_rows,
        old_rows,
        old_cols,
    )
    proj_full = attn_full[:, :OWN]
    raw, attn_full = fence(dot_plain(hidden_one, attn_full), attn_full)
    out_rows = attn_full[:, OWN : OWN + 3 * HD].reshape(GROUP, 3 * HD, 3 * HD)
    out_rows = lax.all_to_all(out_rows, ZC, 0, 0, tiled=True)
    gated_out, attended, prob = attend(raw, bias_tile, lengths_group, gains)
    out_rows = move_rows(spread_rows_kernel, out_rows, (WIDE_HEADS, D))
    mixed_part = dot_plain(gated_out, out_rows).astype(LOW).reshape(4, 2, SEQ, D)
    mixed_part = group_reduce_start(mixed_part, core, deep)
    half_one, half_two = fence(*far_halves(mixed_part))
    near_one, near_two = near_blocks(mixed_part, (half_one, half_two))
    mixed_sum = inputs + mixed_part[0] + near_one.astype(WIDE) + near_two.astype(WIDE)
    inverse_two = inverse_rms(mixed_sum)
    normed_two = mixed_sum * inverse_two
    hidden_two, ffn_full, seed_low = gather_group(
        (normed_two * gain_two).astype(LOW), ffn_full, seed_low
    )
    pair_full = ffn_full[:, : 2 * FF_PART]
    down_full = ffn_full[:, 2 * FF_PART :].reshape(PLANE, 3, 32, 512)
    down_full = jnp.concatenate(
        [down_full[:, part].reshape(FF_PART, 512) for part in range(3)], axis=1
    )

    gate_full = pair_full[:, :FF_PART]
    up_full = pair_full[:, FF_PART:]
    gate_part = dot_plain(hidden_two, gate_full)
    up_part = dot_plain(hidden_two, up_full)
    gate_sig = lax.logistic(gate_part)
    activated = (gate_part * gate_sig * up_part).astype(LOW)
    activated_grad = dot_right_t(seed_low, down_full)
    silu_grad = activated_grad * up_part
    gate_part_grad = silu_grad * gate_sig + silu_grad * gate_part * gate_sig * (1.0 - gate_sig)
    gate_part_grad = gate_part_grad.astype(LOW)
    up_part_grad = (activated_grad * (gate_part * gate_sig)).astype(LOW)
    token_part = dot_right_t(gate_part_grad, gate_full) + dot_right_t(up_part_grad, up_full)
    token_part = token_part.astype(LOW).reshape(4, 2, SEQ, D)
    token_part, hidden_two, gate_part_grad, up_part_grad, activated, seed_low, down_full = fence(
        token_part, hidden_two, gate_part_grad, up_part_grad, activated, seed_low, down_full
    )
    token_got, gate_terms, hidden_two, up_part_grad, activated, seed_low = fence(
        swap_core(lax.dynamic_index_in_dim(token_part, 1 - core, 1, keepdims=False)),
        dot_left_t(hidden_two, gate_part_grad).astype(LOW),
        hidden_two,
        up_part_grad,
        activated,
        seed_low,
    )
    token_part = lax.dynamic_index_in_dim(token_part, core, 1, keepdims=False)
    token_part = token_part.astype(WIDE) + token_got.astype(WIDE)
    token_part, hidden_two, up_part_grad = fence(token_part, hidden_two, up_part_grad)
    token_part = [
        lax.dynamic_index_in_dim(token_part, (deep + step) % 4, 0, keepdims=False)
        for step in (0, 3, 1, 2)
    ]
    half_one, half_two, up_terms, down_terms, activated = fence(
        *far_halves(token_part),
        dot_left_t(hidden_two, up_part_grad).astype(LOW),
        dot_left_t(activated, seed_low).astype(LOW),
        activated,
    )
    down_terms = down_terms.reshape(PLANE, 32, D)
    ffn_terms = jnp.concatenate(
        [
            gate_terms.reshape(PLANE, 96, FF_PART),
            up_terms.reshape(PLANE, 96, FF_PART),
            down_terms[:, :, :512],
            down_terms[:, :, 512:1024],
            down_terms[:, :, 1024:],
        ],
        axis=1,
    )
    out_part = dot_plain(activated, down_full).astype(LOW).reshape(GROUP, SEQ, D)
    near_one, near_two, ffn_terms, out_part = fence(
        *near_blocks(token_part, (half_one, half_two)), ffn_terms, out_part
    )
    ffn_sum = fence(lax.psum_scatter(ffn_terms, XY, scatter_dimension=0, tiled=False))[0]
    hidden_two_grad = token_part[0] + near_one.astype(WIDE) + near_two.astype(WIDE)

    gain_two_grad = jnp.sum(normed_two * hidden_two_grad, axis=0)
    mixed_grad = seed_grad + norm_back(normed_two, inverse_two, hidden_two_grad * gain_two)
    mixed_low, out_part = gather_group(mixed_grad.astype(LOW), out_part)
    gated_grad = dot_right_t(mixed_low, out_rows)
    out_terms = dot_left_t(gated_out, mixed_low)
    out_terms = move_rows(collect_rows_kernel, out_terms, (GROUP, 3 * HD, 3 * HD))
    gated_grad, out_terms = fence(gated_grad, out_terms)
    out_terms = lax.all_to_all(out_terms, ZC, 0, 0, tiled=True)
    raw_grad, forget_sums, gain_sums = attend_back(raw, gated_grad, attended, prob, gains)
    out_terms, raw_grad, forget_sums, gain_sums = fence(
        out_terms, raw_grad, forget_sums, gain_sums
    )
    terms = jnp.concatenate(
        [
            dot_left_t(hidden_one, raw_grad).astype(LOW).reshape(PLANE, 96, OWN),
            out_terms.reshape(PLANE, 96, 3 * HD),
        ],
        axis=2,
    )
    terms, raw_grad = fence(terms, raw_grad)
    terms = lax.all_to_all(terms, XY, 0, 0, tiled=True)

    raw_grad, token_weights, ffn_sum = fence(raw_grad, proj_full, ffn_sum)
    forget_arg = raw[:, OWN + 3 * HD : OWN + 3 * HD + OWN_HEADS] + bias_mine
    log_forget_grad = jnp.einsum(
        "bhu,ut->bth",
        forget_sums[:, :OWN_HEADS],
        later,
        **exact,
    ).reshape(GROUP * SEQ, OWN_HEADS)
    forget_arg_grad = log_forget_grad * (1.0 - lax.logistic(forget_arg))
    forget_low_grad = forget_arg_grad.astype(LOW)
    pair_back = lax.all_gather(ffn_sum[:192], ZC, axis=0, tiled=False)
    raw_grad, forget_low_grad, pair_back = fence(raw_grad, forget_low_grad, pair_back)
    token_part = dot_right_t(raw_grad, token_weights) + dot_right_t(
        forget_low_grad, forget_low
    )
    normed_group = tokens_group.astype(WIDE) * inverse_group
    gain_one_grad = jnp.sum(normed_group * token_part, axis=0)
    token_part = token_part.astype(LOW).reshape(GROUP, SEQ, D)
    head_ids = lax.broadcasted_iota(jnp.int32, (OWN_HEADS, H), 0) + OWN_HEADS * place
    own_heads = head_ids == lax.broadcasted_iota(jnp.int32, (OWN_HEADS, H), 1)
    forget_wide = dot_plain(forget_low_grad, own_heads.astype(LOW)).astype(LOW)
    forget_w_grad = dot_left_t(hidden_one, forget_wide).reshape(288, SEQ)
    forget_bias_grad = jnp.sum(
        jnp.where(own_heads, jnp.sum(forget_arg_grad, axis=0)[:, None], 0.0), axis=0
    )
    out_part, ffn_sum = fence(out_part, ffn_sum)
    hidden_one_grad = lax.psum_scatter(token_part, ZC, scatter_dimension=0, tiled=False)
    pair_back = pair_back.reshape(GROUP, 2, GROUP, 12, FF_PART)
    pair_back = lax.dynamic_index_in_dim(pair_back, place, 2, keepdims=False)
    pair_back = pair_back.reshape(GROUP, 2, 12, 4, 128).transpose(3, 1, 2, 0, 4).reshape(96, 1024)
    pair_back = dot_plain(pair_back, order)
    out_sum = lax.psum_scatter(out_part, ZC, scatter_dimension=0, tiled=False)
    hidden_one_grad = hidden_one_grad.astype(WIDE)
    forget_bias_grad = jnp.pad(forget_bias_grad, (0, SEQ - H))
    small_grads = jnp.concatenate([gain_one_grad, gain_two_grad, gain_sums[0], forget_bias_grad])
    small_grads = small_grads.reshape(26, SEQ)
    terms, pair_back, small_grads, forget_w_grad = fence(
        terms, pair_back, small_grads, forget_w_grad
    )
    attn_part = jnp.sum(terms.astype(WIDE), axis=0)
    attn_part = jnp.pad(attn_part, ((0, 0), (0, HD))).reshape(GROUP, 12, RAW)
    attn_part = lax.all_to_all(attn_part, ZC, 0, 0, tiled=True)
    *measured, flat = measure(
        weight_sums, attn_part, pair_back, ffn_sum, *old_rows, small_grads, forget_w_grad
    )
    grads, rows_new = measured[:3], measured[3:]
    flat = spread_back(spread_sum(flat))
    input_grad = mixed_grad + norm_back(normed_one, inverse_one, hidden_one_grad * gain_one)
    block_out = (mixed_sum + out_sum.astype(WIDE)).astype(LOW)
    fresh = finish(
        flat,
        grads,
        (attn_weights, ffn_weights, down_weight),
        rows_new,
        old_cols,
        param_rows,
        moment_rows,
    )
    attn_new, ffn_new, down_new, attn_copy, ffn_copy, down_copy = fresh[:6]
    attn_cols_new, ffn_cols_new, down_cols_new, small_new, moments_new = fresh[6:]
    return (
        block_out,
        input_grad,
        grads[0],
        attn_new,
        attn_copy,
        rows_new[0].reshape(5, 12),
        attn_cols_new.reshape(5, D),
        grads[1],
        ffn_new,
        ffn_copy,
        rows_new[1].reshape(2, 12),
        ffn_cols_new.reshape(2, FF),
        grads[2],
        down_new,
        down_copy,
        rows_new[2].reshape(32),
        down_cols_new.reshape(D),
        small_vector(flat[FLAT_SMALL : FLAT_SMALL + 314]),
        small_vector(small_new),
        small_vector(moments_new),
    )


def solution(mesh):
    chips = Mesh(mesh.devices.reshape(4, 4, 4, 2), ALL)
    rows_first = P(ALL, None)
    rows_second = P(None, ALL, None)
    stat_rows = P(None, ALL)
    flat = P(ALL)
    whole = P()
    return jax.shard_map(
        shards,
        mesh=chips,
        in_specs=(
            rows_first,
            rows_first,
            flat,
            rows_second,
            stat_rows,
            whole,
            rows_second,
            stat_rows,
            whole,
            rows_first,
            flat,
            whole,
            whole,
            whole,
        ),
        out_specs=(
            rows_first,
            rows_first,
            rows_second,
            rows_second,
            rows_second,
            stat_rows,
            whole,
            rows_second,
            rows_second,
            rows_second,
            stat_rows,
            whole,
            rows_first,
            rows_first,
            rows_first,
            flat,
            whole,
            whole,
            whole,
            whole,
        ),
        check_vma=False,
    )
```

```python
import jax
import jax.numpy as jnp
from jax import lax
from jax.experimental import pallas as pl
from jax.experimental.pallas import tpu as pltpu
from jax.sharding import Mesh
from jax.sharding import PartitionSpec as P

D = 1536
H = 24
HD = 64
FF = 4096
SEQ = 128
HALF = D // 2
HEADS = H // 2
GROUP = 8
PLANE = 16
CHIPS = 64
DEVICES = 128
FF_PART = FF // GROUP
OWN_HEADS = H // GROUP
FLAT_ROWS = 640
FLAT_ROW_SUMS = 120
FLAT_SMALL = 280
FLAT_FORGET = 306
FLAT_WEIGHTS = 594
FLAT_END = 602
OWN = 4 * OWN_HEADS * HD
RAW = OWN + 2 * SEQ
WIDE_HEADS = OWN_HEADS * 2 * HD

BETA = 0.5
CLIP = 0.1
RATE = 3.0
EPS_NORM = 1e-06
EPS_STAT = 1e-30
NEG_FILL = -1e30
LOW = jnp.bfloat16
WIDE = jnp.float32

ALL = ("x", "y", "z", "c")
XYZ = ("x", "y", "z")
XY = ("x", "y")
ZC = ("z", "c")


def dot_plain(left_side, right_side):
    return jnp.dot(left_side, right_side, preferred_element_type=WIDE)


def dot_right_t(left_side, right_side):
    return lax.dot_general(
        left_side, right_side, (((1,), (1,)), ((), ())), preferred_element_type=WIDE
    )


def dot_left_t(left_side, right_side):
    return lax.dot_general(
        left_side, right_side, (((0,), (0,)), ((), ())), preferred_element_type=WIDE
    )


def inverse_rms(values):
    return lax.rsqrt(jnp.mean(values * values, axis=-1, keepdims=True) + EPS_NORM)


def norm_back(normed, inverse, grad_out):
    return inverse * (grad_out - normed * jnp.mean(grad_out * normed, axis=-1, keepdims=True))


def split_small(vector):
    widths = [D, D, HD, HD, H]
    pieces = []
    offset = 0
    for piece_width in widths:
        pieces.append(vector[offset : offset + piece_width])
        offset = offset + piece_width
    pieces.append(vector[offset:].reshape(D, H))
    return pieces


SMALL_WIDTHS = (D, D, HD, HD, H, D * H)


def square_sum(weight):
    return jnp.sum(weight * weight, axis=(1, 2))


def fence(*values):
    return lax.optimization_barrier(values)


def swap_core(value):
    return lax.ppermute(value, "c", [(0, 1), (1, 0)])


def reduce_core(part, core):
    keep = lax.dynamic_index_in_dim(part, core, 0, keepdims=False)
    send = lax.dynamic_index_in_dim(part, 1 - core, 0, keepdims=False)
    return keep + swap_core(send)


def hop(value, axis, step):
    return lax.ppermute(value, axis, [(i, (i + step) % 4) for i in range(4)])


def assemble_kernel(
    place_ref, own, near, far_one, far_two, other, near_other, far_other, whole_ref
):
    deep = place_ref[0]
    core = place_ref[1]
    rows = own.shape[0]
    half = rows // 2

    def put(step, side, start, value):
        at = lax.rem(deep + step, 4)
        whole_ref[at, side, start : start + value.shape[0], :] = value

    put(0, core, 0, own[...])
    put(0, 1 - core, 0, other[...])
    put(3, core, 0, near[:rows])
    put(1, core, 0, near[rows:])
    put(3, 1 - core, 0, near_other[:rows])
    put(1, 1 - core, 0, near_other[rows:])
    put(2, core, 0, far_one[...])
    put(2, core, half, far_two[...])
    put(2, 1 - core, 0, far_other[...])


def assemble(*pieces):
    place = jnp.stack([lax.axis_index("z"), lax.axis_index("c")]).astype(jnp.int32)
    rows, columns = pieces[0].shape
    whole = pl.pallas_call(
        assemble_kernel,
        in_specs=[pl.BlockSpec(memory_space=pltpu.SMEM)]
        + [pl.BlockSpec(memory_space=pltpu.VMEM)] * len(pieces),
        out_shape=jax.ShapeDtypeStruct((4, 2, rows, columns), pieces[0].dtype),
        compiler_params=pltpu.CompilerParams(vmem_limit_bytes=40 * 1024 * 1024),
        name="assemble",
    )(place, *pieces)
    return whole.reshape(GROUP * rows, columns)


def gather_group(value, *others):
    rows = value.shape[0] // 2
    before = hop(value, "z", 1)
    after = hop(value, "z", -1)
    other = swap_core(value)
    before, after, other = fence(before, after, other)
    near = jnp.concatenate([before, after])
    far_one = hop(before[:rows], "z", 1)
    far_two = hop(after[rows:], "z", -1)
    near_other = swap_core(near)
    far_one, far_two, near_other, *others = fence(far_one, far_two, near_other, *others)
    far_other = swap_core(jnp.concatenate([far_one, far_two]))
    whole = assemble(value, near, far_one, far_two, other, near_other, far_other)
    return (whole, *others)


def far_halves(part):
    rows = SEQ // 2
    far = part[3].astype(LOW)
    return (hop(far[:rows], "z", 1), hop(far[rows:], "z", -1))


def near_blocks(part, halves):
    rows = SEQ // 2
    to_after = jnp.concatenate([part[2][:rows] + halves[0].astype(WIDE), part[2][rows:]])
    to_before = jnp.concatenate([part[1][:rows], part[1][rows:] + halves[1].astype(WIDE)])
    return (hop(to_after.astype(LOW), "z", 1), hop(to_before.astype(LOW), "z", -1))


def group_reduce_start(part, core, deep):
    got = swap_core(lax.dynamic_index_in_dim(part, 1 - core, 1, keepdims=False))
    part = lax.dynamic_index_in_dim(part, core, 1, keepdims=False)
    part = part.astype(WIDE) + got.astype(WIDE)
    return [
        lax.dynamic_index_in_dim(part, (deep + step) % 4, 0, keepdims=False)
        for step in (0, 3, 1, 2)
    ]


def direct_sum(blocks, axis, dim):
    here = lax.axis_index(axis)
    total = lax.dynamic_index_in_dim(blocks, here, dim, keepdims=False).astype(WIDE)
    for step in (1, 2, 3):
        block = lax.dynamic_index_in_dim(blocks, (here + step) % 4, dim, keepdims=False)
        total = total + hop(block, axis, step).astype(WIDE)
    return total


def split_far(blocks, axis):
    far = lax.dynamic_index_in_dim(blocks, (lax.axis_index(axis) + 2) % 4, 0, keepdims=False)
    half = far.shape[0] // 2
    return (hop(far[:half], axis, 1), hop(far[half:], axis, -1))


def split_near(blocks, axis, halves):
    here = lax.axis_index(axis)
    after = lax.dynamic_index_in_dim(blocks, (here + 1) % 4, 0, keepdims=False)
    before = lax.dynamic_index_in_dim(blocks, (here + 3) % 4, 0, keepdims=False)
    half = after.shape[0] // 2
    to_after = jnp.concatenate([after[:half] + halves[0], after[half:]])
    to_before = jnp.concatenate([before[:half], before[half:] + halves[1]])
    return (hop(to_after, axis, 1), hop(to_before, axis, -1))


def split_sum(blocks, axis, near):
    own = lax.dynamic_index_in_dim(blocks, lax.axis_index(axis), 0, keepdims=False)
    return (own.astype(WIDE) + near[0].astype(WIDE) + near[1].astype(WIDE)).astype(LOW)


def direct_exchange(blocks, axis):
    here = lax.axis_index(axis)
    pieces = [lax.dynamic_index_in_dim(blocks, here, 0, keepdims=False)]
    for step in (1, 2, 3):
        block = lax.dynamic_index_in_dim(blocks, (here + step) % 4, 0, keepdims=False)
        pieces.append(hop(block, axis, step))
    return pieces


def head_stat(values, lane_low):
    low = jnp.sum(jnp.where(lane_low, values, 0.0), axis=-1, keepdims=True) * (1.0 / HD)
    high = jnp.sum(jnp.where(lane_low, 0.0, values), axis=-1, keepdims=True) * (1.0 / HD)
    return jnp.where(lane_low, low, high)


def head_normed(values, lane_low):
    inverse = lax.rsqrt(head_stat(values * values, lane_low) + EPS_NORM)
    return (values * inverse, inverse)


def far(value):
    return pltpu.with_memory_space_constraint(value, pltpu.HBM)


def attend_kernel(
    raw_ref, bias_ref, length_ref, gains_ref, gated_ref, attended_ref, prob_ref
):
    lane = lax.broadcasted_iota(jnp.int32, (SEQ, SEQ), 1)
    lane_low = lane < HD
    slot = lax.broadcasted_iota(jnp.int32, (SEQ, SEQ), 0)
    allowed = (lane <= slot) & (lane.astype(WIDE) < length_ref[0])
    forget = raw_ref[:, RAW - SEQ :] + bias_ref[0:1]
    mine = (lane >= HD) & (lane < HD + OWN_HEADS)
    log_forget = -jnp.log1p(jnp.exp(jnp.where(mine, -forget, 0.0)))
    cols = lax.dot_general(
        (lane <= slot).astype(WIDE),
        log_forget,
        (((1,), (0,)), ((), ())),
        precision=lax.Precision.HIGHEST,
        preferred_element_type=WIDE,
    )
    rows = cols.T
    for head in range(OWN_HEADS):
        at = 2 * head * SEQ
        normed, _ = head_normed(raw_ref[:, at : at + SEQ], lane_low)
        scaled = normed * gains_ref[0:1]
        query = jnp.where(lane_low, scaled, 0.0).astype(LOW)
        key = pltpu.roll(scaled, HD, 1).astype(LOW)
        value_gate = raw_ref[:, at + SEQ : at + 2 * SEQ]
        score = dot_right_t(query, key) * (HD**-0.5)
        score = score + cols[:, HD + head : HD + head + 1]
        score = score - rows[HD + head : HD + head + 1]
        score = jnp.where(allowed, score, NEG_FILL)
        weight = jnp.exp(score - jnp.max(score, axis=-1, keepdims=True))
        prob = weight / jnp.sum(weight, axis=-1, keepdims=True)
        prob_ref[0, head] = prob
        attended = dot_plain(prob.astype(LOW), value_gate.astype(LOW))
        gate = lax.logistic(pltpu.roll(value_gate, HD, 1))
        attended_ref[:, head * SEQ : (head + 1) * SEQ] = attended
        gated = jnp.where(lane_low, attended * gate, 0.0)
        gated_ref[:, head * SEQ : (head + 1) * SEQ] = gated.astype(LOW)


def attend(raw, bias, lengths, gains):
    return pl.pallas_call(
        attend_kernel,
        grid=(GROUP,),
        in_specs=[
            pl.BlockSpec((SEQ, RAW), lambda i: (i, 0)),
            pl.BlockSpec((8, SEQ), lambda i: (0, 0)),
            pl.BlockSpec((1, 1, SEQ), lambda i: (i, 0, 0)),
            pl.BlockSpec((8, SEQ), lambda i: (0, 0)),
        ],
        out_specs=[
            pl.BlockSpec((SEQ, WIDE_HEADS), lambda i: (i, 0)),
            pl.BlockSpec((SEQ, WIDE_HEADS), lambda i: (i, 0)),
            pl.BlockSpec((1, OWN_HEADS, SEQ, SEQ), lambda i: (i, 0, 0, 0)),
        ],
        out_shape=[
            jax.ShapeDtypeStruct((GROUP * SEQ, WIDE_HEADS), LOW),
            jax.ShapeDtypeStruct((GROUP * SEQ, WIDE_HEADS), WIDE),
            jax.ShapeDtypeStruct((GROUP, OWN_HEADS, SEQ, SEQ), WIDE),
        ],
        compiler_params=pltpu.CompilerParams(vmem_limit_bytes=40 * 1024 * 1024),
        cost_estimate=pl.CostEstimate(
            flops=24 * 4 * SEQ**3, bytes_accessed=6_000_000, transcendentals=24 * SEQ * SEQ
        ),
        name="attend",
    )(far(raw), bias, lengths, gains)


def attend_back_kernel(
    raw_ref, gated_grad_ref, attended_ref, prob_ref, gains_ref, grad_ref, forget_ref, gain_ref
):
    lane_low = lax.broadcasted_iota(jnp.int32, (SEQ, SEQ), 1) < HD
    ones = jnp.ones((8, SEQ), LOW)
    gains = gains_ref[0:1]
    forget_ref[...] = jnp.zeros_like(forget_ref)

    @pl.when(pl.program_id(0) == 0)
    def _():
        gain_ref[...] = jnp.zeros_like(gain_ref)

    for head in range(OWN_HEADS):
        at = 2 * head * SEQ
        normed, inverse = head_normed(raw_ref[:, at : at + SEQ], lane_low)
        swapped = pltpu.roll(normed * gains, HD, 1).astype(LOW)
        value_gate = raw_ref[:, at + SEQ : at + 2 * SEQ]
        gate = lax.logistic(pltpu.roll(value_gate, HD, 1))
        gated_grad = gated_grad_ref[:, head * SEQ : (head + 1) * SEQ]
        gated_grad = jnp.where(lane_low, gated_grad, 0.0)
        out_grad = (gated_grad * gate).astype(LOW)
        attended = attended_ref[:, head * SEQ : (head + 1) * SEQ]
        gate_grad = gated_grad * attended * gate * (1.0 - gate)
        prob = prob_ref[0, head]
        prob_grad = dot_right_t(out_grad, value_gate.astype(LOW))
        delta = jnp.sum(prob * prob_grad, axis=-1, keepdims=True)
        score_grad = (prob * (prob_grad - delta)).astype(LOW)
        value_grad = dot_left_t(prob.astype(LOW), out_grad)
        value_gate_grad = jnp.where(lane_low, value_grad, pltpu.roll(gate_grad, HD, 1))
        grad_ref[:, at + SEQ : at + 2 * SEQ] = value_gate_grad.astype(LOW)
        sums = dot_right_t(ones, score_grad) - dot_plain(ones, score_grad)
        forget_ref[0, head : head + 1] = sums[0:1]
        grad = jnp.where(
            lane_low, dot_plain(score_grad, swapped), dot_left_t(score_grad, swapped)
        ) * (HD**-0.5)
        product = grad * normed
        gain_ref[0:1] += jnp.sum(product, axis=0, keepdims=True)
        mean = head_stat(product * gains, lane_low)
        grad_ref[:, at : at + SEQ] = (inverse * (grad * gains - normed * mean)).astype(LOW)


def attend_back(raw, gated_grad, attended, prob, gains):
    return pl.pallas_call(
        attend_back_kernel,
        grid=(GROUP,),
        in_specs=[
            pl.BlockSpec((SEQ, RAW), lambda i: (i, 0)),
            pl.BlockSpec((SEQ, WIDE_HEADS), lambda i: (i, 0)),
            pl.BlockSpec((SEQ, WIDE_HEADS), lambda i: (i, 0)),
            pl.BlockSpec((1, OWN_HEADS, SEQ, SEQ), lambda i: (i, 0, 0, 0)),
            pl.BlockSpec((8, SEQ), lambda i: (0, 0)),
        ],
        out_specs=[
            pl.BlockSpec((SEQ, OWN), lambda i: (i, 0)),
            pl.BlockSpec((1, 8, SEQ), lambda i: (i, 0, 0)),
            pl.BlockSpec((8, SEQ), lambda i: (0, 0)),
        ],
        out_shape=[
            jax.ShapeDtypeStruct((GROUP * SEQ, OWN), LOW),
            jax.ShapeDtypeStruct((GROUP, 8, SEQ), WIDE),
            jax.ShapeDtypeStruct((8, SEQ), WIDE),
        ],
        compiler_params=pltpu.CompilerParams(vmem_limit_bytes=40 * 1024 * 1024),
        cost_estimate=pl.CostEstimate(
            flops=24 * 10 * SEQ**3, bytes_accessed=8_000_000, transcendentals=2 * SEQ * HALF
        ),
        name="attend_back",
    )(far(raw), far(gated_grad), far(attended), far(prob), gains)


def half_tile(ref, matrix, head):
    tile = ref[matrix, :, SEQ * (head // 2) : SEQ * (head // 2) + SEQ]
    return (tile, pltpu.roll(tile, HD, 1))[:: 1 if head % 2 == 0 else -1]


def pack_kernel(length_ref, weight_ref, forget_ref, packed_ref):
    lane = lax.broadcasted_iota(jnp.int32, (12, SEQ), 1)
    lane_low = lane < HD
    forget = forget_ref[...]
    length = jnp.where(lane == SEQ - 1, length_ref[0], 0.0)
    for place in range(GROUP):
        for slot in range(OWN_HEADS):
            head = OWN_HEADS * place + slot
            for pair in range(2):
                left, _ = half_tile(weight_ref, 2 * pair, head)
                _, right = half_tile(weight_ref, 2 * pair + 1, head)
                at = (2 * slot + pair) * SEQ
                tile = jnp.where(lane_low, left, right)
                packed_ref[place, :, at : at + SEQ] = tile.astype(LOW)
        first, _ = half_tile(weight_ref, 4, OWN_HEADS * place)
        _, second = half_tile(weight_ref, 4, OWN_HEADS * place + 1)
        third, _ = half_tile(weight_ref, 4, OWN_HEADS * place + 2)
        packed_ref[place, :, OWN : OWN + SEQ] = jnp.where(lane_low, first, second).astype(LOW)
        rest = pltpu.roll(forget, (HD - OWN_HEADS * place) % SEQ, 1)
        rest = jnp.where(lane < HD + OWN_HEADS, rest, length)
        packed_ref[place, :, OWN + SEQ :] = jnp.where(lane_low, third, rest).astype(LOW)


def pack(length, weights, forget):
    return pl.pallas_call(
        pack_kernel,
        in_specs=[
            pl.BlockSpec(memory_space=pltpu.SMEM),
            pl.BlockSpec(memory_space=pltpu.VMEM),
            pl.BlockSpec(memory_space=pltpu.VMEM),
        ],
        out_shape=jax.ShapeDtypeStruct((GROUP, 12, RAW), LOW),
        compiler_params=pltpu.CompilerParams(vmem_limit_bytes=40 * 1024 * 1024),
        name="pack",
    )(length, weights, forget)


def spread_rows_kernel(blocks_ref, rows_ref):
    for head in range(OWN_HEADS):
        at = head * SEQ
        for pair in range(GROUP // 2):
            left = blocks_ref[2 * pair, head * HD : head * HD + HD, :]
            right = blocks_ref[2 * pair + 1, head * HD : head * HD + HD, :]
            both = jnp.concatenate([left, right], axis=1)
            rows_ref[at : at + HD, 384 * pair : 384 * pair + 384] = both
        rows_ref[at + HD : at + SEQ, :] = jnp.zeros((HD, D), LOW)


def collect_rows_kernel(rows_ref, blocks_ref):
    for head in range(OWN_HEADS):
        at = head * SEQ
        for pair in range(GROUP // 2):
            both = rows_ref[at : at + HD, 384 * pair : 384 * pair + 384].astype(LOW)
            blocks_ref[2 * pair, head * HD : head * HD + HD, :] = both[:, : 3 * HD]
            blocks_ref[2 * pair + 1, head * HD : head * HD + HD, :] = both[:, 3 * HD :]


def move_rows(kernel, value, shape):
    return pl.pallas_call(
        kernel,
        out_shape=jax.ShapeDtypeStruct(shape, LOW),
        compiler_params=pltpu.CompilerParams(vmem_limit_bytes=40 * 1024 * 1024),
        name="move_rows",
    )(value)


def unpack_kernel(packed_ref, grad_ref):
    lane_low = lax.broadcasted_iota(jnp.int32, (12, SEQ), 1) < HD

    def tile_of(place, at):
        tile = packed_ref[place, :, at : at + SEQ]
        return (tile, pltpu.roll(tile, HD, 1))

    for left in range(0, H, 2):
        places = [(head // OWN_HEADS, head % OWN_HEADS) for head in (left, left + 1)]
        at = SEQ * (left // 2)
        for pair in range(2):
            tiles = [tile_of(place, (2 * slot + pair) * SEQ) for place, slot in places]
            grad_ref[2 * pair, :, at : at + SEQ] = jnp.where(lane_low, tiles[0][0], tiles[1][1])
            grad_ref[2 * pair + 1, :, at : at + SEQ] = jnp.where(lane_low, tiles[0][1], tiles[1][0])
        picked = []
        for side, (place, slot) in enumerate(places):
            tile = tile_of(place, OWN + SEQ * (slot // 2))
            picked.append(tile[(slot % 2) ^ side])
        grad_ref[4, :, at : at + SEQ] = jnp.where(lane_low, picked[0], picked[1])


def tiles_of(columns):
    return [(tile, tile * SEQ) for tile in range(columns // SEQ)]


def row_stats(grad_ref, rows_old, columns):
    total = jnp.zeros((grad_ref.shape[0], SEQ), WIDE)
    for _, at in tiles_of(columns):
        part = grad_ref[:, at : at + SEQ]
        total = total + part * part
    mean = jnp.sum(total, axis=1, keepdims=True) * (1.0 / columns)
    return BETA * rows_old + (1.0 - BETA) * (mean + EPS_STAT)


def column_stats(grad_ref, rows_new, columns, flat_ref, plain_at, scaled_at):
    for tile, at in tiles_of(columns):
        part = grad_ref[:, at : at + SEQ]
        part = part * part
        plain = jnp.sum(part, axis=0, keepdims=True)
        scaled = jnp.sum(part / rows_new, axis=0, keepdims=True)
        flat_ref[plain_at + tile : plain_at + tile + 1] = plain
        flat_ref[scaled_at + tile : scaled_at + tile + 1] = scaled


def measure_kernel(
    sums_ref,
    packed_ref,
    pair_ref,
    ffn_ref,
    attn_rows_ref,
    ffn_rows_ref,
    down_rows_ref,
    small_ref,
    forget_ref,
    attn_grad_ref,
    ffn_grad_ref,
    down_grad_ref,
    attn_rows_new_ref,
    ffn_rows_new_ref,
    down_rows_new_ref,
    flat_ref,
):
    unpack_kernel(packed_ref, attn_grad_ref)
    for block in range(4):
        for matrix in range(2):
            row = 24 * block + 12 * matrix
            ffn_grad_ref[matrix, :, 1024 * block : 1024 * block + 1024] = pair_ref[row : row + 12]
    for part in range(3):
        rows = ffn_ref[192 + 32 * part : 224 + 32 * part]
        down_grad_ref[:, 512 * part : 512 * part + 512] = rows.astype(WIDE)
    flat_ref[FLAT_END:] = jnp.zeros((FLAT_ROWS - FLAT_END, SEQ), WIDE)
    for matrix in range(8):
        value = jnp.full((1, SEQ), sums_ref[matrix], WIDE)
        flat_ref[FLAT_WEIGHTS + matrix : FLAT_WEIGHTS + matrix + 1] = value
    flat_ref[FLAT_SMALL : FLAT_SMALL + 26] = small_ref[...]
    flat_ref[FLAT_FORGET : FLAT_FORGET + 288] = forget_ref[...]
    groups = (
        (attn_grad_ref, attn_rows_ref, attn_rows_new_ref, 5, D, 0, 60, 0),
        (ffn_grad_ref, ffn_rows_ref, ffn_rows_new_ref, 2, FF, 128, 192, 5),
        (down_grad_ref, down_rows_ref, down_rows_new_ref, 1, D, 256, 268, 7),
    )
    for grad_ref, old_ref, new_ref, count, columns, plain_at, scaled_at, first in groups:
        for matrix in range(count):
            mine = grad_ref if first == 7 else grad_ref.at[matrix]
            rows_new = row_stats(mine, old_ref[matrix], columns)
            new_ref[matrix] = rows_new
            at = matrix * (columns // SEQ)
            column_stats(mine, rows_new, columns, flat_ref, plain_at + at, scaled_at + at)
            value = jnp.broadcast_to(jnp.sum(rows_new, axis=0, keepdims=True), (1, SEQ))
            flat_ref[FLAT_ROW_SUMS + first + matrix : FLAT_ROW_SUMS + first + matrix + 1] = value


def measure(sums, packed, pair, ffn, attn_rows, ffn_rows, down_rows, small, forget):
    return pl.pallas_call(
        measure_kernel,
        in_specs=[pl.BlockSpec(memory_space=pltpu.SMEM)]
        + [pl.BlockSpec(memory_space=pltpu.VMEM)] * 8,
        out_shape=[
            jax.ShapeDtypeStruct((5, 12, D), WIDE),
            jax.ShapeDtypeStruct((2, 12, FF), WIDE),
            jax.ShapeDtypeStruct((32, D), WIDE),
            jax.ShapeDtypeStruct((5, 12, 1), WIDE),
            jax.ShapeDtypeStruct((2, 12, 1), WIDE),
            jax.ShapeDtypeStruct((1, 32, 1), WIDE),
            jax.ShapeDtypeStruct((FLAT_ROWS, SEQ), WIDE),
        ],
        compiler_params=pltpu.CompilerParams(vmem_limit_bytes=40 * 1024 * 1024),
        name="measure",
    )(sums, packed, pair, ffn, attn_rows, ffn_rows, down_rows, small, forget)


def square_total(values):
    return jnp.sum(jnp.sum(values * values, axis=0, keepdims=True), axis=1, keepdims=True)


def finish_kernel(
    flat_ref,
    attn_grad_ref,
    ffn_grad_ref,
    down_grad_ref,
    attn_ref,
    ffn_ref,
    down_ref,
    attn_rows_ref,
    ffn_rows_ref,
    down_rows_ref,
    attn_cols_ref,
    ffn_cols_ref,
    down_cols_ref,
    small_ref,
    moments_ref,
    attn_new_ref,
    ffn_new_ref,
    down_new_ref,
    attn_copy_ref,
    ffn_copy_ref,
    down_copy_ref,
    attn_cols_new_ref,
    ffn_cols_new_ref,
    down_cols_new_ref,
    small_new_ref,
    moments_new_ref,
    *scratch,
):
    *held, arrivals = scratch
    sources = (
        (attn_grad_ref, ffn_grad_ref, down_grad_ref, attn_ref, ffn_ref, down_ref)
        + (attn_rows_ref, ffn_rows_ref, down_rows_ref, small_ref, moments_ref)
    )
    copies = [
        pltpu.make_async_copy(source, target, arrivals.at[place])
        for place, (source, target) in enumerate(zip(sources, held))
    ]
    for copy in copies:
        copy.start()
    for copy in copies:
        copy.wait()
    attn_grad_ref, ffn_grad_ref, down_grad_ref, attn_ref, ffn_ref, down_ref = held[:6]
    attn_rows_ref, ffn_rows_ref, down_rows_ref, small_ref, moments_ref = held[6:]
    groups = (
        (attn_grad_ref, attn_ref, attn_rows_ref, attn_cols_ref)
        + (attn_new_ref, attn_copy_ref, attn_cols_new_ref, 5, D, D, 0, 60, 0),
        (ffn_grad_ref, ffn_ref, ffn_rows_ref, ffn_cols_ref)
        + (ffn_new_ref, ffn_copy_ref, ffn_cols_new_ref, 2, D, FF, 128, 192, 5),
        (down_grad_ref, down_ref, down_rows_ref, down_cols_ref)
        + (down_new_ref, down_copy_ref, down_cols_new_ref, 1, FF, D, 256, 268, 7),
    )
    for (
        grad_ref,
        old_ref,
        rows_ref,
        cols_ref,
        new_ref,
        copy_ref,
        cols_new_ref,
        count,
        all_rows,
        columns,
        plain_at,
        scaled_at,
        first,
    ) in groups:
        entries = all_rows * columns
        tiles = columns // SEQ
        for matrix in range(count):
            whole = first == 7
            grad = grad_ref if whole else grad_ref.at[matrix]
            old = old_ref if whole else old_ref.at[matrix]
            new = new_ref if whole else new_ref.at[matrix]
            copy = copy_ref if whole else copy_ref.at[matrix]
            at = matrix * tiles
            fresh_cols = []
            total = jnp.zeros((1, SEQ), WIDE)
            for tile, place in tiles_of(columns):
                row = plain_at + at + tile
                plain = flat_ref[row : row + 1] * (1.0 / all_rows) + EPS_STAT
                held = cols_ref[matrix : matrix + 1, place : place + SEQ]
                piece = BETA * held + (1.0 - BETA) * plain
                cols_new_ref[matrix : matrix + 1, place : place + SEQ] = piece
                row = scaled_at + at + tile
                total = total + flat_ref[row : row + 1] / piece
                fresh_cols.append(piece)
            row = FLAT_ROW_SUMS + first + matrix
            row_mean = flat_ref[row : row + 1] * (1.0 / all_rows)
            row = FLAT_WEIGHTS + first + matrix
            spread = jnp.sqrt(flat_ref[row : row + 1] * (1.0 / entries) + EPS_NORM)
            total = jnp.sum(total, axis=1, keepdims=True)
            mean_square = row_mean * total * (1.0 / entries)
            factor = RATE * spread / jnp.maximum(1.0, jnp.sqrt(mean_square) / CLIP)
            rows_scale = lax.rsqrt(rows_ref[matrix])
            for tile, place in tiles_of(columns):
                cols_scale = lax.rsqrt(fresh_cols[tile] / row_mean) * factor
                step = grad[:, place : place + SEQ] * rows_scale * cols_scale
                value = old[:, place : place + SEQ] - step
                new[:, place : place + SEQ] = value
                copy[:, place : place + SEQ] = value.astype(LOW)

    lane_low = lax.broadcasted_iota(jnp.int32, (1, SEQ), 1) < HD
    for start, rows, width, lanes in (
        (0, 12, D, None),
        (12, 12, D, None),
        (24, 1, HD, lane_low),
        (24, 1, HD, jnp.logical_not(lane_low)),
        (25, 1, H, None),
        (26, 288, D * H, None),
    ):
        param = small_ref[start : start + rows]
        grad = flat_ref[FLAT_SMALL + start : FLAT_SMALL + start + rows]
        fresh = BETA * moments_ref[start : start + rows] + (1.0 - BETA) * (grad * grad + EPS_STAT)
        update = grad * lax.rsqrt(fresh)
        if lanes is not None:
            update = jnp.where(lanes, update, 0.0)
        inside = param if lanes is None else jnp.where(lanes, param, 0.0)
        clip_ratio = jnp.sqrt(square_total(update) * (1.0 / width)) / CLIP
        spread = jnp.sqrt(square_total(inside) * (1.0 / width) + EPS_NORM)
        value = param - RATE * spread * (update / jnp.maximum(1.0, clip_ratio))
        if lanes is None:
            small_new_ref[start : start + rows] = value
        elif width == HD:
            held = small_new_ref[start : start + rows]
            small_new_ref[start : start + rows] = jnp.where(lanes, value, held)
        moments_new_ref[start : start + rows] = fresh


def finish(flat, grads, weights, rows, cols, small, moments):
    return pl.pallas_call(
        finish_kernel,
        in_specs=[pl.BlockSpec(memory_space=pltpu.VMEM)]
        + [pl.BlockSpec(memory_space=pltpu.HBM)] * 9
        + [pl.BlockSpec(memory_space=pltpu.VMEM)] * 3
        + [pl.BlockSpec(memory_space=pltpu.HBM)] * 2,
        scratch_shapes=[
            pltpu.VMEM(value.shape, WIDE)
            for value in (*grads, *weights, *rows, small, moments)
        ]
        + [pltpu.SemaphoreType.DMA((11,))],
        out_shape=[
            jax.ShapeDtypeStruct((5, 12, D), WIDE),
            jax.ShapeDtypeStruct((2, 12, FF), WIDE),
            jax.ShapeDtypeStruct((32, D), WIDE),
            jax.ShapeDtypeStruct((5, 12, D), LOW),
            jax.ShapeDtypeStruct((2, 12, FF), LOW),
            jax.ShapeDtypeStruct((32, D), LOW),
            jax.ShapeDtypeStruct((5, D), WIDE),
            jax.ShapeDtypeStruct((2, FF), WIDE),
            jax.ShapeDtypeStruct((1, D), WIDE),
            jax.ShapeDtypeStruct((314, SEQ), WIDE),
            jax.ShapeDtypeStruct((314, SEQ), WIDE),
        ],
        compiler_params=pltpu.CompilerParams(vmem_limit_bytes=40 * 1024 * 1024),
        name="finish",
    )(
        flat,
        *[far(value) for value in (*grads, *weights, *rows)],
        *cols,
        far(small),
        far(moments),
    )


def small_rows(vector, fill):
    bias = vector[2 * D + 2 * HD : 2 * D + 2 * HD + H]
    bias = jnp.concatenate([bias, jnp.full((SEQ - H,), fill, WIDE)])
    return jnp.concatenate(
        [
            vector[: 2 * D].reshape(24, SEQ),
            vector[2 * D : 2 * D + 2 * HD].reshape(1, SEQ),
            bias.reshape(1, SEQ),
            vector[2 * D + 2 * HD + H :].reshape(288, SEQ),
        ]
    )


def small_vector(rows):
    return jnp.concatenate(
        [rows[:25].reshape(-1), rows[25, :H], rows[26:].reshape(-1)]
    )


def spread_sum(flat):
    pieces = flat.reshape(DEVICES, -1, SEQ)
    return jnp.sum(lax.all_to_all(pieces, ALL, 0, 0, tiled=True), axis=0)


def spread_back(mine):
    whole = jnp.broadcast_to(mine[None], (DEVICES, *mine.shape))
    return lax.all_to_all(whole, ALL, 0, 0, tiled=True).reshape(-1, SEQ)


def column_order():
    source = lax.broadcasted_iota(jnp.int32, (1024, 1024), 0)
    target = lax.broadcasted_iota(jnp.int32, (1024, 1024), 1)
    lane = source % 128
    return (target == (lane // 32) * 256 + (source // 128) * 32 + lane % 32).astype(LOW)


def shards(
    tokens,
    cotangent,
    lengths,
    attn_weights,
    attn_rows,
    attn_cols,
    ffn_weights,
    ffn_rows,
    ffn_cols,
    down_weight,
    down_rows,
    down_cols,
    small_params,
    small_moments,
):
    core = lax.axis_index("c")
    deep = lax.axis_index("z")
    inputs = tokens.astype(WIDE)
    slot_ids = jnp.arange(SEQ, dtype=jnp.int32)
    valid_rows = slot_ids < lengths[0]
    gain_one, gain_two, query_gain, key_gain, forget_bias, forget_weight = split_small(small_params)

    device = ((lax.axis_index("x") * 4 + lax.axis_index("y")) * 4 + deep) * 2 + core
    forget_rows = lax.dynamic_slice_in_dim(forget_weight, device * 12, 12, axis=0)
    forget_rows = jnp.pad(forget_rows, ((0, 0), (0, SEQ - H)))
    attn_low = pack(lengths.astype(WIDE), attn_weights, forget_rows)
    attn_low = lax.all_to_all(attn_low, ZC, 0, 0, tiled=True)
    lengths_group = attn_low[:, 0, RAW - 1].astype(WIDE)
    attn_low = attn_low.reshape(96, RAW)
    attn_full = lax.all_gather(attn_low, XY, axis=0, tiled=True)
    order = column_order()
    pair_low = ffn_weights.astype(LOW).reshape(24, 4, 1024).transpose(1, 0, 2).reshape(96, 1024)
    pair_low = dot_right_t(pair_low, order).astype(LOW).reshape(4, 2, 12, GROUP, 128)
    pair_low = pair_low.transpose(3, 2, 1, 0, 4).reshape(GROUP, 12, 2 * FF_PART)
    pair_low = lax.all_to_all(pair_low, ZC, 0, 0, tiled=True).reshape(96, 2 * FF_PART)
    down_low = jnp.concatenate(
        [down_weight[:, at : at + 512].astype(LOW) for at in (0, 512, 1024)], axis=0
    )
    seed_grad = cotangent.astype(WIDE) * valid_rows[:, None].astype(WIDE)
    seed_grad, pair_low, down_low = fence(seed_grad, pair_low, down_low)
    seed_low = lax.all_gather(seed_grad.astype(LOW), ZC, axis=0, tiled=True)
    ffn_full = lax.all_gather(
        jnp.concatenate([pair_low, down_low], axis=1), XY, axis=0, tiled=True
    )

    inverse_one = inverse_rms(inputs)
    normed_one = inputs * inverse_one
    attn_low, attn_weights, ffn_weights, down_weight, small_params = fence(
        attn_low, attn_weights, ffn_weights, down_weight, small_params
    )
    tokens_group = gather_group(tokens)[0]
    inputs_group = tokens_group.astype(WIDE)
    inverse_group = inverse_rms(inputs_group)
    hidden_one = (inputs_group * inverse_group * gain_one).astype(LOW)
    place = 2 * deep + core

    lengths_group = jnp.broadcast_to(lengths_group[:, None, None], (GROUP, 1, SEQ))
    forget_low = lax.dynamic_slice_in_dim(forget_weight, place * OWN_HEADS, OWN_HEADS, axis=1)
    forget_low = forget_low.astype(LOW)
    bias_mine = lax.dynamic_slice_in_dim(forget_bias, place * OWN_HEADS, OWN_HEADS, axis=0)
    bias_tile = jnp.pad(bias_mine[None], ((0, 7), (HD, HD - OWN_HEADS)))
    exact = {"precision": lax.Precision.HIGHEST, "preferred_element_type": WIDE}
    slots = lax.broadcasted_iota(jnp.int32, (SEQ, SEQ), 0)
    later = (slots >= lax.broadcasted_iota(jnp.int32, (SEQ, SEQ), 1)).astype(WIDE)
    gains = jnp.concatenate([query_gain, key_gain])[None]
    gains = jnp.pad(gains, ((0, 7), (0, 0)))
    (
        attn_full,
        hidden_one,
        tokens_group,
        inverse_group,
        lengths_group,
        forget_low,
        bias_tile,
        gains,
        order,
    ) = fence(
        attn_full,
        hidden_one,
        tokens_group,
        inverse_group,
        lengths_group,
        forget_low,
        bias_tile,
        gains,
        order,
    )
    proj_full = attn_full[:, :OWN]
    raw, attn_full = fence(dot_plain(hidden_one, attn_full), attn_full)
    out_rows = attn_full[:, OWN : OWN + 3 * HD].reshape(GROUP, 3 * HD, 3 * HD)
    out_rows = lax.all_to_all(out_rows, ZC, 0, 0, tiled=True)
    gated_out, attended, prob = attend(raw, bias_tile, lengths_group, gains)
    out_rows = move_rows(spread_rows_kernel, out_rows, (WIDE_HEADS, D))
    mixed_part = dot_plain(gated_out, out_rows).astype(LOW).reshape(4, 2, SEQ, D)
    mixed_part = group_reduce_start(mixed_part, core, deep)
    half_one, half_two = fence(*far_halves(mixed_part))
    near_one, near_two, *held = fence(
        *near_blocks(mixed_part, (half_one, half_two)),
        small_params,
        small_moments,
        attn_weights,
        ffn_weights,
        down_weight,
        attn_rows,
        ffn_rows,
        down_rows,
    )
    small_params, small_moments, attn_weights, ffn_weights, down_weight = held[:5]
    attn_rows, ffn_rows, down_rows = held[5:]
    param_rows = small_rows(small_params, 0.0)
    moment_rows = small_rows(small_moments, 1.0)
    old_rows = (attn_rows[:, :, None], ffn_rows[:, :, None], down_rows[None, :, None])
    old_cols = (attn_cols, ffn_cols, down_cols[None])
    weight_sums = jnp.concatenate(
        [square_sum(attn_weights), square_sum(ffn_weights), square_sum(down_weight[None])]
    )
    mixed_sum = inputs + mixed_part[0] + near_one.astype(WIDE) + near_two.astype(WIDE)
    inverse_two = inverse_rms(mixed_sum)
    normed_two = mixed_sum * inverse_two
    hidden_two, ffn_full, seed_low, param_rows, moment_rows, old_rows, weight_sums = gather_group(
        (normed_two * gain_two).astype(LOW),
        ffn_full,
        seed_low,
        param_rows,
        moment_rows,
        old_rows,
        weight_sums,
    )
    pair_full = ffn_full[:, : 2 * FF_PART]
    down_full = ffn_full[:, 2 * FF_PART :].reshape(PLANE, 3, 32, 512)
    down_full = jnp.concatenate(
        [down_full[:, part].reshape(FF_PART, 512) for part in range(3)], axis=1
    )

    gate_full = pair_full[:, :FF_PART]
    up_full = pair_full[:, FF_PART:]
    gate_part = dot_plain(hidden_two, gate_full)
    up_part = dot_plain(hidden_two, up_full)
    gate_sig = lax.logistic(gate_part)
    activated = (gate_part * gate_sig * up_part).astype(LOW)
    activated_grad = dot_right_t(seed_low, down_full)
    silu_grad = activated_grad * up_part
    gate_part_grad = silu_grad * gate_sig + silu_grad * gate_part * gate_sig * (1.0 - gate_sig)
    gate_part_grad = gate_part_grad.astype(LOW)
    up_part_grad = (activated_grad * (gate_part * gate_sig)).astype(LOW)
    token_part = dot_right_t(gate_part_grad, gate_full) + dot_right_t(up_part_grad, up_full)
    token_part = token_part.astype(LOW).reshape(4, 2, SEQ, D)
    token_part, hidden_two, gate_part_grad, up_part_grad, activated, seed_low, down_full = fence(
        token_part, hidden_two, gate_part_grad, up_part_grad, activated, seed_low, down_full
    )
    token_got, gate_terms, hidden_two, up_part_grad, activated, seed_low = fence(
        swap_core(lax.dynamic_index_in_dim(token_part, 1 - core, 1, keepdims=False)),
        dot_left_t(hidden_two, gate_part_grad).astype(LOW),
        hidden_two,
        up_part_grad,
        activated,
        seed_low,
    )
    token_part = lax.dynamic_index_in_dim(token_part, core, 1, keepdims=False)
    token_part = token_part.astype(WIDE) + token_got.astype(WIDE)
    token_part, hidden_two, up_part_grad = fence(token_part, hidden_two, up_part_grad)
    token_part = [
        lax.dynamic_index_in_dim(token_part, (deep + step) % 4, 0, keepdims=False)
        for step in (0, 3, 1, 2)
    ]
    half_one, half_two, up_terms, down_terms, activated = fence(
        *far_halves(token_part),
        dot_left_t(hidden_two, up_part_grad).astype(LOW),
        dot_left_t(activated, seed_low).astype(LOW),
        activated,
    )
    down_terms = down_terms.reshape(PLANE, 32, D)
    ffn_terms = jnp.concatenate(
        [
            gate_terms.reshape(PLANE, 96, FF_PART),
            up_terms.reshape(PLANE, 96, FF_PART),
            down_terms[:, :, :512],
            down_terms[:, :, 512:1024],
            down_terms[:, :, 1024:],
        ],
        axis=1,
    )
    out_part = dot_plain(activated, down_full).astype(LOW).reshape(GROUP, SEQ, D)
    near_one, near_two, ffn_terms, out_part = fence(
        *near_blocks(token_part, (half_one, half_two)), ffn_terms, out_part
    )
    ffn_sum = fence(lax.psum_scatter(ffn_terms, XY, scatter_dimension=0, tiled=False))[0]
    hidden_two_grad = token_part[0] + near_one.astype(WIDE) + near_two.astype(WIDE)

    gain_two_grad = jnp.sum(normed_two * hidden_two_grad, axis=0)
    mixed_grad = seed_grad + norm_back(normed_two, inverse_two, hidden_two_grad * gain_two)
    mixed_low, out_part = gather_group(mixed_grad.astype(LOW), out_part)
    gated_grad = dot_right_t(mixed_low, out_rows)
    out_terms = dot_left_t(gated_out, mixed_low)
    out_terms = move_rows(collect_rows_kernel, out_terms, (GROUP, 3 * HD, 3 * HD))
    gated_grad, out_terms = fence(gated_grad, out_terms)
    out_terms = lax.all_to_all(out_terms, ZC, 0, 0, tiled=True)
    raw_grad, forget_sums, gain_sums = attend_back(raw, gated_grad, attended, prob, gains)
    out_terms, raw_grad, forget_sums, gain_sums = fence(
        out_terms, raw_grad, forget_sums, gain_sums
    )
    terms = jnp.concatenate(
        [
            dot_left_t(hidden_one, raw_grad).astype(LOW).reshape(PLANE, 96, OWN),
            out_terms.reshape(PLANE, 96, 3 * HD),
        ],
        axis=2,
    )
    terms, raw_grad = fence(terms, raw_grad)
    terms = lax.all_to_all(terms, XY, 0, 0, tiled=True)

    raw_grad, token_weights, ffn_sum = fence(raw_grad, proj_full, ffn_sum)
    forget_arg = raw[:, OWN + 3 * HD : OWN + 3 * HD + OWN_HEADS] + bias_mine
    log_forget_grad = jnp.einsum(
        "bhu,ut->bth",
        forget_sums[:, :OWN_HEADS],
        later,
        **exact,
    ).reshape(GROUP * SEQ, OWN_HEADS)
    forget_arg_grad = log_forget_grad * (1.0 - lax.logistic(forget_arg))
    forget_low_grad = forget_arg_grad.astype(LOW)
    pair_back = lax.all_gather(ffn_sum[:192], ZC, axis=0, tiled=False)
    raw_grad, forget_low_grad, pair_back = fence(raw_grad, forget_low_grad, pair_back)
    token_part = dot_right_t(raw_grad, token_weights) + dot_right_t(
        forget_low_grad, forget_low
    )
    normed_group = tokens_group.astype(WIDE) * inverse_group
    gain_one_grad = jnp.sum(normed_group * token_part, axis=0)
    token_part = token_part.astype(LOW).reshape(GROUP, SEQ, D)
    head_ids = lax.broadcasted_iota(jnp.int32, (OWN_HEADS, H), 0) + OWN_HEADS * place
    own_heads = head_ids == lax.broadcasted_iota(jnp.int32, (OWN_HEADS, H), 1)
    forget_wide = dot_plain(forget_low_grad, own_heads.astype(LOW)).astype(LOW)
    forget_w_grad = dot_left_t(hidden_one, forget_wide).reshape(288, SEQ)
    forget_bias_grad = jnp.sum(
        jnp.where(own_heads, jnp.sum(forget_arg_grad, axis=0)[:, None], 0.0), axis=0
    )
    out_part, ffn_sum = fence(out_part, ffn_sum)
    hidden_one_grad = lax.psum_scatter(token_part, ZC, scatter_dimension=0, tiled=False)
    pair_back = pair_back.reshape(GROUP, 2, GROUP, 12, FF_PART)
    pair_back = lax.dynamic_index_in_dim(pair_back, place, 2, keepdims=False)
    pair_back = pair_back.reshape(GROUP, 2, 12, 4, 128).transpose(3, 1, 2, 0, 4).reshape(96, 1024)
    pair_back = dot_plain(pair_back, order)
    out_sum = lax.psum_scatter(out_part, ZC, scatter_dimension=0, tiled=False)
    hidden_one_grad = hidden_one_grad.astype(WIDE)
    forget_bias_grad = jnp.pad(forget_bias_grad, (0, SEQ - H))
    small_grads = jnp.concatenate([gain_one_grad, gain_two_grad, gain_sums[0], forget_bias_grad])
    small_grads = small_grads.reshape(26, SEQ)
    terms, pair_back, small_grads, forget_w_grad = fence(
        terms, pair_back, small_grads, forget_w_grad
    )
    attn_part = jnp.sum(terms.astype(WIDE), axis=0)
    attn_part = jnp.pad(attn_part, ((0, 0), (0, HD))).reshape(GROUP, 12, RAW)
    attn_part = lax.all_to_all(attn_part, ZC, 0, 0, tiled=True)
    *measured, flat = measure(
        weight_sums, attn_part, pair_back, ffn_sum, *old_rows, small_grads, forget_w_grad
    )
    grads, rows_new = measured[:3], measured[3:]
    flat = spread_back(spread_sum(flat))
    input_grad = mixed_grad + norm_back(normed_one, inverse_one, hidden_one_grad * gain_one)
    block_out = (mixed_sum + out_sum.astype(WIDE)).astype(LOW)
    fresh = finish(
        flat,
        grads,
        (attn_weights, ffn_weights, down_weight),
        rows_new,
        old_cols,
        param_rows,
        moment_rows,
    )
    attn_new, ffn_new, down_new, attn_copy, ffn_copy, down_copy = fresh[:6]
    attn_cols_new, ffn_cols_new, down_cols_new, small_new, moments_new = fresh[6:]
    return (
        block_out,
        input_grad,
        grads[0],
        attn_new,
        attn_copy,
        rows_new[0].reshape(5, 12),
        attn_cols_new,
        grads[1],
        ffn_new,
        ffn_copy,
        rows_new[1].reshape(2, 12),
        ffn_cols_new,
        grads[2],
        down_new,
        down_copy,
        rows_new[2].reshape(32),
        down_cols_new.reshape(D),
        small_vector(flat[FLAT_SMALL : FLAT_SMALL + 314]),
        small_vector(small_new),
        small_vector(moments_new),
    )


def solution(mesh):
    chips = Mesh(mesh.devices.reshape(4, 4, 4, 2), ALL)
    rows_first = P(ALL, None)
    rows_second = P(None, ALL, None)
    stat_rows = P(None, ALL)
    flat = P(ALL)
    whole = P()
    return jax.shard_map(
        shards,
        mesh=chips,
        in_specs=(
            rows_first,
            rows_first,
            flat,
            rows_second,
            stat_rows,
            whole,
            rows_second,
            stat_rows,
            whole,
            rows_first,
            flat,
            whole,
            whole,
            whole,
        ),
        out_specs=(
            rows_first,
            rows_first,
            rows_second,
            rows_second,
            rows_second,
            stat_rows,
            whole,
            rows_second,
            rows_second,
            rows_second,
            stat_rows,
            whole,
            rows_first,
            rows_first,
            rows_first,
            flat,
            whole,
            whole,
            whole,
            whole,
        ),
        check_vma=False,
    )
```

```python
import jax
import jax.numpy as jnp
from jax import lax
from jax.experimental import pallas as pl
from jax.experimental.pallas import tpu as pltpu
from jax.sharding import Mesh
from jax.sharding import PartitionSpec as P

D = 1536
H = 24
HD = 64
FF = 4096
SEQ = 128
HALF = D // 2
HEADS = H // 2
GROUP = 8
PLANE = 16
CHIPS = 64
DEVICES = 128
FF_PART = FF // GROUP
OWN_HEADS = H // GROUP
FLAT_ROWS = 640
FLAT_ROW_SUMS = 120
FLAT_SMALL = 280
FLAT_FORGET = 306
FLAT_WEIGHTS = 594
FLAT_END = 602
OWN = 4 * OWN_HEADS * HD
RAW = OWN + 2 * SEQ
WIDE_HEADS = OWN_HEADS * 2 * HD

BETA = 0.5
CLIP = 0.1
RATE = 3.0
EPS_NORM = 1e-06
EPS_STAT = 1e-30
NEG_FILL = -1e30
LOW = jnp.bfloat16
WIDE = jnp.float32

ALL = ("x", "y", "z", "c")
XYZ = ("x", "y", "z")
XY = ("x", "y")
ZC = ("z", "c")


def dot_plain(left_side, right_side):
    return jnp.dot(left_side, right_side, preferred_element_type=WIDE)


def dot_right_t(left_side, right_side):
    return lax.dot_general(
        left_side, right_side, (((1,), (1,)), ((), ())), preferred_element_type=WIDE
    )


def dot_left_t(left_side, right_side):
    return lax.dot_general(
        left_side, right_side, (((0,), (0,)), ((), ())), preferred_element_type=WIDE
    )


def inverse_rms(values):
    return lax.rsqrt(jnp.mean(values * values, axis=-1, keepdims=True) + EPS_NORM)


def norm_back(normed, inverse, grad_out):
    return inverse * (grad_out - normed * jnp.mean(grad_out * normed, axis=-1, keepdims=True))


def split_small(vector):
    widths = [D, D, HD, HD, H]
    pieces = []
    offset = 0
    for piece_width in widths:
        pieces.append(vector[offset : offset + piece_width])
        offset = offset + piece_width
    pieces.append(vector[offset:].reshape(D, H))
    return pieces


SMALL_WIDTHS = (D, D, HD, HD, H, D * H)


def square_sum(weight):
    return jnp.sum(weight * weight, axis=(1, 2))


def fence(*values):
    return lax.optimization_barrier(values)


def swap_core(value):
    return lax.ppermute(value, "c", [(0, 1), (1, 0)])


def reduce_core(part, core):
    keep = lax.dynamic_index_in_dim(part, core, 0, keepdims=False)
    send = lax.dynamic_index_in_dim(part, 1 - core, 0, keepdims=False)
    return keep + swap_core(send)


def hop(value, axis, step):
    return lax.ppermute(value, axis, [(i, (i + step) % 4) for i in range(4)])


def assemble_kernel(
    place_ref, own, near, far_one, far_two, other, near_other, far_other, whole_ref
):
    deep = place_ref[0]
    core = place_ref[1]
    rows = own.shape[0]
    half = rows // 2

    def put(step, side, start, value):
        at = lax.rem(deep + step, 4)
        whole_ref[at, side, start : start + value.shape[0], :] = value

    put(0, core, 0, own[...])
    put(0, 1 - core, 0, other[...])
    put(3, core, 0, near[:rows])
    put(1, core, 0, near[rows:])
    put(3, 1 - core, 0, near_other[:rows])
    put(1, 1 - core, 0, near_other[rows:])
    put(2, core, 0, far_one[...])
    put(2, core, half, far_two[...])
    put(2, 1 - core, 0, far_other[...])


def assemble(*pieces):
    place = jnp.stack([lax.axis_index("z"), lax.axis_index("c")]).astype(jnp.int32)
    rows, columns = pieces[0].shape
    whole = pl.pallas_call(
        assemble_kernel,
        in_specs=[pl.BlockSpec(memory_space=pltpu.SMEM)]
        + [pl.BlockSpec(memory_space=pltpu.VMEM)] * len(pieces),
        out_shape=jax.ShapeDtypeStruct((4, 2, rows, columns), pieces[0].dtype),
        compiler_params=pltpu.CompilerParams(vmem_limit_bytes=40 * 1024 * 1024),
        name="assemble",
    )(place, *pieces)
    return whole.reshape(GROUP * rows, columns)


def gather_group(value, *others):
    rows = value.shape[0] // 2
    before = hop(value, "z", 1)
    after = hop(value, "z", -1)
    other = swap_core(value)
    before, after, other = fence(before, after, other)
    near = jnp.concatenate([before, after])
    far_one = hop(before[:rows], "z", 1)
    far_two = hop(after[rows:], "z", -1)
    near_other = swap_core(near)
    far_one, far_two, near_other, *others = fence(far_one, far_two, near_other, *others)
    far_other = swap_core(jnp.concatenate([far_one, far_two]))
    whole = assemble(value, near, far_one, far_two, other, near_other, far_other)
    return (whole, *others)


def far_halves(part):
    rows = SEQ // 2
    far = part[3].astype(LOW)
    return (hop(far[:rows], "z", 1), hop(far[rows:], "z", -1))


def near_blocks(part, halves):
    rows = SEQ // 2
    to_after = jnp.concatenate([part[2][:rows] + halves[0].astype(WIDE), part[2][rows:]])
    to_before = jnp.concatenate([part[1][:rows], part[1][rows:] + halves[1].astype(WIDE)])
    return (hop(to_after.astype(LOW), "z", 1), hop(to_before.astype(LOW), "z", -1))


def group_reduce_start(part, core, deep):
    got = swap_core(lax.dynamic_index_in_dim(part, 1 - core, 1, keepdims=False))
    part = lax.dynamic_index_in_dim(part, core, 1, keepdims=False)
    part = part.astype(WIDE) + got.astype(WIDE)
    return [
        lax.dynamic_index_in_dim(part, (deep + step) % 4, 0, keepdims=False)
        for step in (0, 3, 1, 2)
    ]


def direct_sum(blocks, axis, dim):
    here = lax.axis_index(axis)
    total = lax.dynamic_index_in_dim(blocks, here, dim, keepdims=False).astype(WIDE)
    for step in (1, 2, 3):
        block = lax.dynamic_index_in_dim(blocks, (here + step) % 4, dim, keepdims=False)
        total = total + hop(block, axis, step).astype(WIDE)
    return total


def split_far(blocks, axis):
    far = lax.dynamic_index_in_dim(blocks, (lax.axis_index(axis) + 2) % 4, 0, keepdims=False)
    half = far.shape[0] // 2
    return (hop(far[:half], axis, 1), hop(far[half:], axis, -1))


def split_near(blocks, axis, halves):
    here = lax.axis_index(axis)
    after = lax.dynamic_index_in_dim(blocks, (here + 1) % 4, 0, keepdims=False)
    before = lax.dynamic_index_in_dim(blocks, (here + 3) % 4, 0, keepdims=False)
    half = after.shape[0] // 2
    to_after = jnp.concatenate([after[:half] + halves[0], after[half:]])
    to_before = jnp.concatenate([before[:half], before[half:] + halves[1]])
    return (hop(to_after, axis, 1), hop(to_before, axis, -1))


def split_sum(blocks, axis, near):
    own = lax.dynamic_index_in_dim(blocks, lax.axis_index(axis), 0, keepdims=False)
    return (own.astype(WIDE) + near[0].astype(WIDE) + near[1].astype(WIDE)).astype(LOW)


def direct_exchange(blocks, axis):
    here = lax.axis_index(axis)
    pieces = [lax.dynamic_index_in_dim(blocks, here, 0, keepdims=False)]
    for step in (1, 2, 3):
        block = lax.dynamic_index_in_dim(blocks, (here + step) % 4, 0, keepdims=False)
        pieces.append(hop(block, axis, step))
    return pieces


def head_stat(values, lane_low):
    low = jnp.sum(jnp.where(lane_low, values, 0.0), axis=-1, keepdims=True) * (1.0 / HD)
    high = jnp.sum(jnp.where(lane_low, 0.0, values), axis=-1, keepdims=True) * (1.0 / HD)
    return jnp.where(lane_low, low, high)


def head_normed(values, lane_low):
    inverse = lax.rsqrt(head_stat(values * values, lane_low) + EPS_NORM)
    return (values * inverse, inverse)


def far(value):
    return pltpu.with_memory_space_constraint(value, pltpu.HBM)


def attend_kernel(
    raw_ref, bias_ref, length_ref, gains_ref, gated_ref, attended_ref, prob_ref
):
    lane = lax.broadcasted_iota(jnp.int32, (SEQ, SEQ), 1)
    lane_low = lane < HD
    slot = lax.broadcasted_iota(jnp.int32, (SEQ, SEQ), 0)
    allowed = (lane <= slot) & (lane.astype(WIDE) < length_ref[0])
    forget = raw_ref[:, RAW - SEQ :] + bias_ref[0:1]
    mine = (lane >= HD) & (lane < HD + OWN_HEADS)
    log_forget = -jnp.log1p(jnp.exp(jnp.where(mine, -forget, 0.0)))
    cols = lax.dot_general(
        (lane <= slot).astype(WIDE),
        log_forget,
        (((1,), (0,)), ((), ())),
        precision=lax.Precision.HIGHEST,
        preferred_element_type=WIDE,
    )
    rows = cols.T
    for head in range(OWN_HEADS):
        at = 2 * head * SEQ
        normed, _ = head_normed(raw_ref[:, at : at + SEQ], lane_low)
        scaled = normed * gains_ref[0:1]
        query = jnp.where(lane_low, scaled, 0.0).astype(LOW)
        key = pltpu.roll(scaled, HD, 1).astype(LOW)
        value_gate = raw_ref[:, at + SEQ : at + 2 * SEQ]
        score = dot_right_t(query, key) * (HD**-0.5)
        score = score + cols[:, HD + head : HD + head + 1]
        score = score - rows[HD + head : HD + head + 1]
        score = jnp.where(allowed, score, NEG_FILL)
        weight = jnp.exp(score - jnp.max(score, axis=-1, keepdims=True))
        prob = weight / jnp.sum(weight, axis=-1, keepdims=True)
        prob_ref[0, head] = prob
        attended = dot_plain(prob.astype(LOW), value_gate.astype(LOW))
        gate = lax.logistic(pltpu.roll(value_gate, HD, 1))
        attended_ref[:, head * SEQ : (head + 1) * SEQ] = attended
        gated = jnp.where(lane_low, attended * gate, 0.0)
        gated_ref[:, head * SEQ : (head + 1) * SEQ] = gated.astype(LOW)


def attend(raw, bias, lengths, gains):
    return pl.pallas_call(
        attend_kernel,
        grid=(GROUP,),
        in_specs=[
            pl.BlockSpec((SEQ, RAW), lambda i: (i, 0)),
            pl.BlockSpec((8, SEQ), lambda i: (0, 0)),
            pl.BlockSpec((1, 1, SEQ), lambda i: (i, 0, 0)),
            pl.BlockSpec((8, SEQ), lambda i: (0, 0)),
        ],
        out_specs=[
            pl.BlockSpec((SEQ, WIDE_HEADS), lambda i: (i, 0)),
            pl.BlockSpec((SEQ, WIDE_HEADS), lambda i: (i, 0)),
            pl.BlockSpec((1, OWN_HEADS, SEQ, SEQ), lambda i: (i, 0, 0, 0)),
        ],
        out_shape=[
            jax.ShapeDtypeStruct((GROUP * SEQ, WIDE_HEADS), LOW),
            jax.ShapeDtypeStruct((GROUP * SEQ, WIDE_HEADS), WIDE),
            jax.ShapeDtypeStruct((GROUP, OWN_HEADS, SEQ, SEQ), WIDE),
        ],
        compiler_params=pltpu.CompilerParams(vmem_limit_bytes=40 * 1024 * 1024),
        cost_estimate=pl.CostEstimate(
            flops=24 * 4 * SEQ**3, bytes_accessed=6_000_000, transcendentals=24 * SEQ * SEQ
        ),
        name="attend",
    )(far(raw), bias, lengths, gains)


def attend_back_kernel(
    raw_ref, gated_grad_ref, attended_ref, prob_ref, gains_ref, grad_ref, forget_ref, gain_ref
):
    lane_low = lax.broadcasted_iota(jnp.int32, (SEQ, SEQ), 1) < HD
    ones = jnp.ones((8, SEQ), LOW)
    gains = gains_ref[0:1]
    forget_ref[...] = jnp.zeros_like(forget_ref)

    @pl.when(pl.program_id(0) == 0)
    def _():
        gain_ref[...] = jnp.zeros_like(gain_ref)

    for head in range(OWN_HEADS):
        at = 2 * head * SEQ
        normed, inverse = head_normed(raw_ref[:, at : at + SEQ], lane_low)
        swapped = pltpu.roll(normed * gains, HD, 1).astype(LOW)
        value_gate = raw_ref[:, at + SEQ : at + 2 * SEQ]
        gate = lax.logistic(pltpu.roll(value_gate, HD, 1))
        gated_grad = gated_grad_ref[:, head * SEQ : (head + 1) * SEQ]
        gated_grad = jnp.where(lane_low, gated_grad, 0.0)
        out_grad = (gated_grad * gate).astype(LOW)
        attended = attended_ref[:, head * SEQ : (head + 1) * SEQ]
        gate_grad = gated_grad * attended * gate * (1.0 - gate)
        prob = prob_ref[0, head]
        prob_grad = dot_right_t(out_grad, value_gate.astype(LOW))
        delta = jnp.sum(prob * prob_grad, axis=-1, keepdims=True)
        score_grad = (prob * (prob_grad - delta)).astype(LOW)
        value_grad = dot_left_t(prob.astype(LOW), out_grad)
        value_gate_grad = jnp.where(lane_low, value_grad, pltpu.roll(gate_grad, HD, 1))
        grad_ref[:, at + SEQ : at + 2 * SEQ] = value_gate_grad.astype(LOW)
        sums = dot_right_t(ones, score_grad) - dot_plain(ones, score_grad)
        forget_ref[0, head : head + 1] = sums[0:1]
        grad = jnp.where(
            lane_low, dot_plain(score_grad, swapped), dot_left_t(score_grad, swapped)
        ) * (HD**-0.5)
        product = grad * normed
        gain_ref[0:1] += jnp.sum(product, axis=0, keepdims=True)
        mean = head_stat(product * gains, lane_low)
        grad_ref[:, at : at + SEQ] = (inverse * (grad * gains - normed * mean)).astype(LOW)


def attend_back(raw, gated_grad, attended, prob, gains):
    return pl.pallas_call(
        attend_back_kernel,
        grid=(GROUP,),
        in_specs=[
            pl.BlockSpec((SEQ, RAW), lambda i: (i, 0)),
            pl.BlockSpec((SEQ, WIDE_HEADS), lambda i: (i, 0)),
            pl.BlockSpec((SEQ, WIDE_HEADS), lambda i: (i, 0)),
            pl.BlockSpec((1, OWN_HEADS, SEQ, SEQ), lambda i: (i, 0, 0, 0)),
            pl.BlockSpec((8, SEQ), lambda i: (0, 0)),
        ],
        out_specs=[
            pl.BlockSpec((SEQ, OWN), lambda i: (i, 0)),
            pl.BlockSpec((1, 8, SEQ), lambda i: (i, 0, 0)),
            pl.BlockSpec((8, SEQ), lambda i: (0, 0)),
        ],
        out_shape=[
            jax.ShapeDtypeStruct((GROUP * SEQ, OWN), LOW),
            jax.ShapeDtypeStruct((GROUP, 8, SEQ), WIDE),
            jax.ShapeDtypeStruct((8, SEQ), WIDE),
        ],
        compiler_params=pltpu.CompilerParams(vmem_limit_bytes=40 * 1024 * 1024),
        cost_estimate=pl.CostEstimate(
            flops=24 * 10 * SEQ**3, bytes_accessed=8_000_000, transcendentals=2 * SEQ * HALF
        ),
        name="attend_back",
    )(far(raw), far(gated_grad), far(attended), far(prob), gains)


def half_tile(ref, matrix, head):
    tile = ref[matrix, :, SEQ * (head // 2) : SEQ * (head // 2) + SEQ]
    return (tile, pltpu.roll(tile, HD, 1))[:: 1 if head % 2 == 0 else -1]


def pack_kernel(length_ref, weight_ref, forget_ref, packed_ref):
    lane = lax.broadcasted_iota(jnp.int32, (12, SEQ), 1)
    lane_low = lane < HD
    forget = forget_ref[...]
    length = jnp.where(lane == SEQ - 1, length_ref[0], 0.0)
    for place in range(GROUP):
        for slot in range(OWN_HEADS):
            head = OWN_HEADS * place + slot
            for pair in range(2):
                left, _ = half_tile(weight_ref, 2 * pair, head)
                _, right = half_tile(weight_ref, 2 * pair + 1, head)
                at = (2 * slot + pair) * SEQ
                tile = jnp.where(lane_low, left, right)
                packed_ref[place, :, at : at + SEQ] = tile.astype(LOW)
        first, _ = half_tile(weight_ref, 4, OWN_HEADS * place)
        _, second = half_tile(weight_ref, 4, OWN_HEADS * place + 1)
        third, _ = half_tile(weight_ref, 4, OWN_HEADS * place + 2)
        packed_ref[place, :, OWN : OWN + SEQ] = jnp.where(lane_low, first, second).astype(LOW)
        rest = pltpu.roll(forget, (HD - OWN_HEADS * place) % SEQ, 1)
        rest = jnp.where(lane < HD + OWN_HEADS, rest, length)
        packed_ref[place, :, OWN + SEQ :] = jnp.where(lane_low, third, rest).astype(LOW)


def pack(length, weights, forget):
    return pl.pallas_call(
        pack_kernel,
        in_specs=[
            pl.BlockSpec(memory_space=pltpu.SMEM),
            pl.BlockSpec(memory_space=pltpu.VMEM),
            pl.BlockSpec(memory_space=pltpu.VMEM),
        ],
        out_shape=jax.ShapeDtypeStruct((GROUP, 12, RAW), LOW),
        compiler_params=pltpu.CompilerParams(vmem_limit_bytes=40 * 1024 * 1024),
        name="pack",
    )(length, weights, forget)


def spread_rows_kernel(blocks_ref, rows_ref):
    for head in range(OWN_HEADS):
        at = head * SEQ
        for pair in range(GROUP // 2):
            left = blocks_ref[2 * pair, head * HD : head * HD + HD, :]
            right = blocks_ref[2 * pair + 1, head * HD : head * HD + HD, :]
            both = jnp.concatenate([left, right], axis=1)
            rows_ref[at : at + HD, 384 * pair : 384 * pair + 384] = both
        rows_ref[at + HD : at + SEQ, :] = jnp.zeros((HD, D), LOW)


def collect_rows_kernel(rows_ref, blocks_ref):
    pieces = [rows_ref[head * SEQ : head * SEQ + HD] for head in range(OWN_HEADS)]
    rows = jnp.concatenate(pieces, axis=0).astype(LOW)
    for block in range(PLANE):
        mine = rows[12 * block : 12 * block + 12]
        blocks_ref[block, :12, :] = mine[:, :OWN]
        blocks_ref[block, 12:, :] = mine[:, OWN:]


def move_rows(kernel, value, shape):
    return pl.pallas_call(
        kernel,
        out_shape=jax.ShapeDtypeStruct(shape, LOW),
        compiler_params=pltpu.CompilerParams(vmem_limit_bytes=40 * 1024 * 1024),
        name="move_rows",
    )(value)


def unpack_kernel(packed_ref, grad_ref):
    lane_low = lax.broadcasted_iota(jnp.int32, (12, SEQ), 1) < HD

    def tile_of(place, at):
        tile = packed_ref[place, :, at : at + SEQ]
        return (tile, pltpu.roll(tile, HD, 1))

    for left in range(0, H, 2):
        places = [(head // OWN_HEADS, head % OWN_HEADS) for head in (left, left + 1)]
        at = SEQ * (left // 2)
        for pair in range(2):
            tiles = [tile_of(place, (2 * slot + pair) * SEQ) for place, slot in places]
            grad_ref[2 * pair, :, at : at + SEQ] = jnp.where(lane_low, tiles[0][0], tiles[1][1])
            grad_ref[2 * pair + 1, :, at : at + SEQ] = jnp.where(lane_low, tiles[0][1], tiles[1][0])


def tiles_of(columns):
    return [(tile, tile * SEQ) for tile in range(columns // SEQ)]


def row_stats(grad_ref, rows_old, columns):
    total = jnp.zeros((grad_ref.shape[0], SEQ), WIDE)
    for _, at in tiles_of(columns):
        part = grad_ref[:, at : at + SEQ]
        total = total + part * part
    mean = jnp.sum(total, axis=1, keepdims=True) * (1.0 / columns)
    return BETA * rows_old + (1.0 - BETA) * (mean + EPS_STAT)


def column_stats(grad_ref, rows_new, columns, flat_ref, plain_at, scaled_at):
    for tile, at in tiles_of(columns):
        part = grad_ref[:, at : at + SEQ]
        part = part * part
        plain = jnp.sum(part, axis=0, keepdims=True)
        scaled = jnp.sum(part / rows_new, axis=0, keepdims=True)
        flat_ref[plain_at + tile : plain_at + tile + 1] = plain
        flat_ref[scaled_at + tile : scaled_at + tile + 1] = scaled


def measure_kernel(
    sums_ref,
    packed_ref,
    out_ref,
    pair_ref,
    ffn_ref,
    attn_rows_ref,
    ffn_rows_ref,
    down_rows_ref,
    small_ref,
    forget_ref,
    attn_grad_ref,
    ffn_grad_ref,
    down_grad_ref,
    attn_rows_new_ref,
    ffn_rows_new_ref,
    down_rows_new_ref,
    flat_ref,
):
    unpack_kernel(packed_ref, attn_grad_ref)
    attn_grad_ref[4] = out_ref[...]
    for block in range(4):
        for matrix in range(2):
            row = 24 * block + 12 * matrix
            ffn_grad_ref[matrix, :, 1024 * block : 1024 * block + 1024] = pair_ref[row : row + 12]
    for part in range(3):
        rows = ffn_ref[192 + 32 * part : 224 + 32 * part]
        down_grad_ref[:, 512 * part : 512 * part + 512] = rows.astype(WIDE)
    flat_ref[FLAT_END:] = jnp.zeros((FLAT_ROWS - FLAT_END, SEQ), WIDE)
    for matrix in range(8):
        value = jnp.full((1, SEQ), sums_ref[matrix], WIDE)
        flat_ref[FLAT_WEIGHTS + matrix : FLAT_WEIGHTS + matrix + 1] = value
    flat_ref[FLAT_SMALL : FLAT_SMALL + 26] = small_ref[...]
    flat_ref[FLAT_FORGET : FLAT_FORGET + 288] = forget_ref[...]
    groups = (
        (attn_grad_ref, attn_rows_ref, attn_rows_new_ref, 5, D, 0, 60, 0),
        (ffn_grad_ref, ffn_rows_ref, ffn_rows_new_ref, 2, FF, 128, 192, 5),
        (down_grad_ref, down_rows_ref, down_rows_new_ref, 1, D, 256, 268, 7),
    )
    for grad_ref, old_ref, new_ref, count, columns, plain_at, scaled_at, first in groups:
        for matrix in range(count):
            mine = grad_ref if first == 7 else grad_ref.at[matrix]
            rows_new = row_stats(mine, old_ref[matrix], columns)
            new_ref[matrix] = rows_new
            at = matrix * (columns // SEQ)
            column_stats(mine, rows_new, columns, flat_ref, plain_at + at, scaled_at + at)
            value = jnp.broadcast_to(jnp.sum(rows_new, axis=0, keepdims=True), (1, SEQ))
            flat_ref[FLAT_ROW_SUMS + first + matrix : FLAT_ROW_SUMS + first + matrix + 1] = value


def measure(sums, packed, out, pair, ffn, attn_rows, ffn_rows, down_rows, small, forget):
    return pl.pallas_call(
        measure_kernel,
        in_specs=[pl.BlockSpec(memory_space=pltpu.SMEM)]
        + [pl.BlockSpec(memory_space=pltpu.VMEM)] * 9,
        out_shape=[
            jax.ShapeDtypeStruct((5, 12, D), WIDE),
            jax.ShapeDtypeStruct((2, 12, FF), WIDE),
            jax.ShapeDtypeStruct((32, D), WIDE),
            jax.ShapeDtypeStruct((5, 12, 1), WIDE),
            jax.ShapeDtypeStruct((2, 12, 1), WIDE),
            jax.ShapeDtypeStruct((1, 32, 1), WIDE),
            jax.ShapeDtypeStruct((FLAT_ROWS, SEQ), WIDE),
        ],
        compiler_params=pltpu.CompilerParams(vmem_limit_bytes=40 * 1024 * 1024),
        name="measure",
    )(sums, packed, out, pair, ffn, attn_rows, ffn_rows, down_rows, small, forget)


def square_total(values):
    return jnp.sum(jnp.sum(values * values, axis=0, keepdims=True), axis=1, keepdims=True)


def finish_kernel(
    flat_ref,
    attn_grad_ref,
    ffn_grad_ref,
    down_grad_ref,
    attn_ref,
    ffn_ref,
    down_ref,
    attn_rows_ref,
    ffn_rows_ref,
    down_rows_ref,
    attn_cols_ref,
    ffn_cols_ref,
    down_cols_ref,
    small_ref,
    moments_ref,
    attn_new_ref,
    ffn_new_ref,
    down_new_ref,
    attn_copy_ref,
    ffn_copy_ref,
    down_copy_ref,
    attn_cols_new_ref,
    ffn_cols_new_ref,
    down_cols_new_ref,
    small_new_ref,
    moments_new_ref,
    *scratch,
):
    *held, arrivals = scratch
    sources = (
        (attn_grad_ref, ffn_grad_ref, down_grad_ref, attn_ref, ffn_ref, down_ref)
        + (attn_rows_ref, ffn_rows_ref, down_rows_ref, small_ref, moments_ref)
    )
    copies = [
        pltpu.make_async_copy(source, target, arrivals.at[place])
        for place, (source, target) in enumerate(zip(sources, held))
    ]
    for copy in copies:
        copy.start()
    for copy in copies:
        copy.wait()
    attn_grad_ref, ffn_grad_ref, down_grad_ref, attn_ref, ffn_ref, down_ref = held[:6]
    attn_rows_ref, ffn_rows_ref, down_rows_ref, small_ref, moments_ref = held[6:]
    groups = (
        (attn_grad_ref, attn_ref, attn_rows_ref, attn_cols_ref)
        + (attn_new_ref, attn_copy_ref, attn_cols_new_ref, 5, D, D, 0, 60, 0),
        (ffn_grad_ref, ffn_ref, ffn_rows_ref, ffn_cols_ref)
        + (ffn_new_ref, ffn_copy_ref, ffn_cols_new_ref, 2, D, FF, 128, 192, 5),
        (down_grad_ref, down_ref, down_rows_ref, down_cols_ref)
        + (down_new_ref, down_copy_ref, down_cols_new_ref, 1, FF, D, 256, 268, 7),
    )
    for (
        grad_ref,
        old_ref,
        rows_ref,
        cols_ref,
        new_ref,
        copy_ref,
        cols_new_ref,
        count,
        all_rows,
        columns,
        plain_at,
        scaled_at,
        first,
    ) in groups:
        entries = all_rows * columns
        tiles = columns // SEQ
        for matrix in range(count):
            whole = first == 7
            grad = grad_ref if whole else grad_ref.at[matrix]
            old = old_ref if whole else old_ref.at[matrix]
            new = new_ref if whole else new_ref.at[matrix]
            copy = copy_ref if whole else copy_ref.at[matrix]
            at = matrix * tiles
            fresh_cols = []
            total = jnp.zeros((1, SEQ), WIDE)
            for tile, place in tiles_of(columns):
                row = plain_at + at + tile
                plain = flat_ref[row : row + 1] * (1.0 / all_rows) + EPS_STAT
                held = cols_ref[matrix : matrix + 1, place : place + SEQ]
                piece = BETA * held + (1.0 - BETA) * plain
                cols_new_ref[matrix : matrix + 1, place : place + SEQ] = piece
                row = scaled_at + at + tile
                total = total + flat_ref[row : row + 1] / piece
                fresh_cols.append(piece)
            row = FLAT_ROW_SUMS + first + matrix
            row_mean = flat_ref[row : row + 1] * (1.0 / all_rows)
            row = FLAT_WEIGHTS + first + matrix
            spread = jnp.sqrt(flat_ref[row : row + 1] * (1.0 / entries) + EPS_NORM)
            total = jnp.sum(total, axis=1, keepdims=True)
            mean_square = row_mean * total * (1.0 / entries)
            factor = RATE * spread / jnp.maximum(1.0, jnp.sqrt(mean_square) / CLIP)
            rows_scale = lax.rsqrt(rows_ref[matrix])
            for tile, place in tiles_of(columns):
                cols_scale = lax.rsqrt(fresh_cols[tile] / row_mean) * factor
                step = grad[:, place : place + SEQ] * rows_scale * cols_scale
                value = old[:, place : place + SEQ] - step
                new[:, place : place + SEQ] = value
                copy[:, place : place + SEQ] = value.astype(LOW)

    lane_low = lax.broadcasted_iota(jnp.int32, (1, SEQ), 1) < HD
    for start, rows, width, lanes in (
        (0, 12, D, None),
        (12, 12, D, None),
        (24, 1, HD, lane_low),
        (24, 1, HD, jnp.logical_not(lane_low)),
        (25, 1, H, None),
        (26, 288, D * H, None),
    ):
        param = small_ref[start : start + rows]
        grad = flat_ref[FLAT_SMALL + start : FLAT_SMALL + start + rows]
        fresh = BETA * moments_ref[start : start + rows] + (1.0 - BETA) * (grad * grad + EPS_STAT)
        update = grad * lax.rsqrt(fresh)
        if lanes is not None:
            update = jnp.where(lanes, update, 0.0)
        inside = param if lanes is None else jnp.where(lanes, param, 0.0)
        clip_ratio = jnp.sqrt(square_total(update) * (1.0 / width)) / CLIP
        spread = jnp.sqrt(square_total(inside) * (1.0 / width) + EPS_NORM)
        value = param - RATE * spread * (update / jnp.maximum(1.0, clip_ratio))
        if lanes is None:
            small_new_ref[start : start + rows] = value
        elif width == HD:
            held = small_new_ref[start : start + rows]
            small_new_ref[start : start + rows] = jnp.where(lanes, value, held)
        moments_new_ref[start : start + rows] = fresh


def finish(flat, grads, weights, rows, cols, small, moments):
    return pl.pallas_call(
        finish_kernel,
        in_specs=[pl.BlockSpec(memory_space=pltpu.VMEM)]
        + [pl.BlockSpec(memory_space=pltpu.HBM)] * 9
        + [pl.BlockSpec(memory_space=pltpu.VMEM)] * 3
        + [pl.BlockSpec(memory_space=pltpu.HBM)] * 2,
        scratch_shapes=[
            pltpu.VMEM(value.shape, WIDE)
            for value in (*grads, *weights, *rows, small, moments)
        ]
        + [pltpu.SemaphoreType.DMA((11,))],
        out_shape=[
            jax.ShapeDtypeStruct((5, 12, D), WIDE),
            jax.ShapeDtypeStruct((2, 12, FF), WIDE),
            jax.ShapeDtypeStruct((32, D), WIDE),
            jax.ShapeDtypeStruct((5, 12, D), LOW),
            jax.ShapeDtypeStruct((2, 12, FF), LOW),
            jax.ShapeDtypeStruct((32, D), LOW),
            jax.ShapeDtypeStruct((5, D), WIDE),
            jax.ShapeDtypeStruct((2, FF), WIDE),
            jax.ShapeDtypeStruct((1, D), WIDE),
            jax.ShapeDtypeStruct((314, SEQ), WIDE),
            jax.ShapeDtypeStruct((314, SEQ), WIDE),
        ],
        compiler_params=pltpu.CompilerParams(vmem_limit_bytes=40 * 1024 * 1024),
        name="finish",
    )(
        flat,
        *[far(value) for value in (*grads, *weights, *rows)],
        *cols,
        far(small),
        far(moments),
    )


def small_rows(vector, fill):
    bias = vector[2 * D + 2 * HD : 2 * D + 2 * HD + H]
    bias = jnp.concatenate([bias, jnp.full((SEQ - H,), fill, WIDE)])
    return jnp.concatenate(
        [
            vector[: 2 * D].reshape(24, SEQ),
            vector[2 * D : 2 * D + 2 * HD].reshape(1, SEQ),
            bias.reshape(1, SEQ),
            vector[2 * D + 2 * HD + H :].reshape(288, SEQ),
        ]
    )


def small_vector(rows):
    return jnp.concatenate(
        [rows[:25].reshape(-1), rows[25, :H], rows[26:].reshape(-1)]
    )


def spread_sum(flat):
    pieces = flat.reshape(DEVICES, -1, SEQ)
    return jnp.sum(lax.all_to_all(pieces, ALL, 0, 0, tiled=True), axis=0)


def spread_back(mine):
    whole = jnp.broadcast_to(mine[None], (DEVICES, *mine.shape))
    return lax.all_to_all(whole, ALL, 0, 0, tiled=True).reshape(-1, SEQ)


def column_order():
    source = lax.broadcasted_iota(jnp.int32, (1024, 1024), 0)
    target = lax.broadcasted_iota(jnp.int32, (1024, 1024), 1)
    lane = source % 128
    return (target == (lane // 32) * 256 + (source // 128) * 32 + lane % 32).astype(LOW)


def shards(
    tokens,
    cotangent,
    lengths,
    attn_weights,
    attn_rows,
    attn_cols,
    ffn_weights,
    ffn_rows,
    ffn_cols,
    down_weight,
    down_rows,
    down_cols,
    small_params,
    small_moments,
):
    core = lax.axis_index("c")
    deep = lax.axis_index("z")
    inputs = tokens.astype(WIDE)
    slot_ids = jnp.arange(SEQ, dtype=jnp.int32)
    valid_rows = slot_ids < lengths[0]
    gain_one, gain_two, query_gain, key_gain, forget_bias, forget_weight = split_small(small_params)

    device = ((lax.axis_index("x") * 4 + lax.axis_index("y")) * 4 + deep) * 2 + core
    forget_rows = lax.dynamic_slice_in_dim(forget_weight, device * 12, 12, axis=0)
    forget_rows = jnp.pad(forget_rows, ((0, 0), (0, SEQ - H)))
    attn_low = pack(lengths.astype(WIDE), attn_weights, forget_rows)
    attn_low = lax.all_to_all(attn_low, ZC, 0, 0, tiled=True)
    lengths_group = attn_low[:, 0, RAW - 1].astype(WIDE)
    attn_low = attn_low.reshape(96, RAW)
    attn_full = lax.all_gather(attn_low, XY, axis=0, tiled=True)
    order = column_order()
    pair_low = ffn_weights.astype(LOW).reshape(24, 4, 1024).transpose(1, 0, 2).reshape(96, 1024)
    pair_low = dot_right_t(pair_low, order).astype(LOW).reshape(4, 2, 12, GROUP, 128)
    pair_low = pair_low.transpose(3, 2, 1, 0, 4).reshape(GROUP, 12, 2 * FF_PART)
    pair_low = lax.all_to_all(pair_low, ZC, 0, 0, tiled=True).reshape(96, 2 * FF_PART)
    down_low = jnp.concatenate(
        [down_weight[:, at : at + 512].astype(LOW) for at in (0, 512, 1024)], axis=0
    )
    seed_grad = cotangent.astype(WIDE) * valid_rows[:, None].astype(WIDE)
    seed_grad, pair_low, down_low = fence(seed_grad, pair_low, down_low)
    seed_low = lax.all_gather(seed_grad.astype(LOW), ZC, axis=0, tiled=True)
    ffn_full = lax.all_gather(
        jnp.concatenate([pair_low, down_low], axis=1), XY, axis=0, tiled=True
    )

    inverse_one = inverse_rms(inputs)
    normed_one = inputs * inverse_one
    attn_low, attn_weights, ffn_weights, down_weight, small_params = fence(
        attn_low, attn_weights, ffn_weights, down_weight, small_params
    )
    tokens_group = gather_group(tokens)[0]
    inputs_group = tokens_group.astype(WIDE)
    inverse_group = inverse_rms(inputs_group)
    hidden_one = (inputs_group * inverse_group * gain_one).astype(LOW)
    place = 2 * deep + core

    lengths_group = jnp.broadcast_to(lengths_group[:, None, None], (GROUP, 1, SEQ))
    forget_low = lax.dynamic_slice_in_dim(forget_weight, place * OWN_HEADS, OWN_HEADS, axis=1)
    forget_low = forget_low.astype(LOW)
    bias_mine = lax.dynamic_slice_in_dim(forget_bias, place * OWN_HEADS, OWN_HEADS, axis=0)
    bias_tile = jnp.pad(bias_mine[None], ((0, 7), (HD, HD - OWN_HEADS)))
    exact = {"precision": lax.Precision.HIGHEST, "preferred_element_type": WIDE}
    slots = lax.broadcasted_iota(jnp.int32, (SEQ, SEQ), 0)
    later = (slots >= lax.broadcasted_iota(jnp.int32, (SEQ, SEQ), 1)).astype(WIDE)
    gains = jnp.concatenate([query_gain, key_gain])[None]
    gains = jnp.pad(gains, ((0, 7), (0, 0)))
    (
        attn_full,
        hidden_one,
        tokens_group,
        inverse_group,
        lengths_group,
        forget_low,
        bias_tile,
        gains,
        order,
    ) = fence(
        attn_full,
        hidden_one,
        tokens_group,
        inverse_group,
        lengths_group,
        forget_low,
        bias_tile,
        gains,
        order,
    )
    proj_full = attn_full[:, :OWN]
    raw, attn_full = fence(dot_plain(hidden_one, attn_full), attn_full)
    out_rows = attn_full[:, OWN : OWN + 3 * HD].reshape(GROUP, 3 * HD, 3 * HD)
    out_rows = lax.all_to_all(out_rows, ZC, 0, 0, tiled=True)
    gated_out, attended, prob = attend(raw, bias_tile, lengths_group, gains)
    out_rows = move_rows(spread_rows_kernel, out_rows, (WIDE_HEADS, D))
    mixed_part = dot_plain(gated_out, out_rows).astype(LOW).reshape(4, 2, SEQ, D)
    mixed_part = group_reduce_start(mixed_part, core, deep)
    half_one, half_two = fence(*far_halves(mixed_part))
    near_one, near_two, *held = fence(
        *near_blocks(mixed_part, (half_one, half_two)),
        small_params,
        small_moments,
        attn_weights,
        ffn_weights,
        down_weight,
        attn_rows,
        ffn_rows,
        down_rows,
    )
    small_params, small_moments, attn_weights, ffn_weights, down_weight = held[:5]
    attn_rows, ffn_rows, down_rows = held[5:]
    param_rows = small_rows(small_params, 0.0)
    moment_rows = small_rows(small_moments, 1.0)
    old_rows = (attn_rows[:, :, None], ffn_rows[:, :, None], down_rows[None, :, None])
    old_cols = (attn_cols, ffn_cols, down_cols[None])
    weight_sums = jnp.concatenate(
        [square_sum(attn_weights), square_sum(ffn_weights), square_sum(down_weight[None])]
    )
    mixed_sum = inputs + mixed_part[0] + near_one.astype(WIDE) + near_two.astype(WIDE)
    inverse_two = inverse_rms(mixed_sum)
    normed_two = mixed_sum * inverse_two
    hidden_two, ffn_full, seed_low, param_rows, moment_rows, old_rows, weight_sums = gather_group(
        (normed_two * gain_two).astype(LOW),
        ffn_full,
        seed_low,
        param_rows,
        moment_rows,
        old_rows,
        weight_sums,
    )
    pair_full = ffn_full[:, : 2 * FF_PART]
    down_full = ffn_full[:, 2 * FF_PART :].reshape(PLANE, 3, 32, 512)
    down_full = jnp.concatenate(
        [down_full[:, part].reshape(FF_PART, 512) for part in range(3)], axis=1
    )

    gate_full = pair_full[:, :FF_PART]
    up_full = pair_full[:, FF_PART:]
    gate_part = dot_plain(hidden_two, gate_full)
    up_part = dot_plain(hidden_two, up_full)
    gate_sig = lax.logistic(gate_part)
    activated = (gate_part * gate_sig * up_part).astype(LOW)
    activated_grad = dot_right_t(seed_low, down_full)
    silu_grad = activated_grad * up_part
    gate_part_grad = silu_grad * gate_sig + silu_grad * gate_part * gate_sig * (1.0 - gate_sig)
    gate_part_grad = gate_part_grad.astype(LOW)
    up_part_grad = (activated_grad * (gate_part * gate_sig)).astype(LOW)
    token_part = dot_right_t(gate_part_grad, gate_full) + dot_right_t(up_part_grad, up_full)
    token_part = token_part.astype(LOW).reshape(4, 2, SEQ, D)
    token_part, hidden_two, gate_part_grad, up_part_grad, activated, seed_low, down_full = fence(
        token_part, hidden_two, gate_part_grad, up_part_grad, activated, seed_low, down_full
    )
    token_got, gate_terms, hidden_two, up_part_grad, activated, seed_low = fence(
        swap_core(lax.dynamic_index_in_dim(token_part, 1 - core, 1, keepdims=False)),
        dot_left_t(hidden_two, gate_part_grad).astype(LOW),
        hidden_two,
        up_part_grad,
        activated,
        seed_low,
    )
    token_part = lax.dynamic_index_in_dim(token_part, core, 1, keepdims=False)
    token_part = token_part.astype(WIDE) + token_got.astype(WIDE)
    token_part, hidden_two, up_part_grad = fence(token_part, hidden_two, up_part_grad)
    token_part = [
        lax.dynamic_index_in_dim(token_part, (deep + step) % 4, 0, keepdims=False)
        for step in (0, 3, 1, 2)
    ]
    half_one, half_two, up_terms, down_terms, activated = fence(
        *far_halves(token_part),
        dot_left_t(hidden_two, up_part_grad).astype(LOW),
        dot_left_t(activated, seed_low).astype(LOW),
        activated,
    )
    down_terms = down_terms.reshape(PLANE, 32, D)
    ffn_terms = jnp.concatenate(
        [
            gate_terms.reshape(PLANE, 96, FF_PART),
            up_terms.reshape(PLANE, 96, FF_PART),
            down_terms[:, :, :512],
            down_terms[:, :, 512:1024],
            down_terms[:, :, 1024:],
        ],
        axis=1,
    )
    out_part = dot_plain(activated, down_full).astype(LOW).reshape(GROUP, SEQ, D)
    near_one, near_two, ffn_terms, out_part = fence(
        *near_blocks(token_part, (half_one, half_two)), ffn_terms, out_part
    )
    ffn_got = lax.all_to_all(ffn_terms, XY, 0, 0, tiled=True)
    hidden_two_grad = token_part[0] + near_one.astype(WIDE) + near_two.astype(WIDE)

    gain_two_grad = jnp.sum(normed_two * hidden_two_grad, axis=0)
    mixed_grad = seed_grad + norm_back(normed_two, inverse_two, hidden_two_grad * gain_two)
    mixed_low, out_part = gather_group(mixed_grad.astype(LOW), out_part)
    gated_grad = dot_right_t(mixed_low, out_rows)
    out_terms = dot_left_t(gated_out, mixed_low)
    out_terms = move_rows(collect_rows_kernel, out_terms, (PLANE, 24, OWN))
    gated_grad, out_terms = fence(gated_grad, out_terms)
    raw_grad, forget_sums, gain_sums = attend_back(raw, gated_grad, attended, prob, gains)
    out_terms, raw_grad, forget_sums, gain_sums = fence(
        out_terms, raw_grad, forget_sums, gain_sums
    )
    terms = jnp.concatenate(
        [
            dot_left_t(hidden_one, raw_grad).astype(LOW).reshape(PLANE, 96, OWN),
            out_terms,
        ],
        axis=1,
    )
    terms, raw_grad, ffn_got = fence(terms, raw_grad, ffn_got)
    terms = lax.all_to_all(terms, XY, 0, 0, tiled=True)
    ffn_sum = jnp.sum(ffn_got.astype(WIDE), axis=0).astype(LOW)

    raw_grad, token_weights, ffn_sum = fence(raw_grad, proj_full, ffn_sum)
    forget_arg = raw[:, OWN + 3 * HD : OWN + 3 * HD + OWN_HEADS] + bias_mine
    log_forget_grad = jnp.einsum(
        "bhu,ut->bth",
        forget_sums[:, :OWN_HEADS],
        later,
        **exact,
    ).reshape(GROUP * SEQ, OWN_HEADS)
    forget_arg_grad = log_forget_grad * (1.0 - lax.logistic(forget_arg))
    forget_low_grad = forget_arg_grad.astype(LOW)
    pair_back = lax.all_gather(ffn_sum[:192], ZC, axis=0, tiled=False)
    raw_grad, forget_low_grad, pair_back = fence(raw_grad, forget_low_grad, pair_back)
    token_part = dot_right_t(raw_grad, token_weights) + dot_right_t(
        forget_low_grad, forget_low
    )
    normed_group = tokens_group.astype(WIDE) * inverse_group
    gain_one_grad = jnp.sum(normed_group * token_part, axis=0)
    token_part = token_part.astype(LOW).reshape(GROUP, SEQ, D)
    head_ids = lax.broadcasted_iota(jnp.int32, (OWN_HEADS, H), 0) + OWN_HEADS * place
    own_heads = head_ids == lax.broadcasted_iota(jnp.int32, (OWN_HEADS, H), 1)
    forget_wide = dot_plain(forget_low_grad, own_heads.astype(LOW)).astype(LOW)
    forget_w_grad = dot_left_t(hidden_one, forget_wide).reshape(288, SEQ)
    forget_bias_grad = jnp.sum(
        jnp.where(own_heads, jnp.sum(forget_arg_grad, axis=0)[:, None], 0.0), axis=0
    )
    out_part, ffn_sum = fence(out_part, ffn_sum)
    hidden_one_grad = lax.psum_scatter(token_part, ZC, scatter_dimension=0, tiled=False)
    pair_back = pair_back.reshape(GROUP, 2, GROUP, 12, FF_PART)
    pair_back = lax.dynamic_index_in_dim(pair_back, place, 2, keepdims=False)
    pair_back = pair_back.reshape(GROUP, 2, 12, 4, 128).transpose(3, 1, 2, 0, 4).reshape(96, 1024)
    pair_back = dot_plain(pair_back, order)
    out_sum = lax.psum_scatter(out_part, ZC, scatter_dimension=0, tiled=False)
    hidden_one_grad = hidden_one_grad.astype(WIDE)
    forget_bias_grad = jnp.pad(forget_bias_grad, (0, SEQ - H))
    small_grads = jnp.concatenate([gain_one_grad, gain_two_grad, gain_sums[0], forget_bias_grad])
    small_grads = small_grads.reshape(26, SEQ)
    terms, pair_back, small_grads, forget_w_grad = fence(
        terms, pair_back, small_grads, forget_w_grad
    )
    attn_part = jnp.sum(terms.astype(WIDE), axis=0)
    out_part = jnp.concatenate([attn_part[96:108], attn_part[108:]], axis=1)
    out_part = lax.ppermute(
        out_part,
        ALL,
        [(GROUP * row + col, PLANE * col + row) for row in range(PLANE) for col in range(GROUP)],
    )
    attn_part = attn_part[:96].reshape(GROUP, 12, OWN)
    attn_part = lax.all_to_all(attn_part, ZC, 0, 0, tiled=True)
    *measured, flat = measure(
        weight_sums, attn_part, out_part, pair_back, ffn_sum, *old_rows, small_grads, forget_w_grad
    )
    grads, rows_new = measured[:3], measured[3:]
    flat = spread_back(spread_sum(flat))
    input_grad = mixed_grad + norm_back(normed_one, inverse_one, hidden_one_grad * gain_one)
    block_out = (mixed_sum + out_sum.astype(WIDE)).astype(LOW)
    fresh = finish(
        flat,
        grads,
        (attn_weights, ffn_weights, down_weight),
        rows_new,
        old_cols,
        param_rows,
        moment_rows,
    )
    attn_new, ffn_new, down_new, attn_copy, ffn_copy, down_copy = fresh[:6]
    attn_cols_new, ffn_cols_new, down_cols_new, small_new, moments_new = fresh[6:]
    return (
        block_out,
        input_grad,
        grads[0],
        attn_new,
        attn_copy,
        rows_new[0].reshape(5, 12),
        attn_cols_new,
        grads[1],
        ffn_new,
        ffn_copy,
        rows_new[1].reshape(2, 12),
        ffn_cols_new,
        grads[2],
        down_new,
        down_copy,
        rows_new[2].reshape(32),
        down_cols_new.reshape(D),
        small_vector(flat[FLAT_SMALL : FLAT_SMALL + 314]),
        small_vector(small_new),
        small_vector(moments_new),
    )


def solution(mesh):
    chips = Mesh(mesh.devices.reshape(4, 4, 4, 2), ALL)
    rows_first = P(ALL, None)
    rows_second = P(None, ALL, None)
    stat_rows = P(None, ALL)
    flat = P(ALL)
    whole = P()
    return jax.shard_map(
        shards,
        mesh=chips,
        in_specs=(
            rows_first,
            rows_first,
            flat,
            rows_second,
            stat_rows,
            whole,
            rows_second,
            stat_rows,
            whole,
            rows_first,
            flat,
            whole,
            whole,
            whole,
        ),
        out_specs=(
            rows_first,
            rows_first,
            rows_second,
            rows_second,
            rows_second,
            stat_rows,
            whole,
            rows_second,
            rows_second,
            rows_second,
            stat_rows,
            whole,
            rows_first,
            rows_first,
            rows_first,
            flat,
            whole,
            whole,
            whole,
            whole,
        ),
        check_vma=False,
    )
```

```python
import jax
import jax.numpy as jnp
from jax import lax
from jax.experimental import pallas as pl
from jax.experimental.pallas import tpu as pltpu
from jax.sharding import Mesh
from jax.sharding import PartitionSpec as P

D = 1536
H = 24
HD = 64
FF = 4096
SEQ = 128
HALF = D // 2
HEADS = H // 2
GROUP = 8
PLANE = 16
CHIPS = 64
DEVICES = 128
FF_PART = FF // GROUP
OWN_HEADS = H // GROUP
FLAT_ROWS = 640
FLAT_ROW_SUMS = 120
FLAT_SMALL = 280
FLAT_FORGET = 306
FLAT_WEIGHTS = 594
FLAT_END = 602
OWN = 4 * OWN_HEADS * HD
RAW = OWN + 2 * SEQ
WIDE_HEADS = OWN_HEADS * 2 * HD

BETA = 0.5
CLIP = 0.1
RATE = 3.0
EPS_NORM = 1e-06
EPS_STAT = 1e-30
NEG_FILL = -1e30
LOW = jnp.bfloat16
WIDE = jnp.float32

ALL = ("x", "y", "z", "c")
XYZ = ("x", "y", "z")
XY = ("x", "y")
ZC = ("z", "c")


def dot_plain(left_side, right_side):
    return jnp.dot(left_side, right_side, preferred_element_type=WIDE)


def dot_right_t(left_side, right_side):
    return lax.dot_general(
        left_side, right_side, (((1,), (1,)), ((), ())), preferred_element_type=WIDE
    )


def dot_left_t(left_side, right_side):
    return lax.dot_general(
        left_side, right_side, (((0,), (0,)), ((), ())), preferred_element_type=WIDE
    )


def inverse_rms(values):
    return lax.rsqrt(jnp.mean(values * values, axis=-1, keepdims=True) + EPS_NORM)


def norm_back(normed, inverse, grad_out):
    return inverse * (grad_out - normed * jnp.mean(grad_out * normed, axis=-1, keepdims=True))


def split_small(vector):
    widths = [D, D, HD, HD, H]
    pieces = []
    offset = 0
    for piece_width in widths:
        pieces.append(vector[offset : offset + piece_width])
        offset = offset + piece_width
    pieces.append(vector[offset:].reshape(D, H))
    return pieces


SMALL_WIDTHS = (D, D, HD, HD, H, D * H)


def square_sum(weight):
    return jnp.sum(weight * weight, axis=(1, 2))


def fence(*values):
    return lax.optimization_barrier(values)


def swap_core(value):
    return lax.ppermute(value, "c", [(0, 1), (1, 0)])


def reduce_core(part, core):
    keep = lax.dynamic_index_in_dim(part, core, 0, keepdims=False)
    send = lax.dynamic_index_in_dim(part, 1 - core, 0, keepdims=False)
    return keep + swap_core(send)


def hop(value, axis, step):
    return lax.ppermute(value, axis, [(i, (i + step) % 4) for i in range(4)])


def assemble_kernel(
    place_ref, own, near, far_one, far_two, other, near_other, far_other, whole_ref
):
    deep = place_ref[0]
    core = place_ref[1]
    rows = own.shape[0]
    half = rows // 2

    def put(step, side, start, value):
        at = lax.rem(deep + step, 4)
        whole_ref[at, side, start : start + value.shape[0], :] = value

    put(0, core, 0, own[...])
    put(0, 1 - core, 0, other[...])
    put(3, core, 0, near[:rows])
    put(1, core, 0, near[rows:])
    put(3, 1 - core, 0, near_other[:rows])
    put(1, 1 - core, 0, near_other[rows:])
    put(2, core, 0, far_one[...])
    put(2, core, half, far_two[...])
    put(2, 1 - core, 0, far_other[...])


def assemble(*pieces):
    place = jnp.stack([lax.axis_index("z"), lax.axis_index("c")]).astype(jnp.int32)
    rows, columns = pieces[0].shape
    whole = pl.pallas_call(
        assemble_kernel,
        in_specs=[pl.BlockSpec(memory_space=pltpu.SMEM)]
        + [pl.BlockSpec(memory_space=pltpu.VMEM)] * len(pieces),
        out_shape=jax.ShapeDtypeStruct((4, 2, rows, columns), pieces[0].dtype),
        compiler_params=pltpu.CompilerParams(vmem_limit_bytes=40 * 1024 * 1024),
        name="assemble",
    )(place, *pieces)
    return whole.reshape(GROUP * rows, columns)


def gather_group(value, *others):
    rows = value.shape[0] // 2
    before = hop(value, "z", 1)
    after = hop(value, "z", -1)
    other = swap_core(value)
    before, after, other = fence(before, after, other)
    near = jnp.concatenate([before, after])
    far_one = hop(before[:rows], "z", 1)
    far_two = hop(after[rows:], "z", -1)
    near_other = swap_core(near)
    far_one, far_two, near_other, *others = fence(far_one, far_two, near_other, *others)
    far_other = swap_core(jnp.concatenate([far_one, far_two]))
    whole = assemble(value, near, far_one, far_two, other, near_other, far_other)
    return (whole, *others)


def far_halves(part):
    rows = SEQ // 2
    far = part[3].astype(LOW)
    return (hop(far[:rows], "z", 1), hop(far[rows:], "z", -1))


def near_blocks(part, halves):
    rows = SEQ // 2
    to_after = jnp.concatenate([part[2][:rows] + halves[0].astype(WIDE), part[2][rows:]])
    to_before = jnp.concatenate([part[1][:rows], part[1][rows:] + halves[1].astype(WIDE)])
    return (hop(to_after.astype(LOW), "z", 1), hop(to_before.astype(LOW), "z", -1))


def group_reduce_start(part, core, deep):
    got = swap_core(lax.dynamic_index_in_dim(part, 1 - core, 1, keepdims=False))
    part = lax.dynamic_index_in_dim(part, core, 1, keepdims=False)
    part = part.astype(WIDE) + got.astype(WIDE)
    return [
        lax.dynamic_index_in_dim(part, (deep + step) % 4, 0, keepdims=False)
        for step in (0, 3, 1, 2)
    ]


def direct_sum(blocks, axis, dim):
    here = lax.axis_index(axis)
    total = lax.dynamic_index_in_dim(blocks, here, dim, keepdims=False).astype(WIDE)
    for step in (1, 2, 3):
        block = lax.dynamic_index_in_dim(blocks, (here + step) % 4, dim, keepdims=False)
        total = total + hop(block, axis, step).astype(WIDE)
    return total


def split_far(blocks, axis):
    far = lax.dynamic_index_in_dim(blocks, (lax.axis_index(axis) + 2) % 4, 0, keepdims=False)
    half = far.shape[0] // 2
    return (hop(far[:half], axis, 1), hop(far[half:], axis, -1))


def split_near(blocks, axis, halves):
    here = lax.axis_index(axis)
    after = lax.dynamic_index_in_dim(blocks, (here + 1) % 4, 0, keepdims=False)
    before = lax.dynamic_index_in_dim(blocks, (here + 3) % 4, 0, keepdims=False)
    half = after.shape[0] // 2
    to_after = jnp.concatenate([after[:half] + halves[0], after[half:]])
    to_before = jnp.concatenate([before[:half], before[half:] + halves[1]])
    return (hop(to_after, axis, 1), hop(to_before, axis, -1))


def split_sum(blocks, axis, near):
    own = lax.dynamic_index_in_dim(blocks, lax.axis_index(axis), 0, keepdims=False)
    return (own.astype(WIDE) + near[0].astype(WIDE) + near[1].astype(WIDE)).astype(LOW)


def direct_exchange(blocks, axis):
    here = lax.axis_index(axis)
    pieces = [lax.dynamic_index_in_dim(blocks, here, 0, keepdims=False)]
    for step in (1, 2, 3):
        block = lax.dynamic_index_in_dim(blocks, (here + step) % 4, 0, keepdims=False)
        pieces.append(hop(block, axis, step))
    return pieces


def head_stat(values, lane_low):
    low = jnp.sum(jnp.where(lane_low, values, 0.0), axis=-1, keepdims=True) * (1.0 / HD)
    high = jnp.sum(jnp.where(lane_low, 0.0, values), axis=-1, keepdims=True) * (1.0 / HD)
    return jnp.where(lane_low, low, high)


def head_normed(values, lane_low):
    inverse = lax.rsqrt(head_stat(values * values, lane_low) + EPS_NORM)
    return (values * inverse, inverse)


def far(value):
    return pltpu.with_memory_space_constraint(value, pltpu.HBM)


def attend_kernel(
    raw_ref, bias_ref, length_ref, gains_ref, gated_ref, attended_ref, prob_ref
):
    lane = lax.broadcasted_iota(jnp.int32, (SEQ, SEQ), 1)
    lane_low = lane < HD
    slot = lax.broadcasted_iota(jnp.int32, (SEQ, SEQ), 0)
    allowed = (lane <= slot) & (lane.astype(WIDE) < length_ref[0])
    forget = raw_ref[:, RAW - SEQ :] + bias_ref[0:1]
    mine = (lane >= HD) & (lane < HD + OWN_HEADS)
    log_forget = -jnp.log1p(jnp.exp(jnp.where(mine, -forget, 0.0)))
    cols = lax.dot_general(
        (lane <= slot).astype(WIDE),
        log_forget,
        (((1,), (0,)), ((), ())),
        precision=lax.Precision.HIGHEST,
        preferred_element_type=WIDE,
    )
    rows = cols.T
    for head in range(OWN_HEADS):
        at = 2 * head * SEQ
        normed, _ = head_normed(raw_ref[:, at : at + SEQ], lane_low)
        scaled = normed * gains_ref[0:1]
        query = jnp.where(lane_low, scaled, 0.0).astype(LOW)
        key = pltpu.roll(scaled, HD, 1).astype(LOW)
        value_gate = raw_ref[:, at + SEQ : at + 2 * SEQ]
        score = dot_right_t(query, key) * (HD**-0.5)
        score = score + cols[:, HD + head : HD + head + 1]
        score = score - rows[HD + head : HD + head + 1]
        score = jnp.where(allowed, score, NEG_FILL)
        weight = jnp.exp(score - jnp.max(score, axis=-1, keepdims=True))
        prob = weight / jnp.sum(weight, axis=-1, keepdims=True)
        prob_ref[0, head] = prob
        attended = dot_plain(prob.astype(LOW), value_gate.astype(LOW))
        gate = lax.logistic(pltpu.roll(value_gate, HD, 1))
        attended_ref[:, head * SEQ : (head + 1) * SEQ] = attended
        gated = jnp.where(lane_low, attended * gate, 0.0)
        gated_ref[:, head * SEQ : (head + 1) * SEQ] = gated.astype(LOW)


def attend(raw, bias, lengths, gains):
    return pl.pallas_call(
        attend_kernel,
        grid=(GROUP,),
        in_specs=[
            pl.BlockSpec((SEQ, RAW), lambda i: (i, 0)),
            pl.BlockSpec((8, SEQ), lambda i: (0, 0)),
            pl.BlockSpec((1, 1, SEQ), lambda i: (i, 0, 0)),
            pl.BlockSpec((8, SEQ), lambda i: (0, 0)),
        ],
        out_specs=[
            pl.BlockSpec((SEQ, WIDE_HEADS), lambda i: (i, 0)),
            pl.BlockSpec((SEQ, WIDE_HEADS), lambda i: (i, 0)),
            pl.BlockSpec((1, OWN_HEADS, SEQ, SEQ), lambda i: (i, 0, 0, 0)),
        ],
        out_shape=[
            jax.ShapeDtypeStruct((GROUP * SEQ, WIDE_HEADS), LOW),
            jax.ShapeDtypeStruct((GROUP * SEQ, WIDE_HEADS), WIDE),
            jax.ShapeDtypeStruct((GROUP, OWN_HEADS, SEQ, SEQ), WIDE),
        ],
        compiler_params=pltpu.CompilerParams(vmem_limit_bytes=40 * 1024 * 1024),
        cost_estimate=pl.CostEstimate(
            flops=24 * 4 * SEQ**3, bytes_accessed=6_000_000, transcendentals=24 * SEQ * SEQ
        ),
        name="attend",
    )(far(raw), bias, lengths, gains)


def attend_back_kernel(
    raw_ref, gated_grad_ref, attended_ref, prob_ref, gains_ref, grad_ref, forget_ref, gain_ref
):
    lane_low = lax.broadcasted_iota(jnp.int32, (SEQ, SEQ), 1) < HD
    ones = jnp.ones((8, SEQ), LOW)
    gains = gains_ref[0:1]
    forget_ref[...] = jnp.zeros_like(forget_ref)

    @pl.when(pl.program_id(0) == 0)
    def _():
        gain_ref[...] = jnp.zeros_like(gain_ref)

    for head in range(OWN_HEADS):
        at = 2 * head * SEQ
        normed, inverse = head_normed(raw_ref[:, at : at + SEQ], lane_low)
        swapped = pltpu.roll(normed * gains, HD, 1).astype(LOW)
        value_gate = raw_ref[:, at + SEQ : at + 2 * SEQ]
        gate = lax.logistic(pltpu.roll(value_gate, HD, 1))
        gated_grad = gated_grad_ref[:, head * SEQ : (head + 1) * SEQ]
        gated_grad = jnp.where(lane_low, gated_grad, 0.0)
        out_grad = (gated_grad * gate).astype(LOW)
        attended = attended_ref[:, head * SEQ : (head + 1) * SEQ]
        gate_grad = gated_grad * attended * gate * (1.0 - gate)
        prob = prob_ref[0, head]
        prob_grad = dot_right_t(out_grad, value_gate.astype(LOW))
        delta = jnp.sum(prob * prob_grad, axis=-1, keepdims=True)
        score_grad = (prob * (prob_grad - delta)).astype(LOW)
        value_grad = dot_left_t(prob.astype(LOW), out_grad)
        value_gate_grad = jnp.where(lane_low, value_grad, pltpu.roll(gate_grad, HD, 1))
        grad_ref[:, at + SEQ : at + 2 * SEQ] = value_gate_grad.astype(LOW)
        sums = dot_right_t(ones, score_grad) - dot_plain(ones, score_grad)
        forget_ref[0, head : head + 1] = sums[0:1]
        grad = jnp.where(
            lane_low, dot_plain(score_grad, swapped), dot_left_t(score_grad, swapped)
        ) * (HD**-0.5)
        product = grad * normed
        gain_ref[0:1] += jnp.sum(product, axis=0, keepdims=True)
        mean = head_stat(product * gains, lane_low)
        grad_ref[:, at : at + SEQ] = (inverse * (grad * gains - normed * mean)).astype(LOW)


def attend_back(raw, gated_grad, attended, prob, gains):
    return pl.pallas_call(
        attend_back_kernel,
        grid=(GROUP,),
        in_specs=[
            pl.BlockSpec((SEQ, RAW), lambda i: (i, 0)),
            pl.BlockSpec((SEQ, WIDE_HEADS), lambda i: (i, 0)),
            pl.BlockSpec((SEQ, WIDE_HEADS), lambda i: (i, 0)),
            pl.BlockSpec((1, OWN_HEADS, SEQ, SEQ), lambda i: (i, 0, 0, 0)),
            pl.BlockSpec((8, SEQ), lambda i: (0, 0)),
        ],
        out_specs=[
            pl.BlockSpec((SEQ, OWN), lambda i: (i, 0)),
            pl.BlockSpec((1, 8, SEQ), lambda i: (i, 0, 0)),
            pl.BlockSpec((8, SEQ), lambda i: (0, 0)),
        ],
        out_shape=[
            jax.ShapeDtypeStruct((GROUP * SEQ, OWN), LOW),
            jax.ShapeDtypeStruct((GROUP, 8, SEQ), WIDE),
            jax.ShapeDtypeStruct((8, SEQ), WIDE),
        ],
        compiler_params=pltpu.CompilerParams(vmem_limit_bytes=40 * 1024 * 1024),
        cost_estimate=pl.CostEstimate(
            flops=24 * 10 * SEQ**3, bytes_accessed=8_000_000, transcendentals=2 * SEQ * HALF
        ),
        name="attend_back",
    )(far(raw), far(gated_grad), far(attended), far(prob), gains)


def half_tile(ref, matrix, head):
    tile = ref[matrix, :, SEQ * (head // 2) : SEQ * (head // 2) + SEQ]
    return (tile, pltpu.roll(tile, HD, 1))[:: 1 if head % 2 == 0 else -1]


def pack_kernel(length_ref, weight_ref, forget_ref, packed_ref):
    lane = lax.broadcasted_iota(jnp.int32, (12, SEQ), 1)
    lane_low = lane < HD
    forget = forget_ref[...]
    length = jnp.where(lane == SEQ - 1, length_ref[0], 0.0)
    for place in range(GROUP):
        for slot in range(OWN_HEADS):
            head = OWN_HEADS * place + slot
            for pair in range(2):
                left, _ = half_tile(weight_ref, 2 * pair, head)
                _, right = half_tile(weight_ref, 2 * pair + 1, head)
                at = (2 * slot + pair) * SEQ
                tile = jnp.where(lane_low, left, right)
                packed_ref[place, :, at : at + SEQ] = tile.astype(LOW)
        first, _ = half_tile(weight_ref, 4, OWN_HEADS * place)
        _, second = half_tile(weight_ref, 4, OWN_HEADS * place + 1)
        third, _ = half_tile(weight_ref, 4, OWN_HEADS * place + 2)
        packed_ref[place, :, OWN : OWN + SEQ] = jnp.where(lane_low, first, second).astype(LOW)
        rest = pltpu.roll(forget, (HD - OWN_HEADS * place) % SEQ, 1)
        rest = jnp.where(lane < HD + OWN_HEADS, rest, length)
        packed_ref[place, :, OWN + SEQ :] = jnp.where(lane_low, third, rest).astype(LOW)


def pack(length, weights, forget):
    return pl.pallas_call(
        pack_kernel,
        in_specs=[
            pl.BlockSpec(memory_space=pltpu.SMEM),
            pl.BlockSpec(memory_space=pltpu.VMEM),
            pl.BlockSpec(memory_space=pltpu.VMEM),
        ],
        out_shape=jax.ShapeDtypeStruct((GROUP, 12, RAW), LOW),
        compiler_params=pltpu.CompilerParams(vmem_limit_bytes=40 * 1024 * 1024),
        name="pack",
    )(length, weights, forget)


def spread_rows_kernel(blocks_ref, rows_ref):
    for head in range(OWN_HEADS):
        at = head * SEQ
        for pair in range(GROUP // 2):
            left = blocks_ref[2 * pair, head * HD : head * HD + HD, :]
            right = blocks_ref[2 * pair + 1, head * HD : head * HD + HD, :]
            both = jnp.concatenate([left, right], axis=1)
            rows_ref[at : at + HD, 384 * pair : 384 * pair + 384] = both
        rows_ref[at + HD : at + SEQ, :] = jnp.zeros((HD, D), LOW)


def collect_rows_kernel(rows_ref, blocks_ref):
    pieces = [rows_ref[head * SEQ : head * SEQ + HD] for head in range(OWN_HEADS)]
    rows = jnp.concatenate(pieces, axis=0).astype(LOW)
    for block in range(PLANE):
        mine = rows[12 * block : 12 * block + 12]
        blocks_ref[block, :12, :] = mine[:, :OWN]
        blocks_ref[block, 12:, :] = mine[:, OWN:]


def move_rows(kernel, value, shape):
    return pl.pallas_call(
        kernel,
        out_shape=jax.ShapeDtypeStruct(shape, LOW),
        compiler_params=pltpu.CompilerParams(vmem_limit_bytes=40 * 1024 * 1024),
        name="move_rows",
    )(value)


def unpack_kernel(packed_ref, grad_ref):
    lane_low = lax.broadcasted_iota(jnp.int32, (12, SEQ), 1) < HD

    def tile_of(place, at):
        tile = packed_ref[place, :, at : at + SEQ]
        return (tile, pltpu.roll(tile, HD, 1))

    for left in range(0, H, 2):
        places = [(head // OWN_HEADS, head % OWN_HEADS) for head in (left, left + 1)]
        at = SEQ * (left // 2)
        for pair in range(2):
            tiles = [tile_of(place, (2 * slot + pair) * SEQ) for place, slot in places]
            grad_ref[2 * pair, :, at : at + SEQ] = jnp.where(lane_low, tiles[0][0], tiles[1][1])
            grad_ref[2 * pair + 1, :, at : at + SEQ] = jnp.where(lane_low, tiles[0][1], tiles[1][0])


def tiles_of(columns):
    return [(tile, tile * SEQ) for tile in range(columns // SEQ)]


def row_stats(grad_ref, rows_old, columns):
    total = jnp.zeros((grad_ref.shape[0], SEQ), WIDE)
    for _, at in tiles_of(columns):
        part = grad_ref[:, at : at + SEQ]
        total = total + part * part
    mean = jnp.sum(total, axis=1, keepdims=True) * (1.0 / columns)
    return BETA * rows_old + (1.0 - BETA) * (mean + EPS_STAT)


def column_stats(grad_ref, rows_new, columns, flat_ref, plain_at, scaled_at):
    for tile, at in tiles_of(columns):
        part = grad_ref[:, at : at + SEQ]
        part = part * part
        plain = jnp.sum(part, axis=0, keepdims=True)
        scaled = jnp.sum(part / rows_new, axis=0, keepdims=True)
        flat_ref[plain_at + tile : plain_at + tile + 1] = plain
        flat_ref[scaled_at + tile : scaled_at + tile + 1] = scaled


def measure_kernel(
    sums_ref,
    packed_ref,
    out_ref,
    pair_ref,
    ffn_ref,
    attn_rows_ref,
    ffn_rows_ref,
    down_rows_ref,
    small_ref,
    forget_ref,
    attn_grad_ref,
    ffn_grad_ref,
    down_grad_ref,
    attn_rows_new_ref,
    ffn_rows_new_ref,
    down_rows_new_ref,
    flat_ref,
):
    unpack_kernel(packed_ref, attn_grad_ref)
    attn_grad_ref[4] = out_ref[...]
    for block in range(4):
        for matrix in range(2):
            row = 24 * block + 12 * matrix
            ffn_grad_ref[matrix, :, 1024 * block : 1024 * block + 1024] = pair_ref[row : row + 12]
    for part in range(3):
        rows = ffn_ref[32 * part : 32 * part + 32]
        down_grad_ref[:, 512 * part : 512 * part + 512] = rows.astype(WIDE)
    flat_ref[FLAT_END:] = jnp.zeros((FLAT_ROWS - FLAT_END, SEQ), WIDE)
    for matrix in range(8):
        value = jnp.full((1, SEQ), sums_ref[matrix], WIDE)
        flat_ref[FLAT_WEIGHTS + matrix : FLAT_WEIGHTS + matrix + 1] = value
    flat_ref[FLAT_SMALL : FLAT_SMALL + 26] = small_ref[...]
    flat_ref[FLAT_FORGET : FLAT_FORGET + 288] = forget_ref[...]
    groups = (
        (attn_grad_ref, attn_rows_ref, attn_rows_new_ref, 5, D, 0, 60, 0),
        (ffn_grad_ref, ffn_rows_ref, ffn_rows_new_ref, 2, FF, 128, 192, 5),
        (down_grad_ref, down_rows_ref, down_rows_new_ref, 1, D, 256, 268, 7),
    )
    for grad_ref, old_ref, new_ref, count, columns, plain_at, scaled_at, first in groups:
        for matrix in range(count):
            mine = grad_ref if first == 7 else grad_ref.at[matrix]
            rows_new = row_stats(mine, old_ref[matrix], columns)
            new_ref[matrix] = rows_new
            at = matrix * (columns // SEQ)
            column_stats(mine, rows_new, columns, flat_ref, plain_at + at, scaled_at + at)
            value = jnp.broadcast_to(jnp.sum(rows_new, axis=0, keepdims=True), (1, SEQ))
            flat_ref[FLAT_ROW_SUMS + first + matrix : FLAT_ROW_SUMS + first + matrix + 1] = value


def measure(sums, packed, out, pair, ffn, attn_rows, ffn_rows, down_rows, small, forget):
    return pl.pallas_call(
        measure_kernel,
        in_specs=[pl.BlockSpec(memory_space=pltpu.SMEM)]
        + [pl.BlockSpec(memory_space=pltpu.VMEM)] * 9,
        out_shape=[
            jax.ShapeDtypeStruct((5, 12, D), WIDE),
            jax.ShapeDtypeStruct((2, 12, FF), WIDE),
            jax.ShapeDtypeStruct((32, D), WIDE),
            jax.ShapeDtypeStruct((5, 12, 1), WIDE),
            jax.ShapeDtypeStruct((2, 12, 1), WIDE),
            jax.ShapeDtypeStruct((1, 32, 1), WIDE),
            jax.ShapeDtypeStruct((FLAT_ROWS, SEQ), WIDE),
        ],
        compiler_params=pltpu.CompilerParams(vmem_limit_bytes=40 * 1024 * 1024),
        name="measure",
    )(sums, packed, out, pair, ffn, attn_rows, ffn_rows, down_rows, small, forget)


def square_total(values):
    return jnp.sum(jnp.sum(values * values, axis=0, keepdims=True), axis=1, keepdims=True)


def finish_kernel(
    flat_ref,
    attn_grad_ref,
    ffn_grad_ref,
    down_grad_ref,
    attn_ref,
    ffn_ref,
    down_ref,
    attn_rows_ref,
    ffn_rows_ref,
    down_rows_ref,
    attn_cols_ref,
    ffn_cols_ref,
    down_cols_ref,
    small_ref,
    moments_ref,
    attn_new_ref,
    ffn_new_ref,
    down_new_ref,
    attn_copy_ref,
    ffn_copy_ref,
    down_copy_ref,
    attn_cols_new_ref,
    ffn_cols_new_ref,
    down_cols_new_ref,
    small_new_ref,
    moments_new_ref,
    *scratch,
):
    *held, arrivals = scratch
    sources = (
        (attn_grad_ref, ffn_grad_ref, down_grad_ref, attn_ref, ffn_ref, down_ref)
        + (attn_rows_ref, ffn_rows_ref, down_rows_ref, small_ref, moments_ref)
    )
    copies = [
        pltpu.make_async_copy(source, target, arrivals.at[place])
        for place, (source, target) in enumerate(zip(sources, held))
    ]
    for copy in copies:
        copy.start()
    for copy in copies:
        copy.wait()
    attn_grad_ref, ffn_grad_ref, down_grad_ref, attn_ref, ffn_ref, down_ref = held[:6]
    attn_rows_ref, ffn_rows_ref, down_rows_ref, small_ref, moments_ref = held[6:]
    groups = (
        (attn_grad_ref, attn_ref, attn_rows_ref, attn_cols_ref)
        + (attn_new_ref, attn_copy_ref, attn_cols_new_ref, 5, D, D, 0, 60, 0),
        (ffn_grad_ref, ffn_ref, ffn_rows_ref, ffn_cols_ref)
        + (ffn_new_ref, ffn_copy_ref, ffn_cols_new_ref, 2, D, FF, 128, 192, 5),
        (down_grad_ref, down_ref, down_rows_ref, down_cols_ref)
        + (down_new_ref, down_copy_ref, down_cols_new_ref, 1, FF, D, 256, 268, 7),
    )
    for (
        grad_ref,
        old_ref,
        rows_ref,
        cols_ref,
        new_ref,
        copy_ref,
        cols_new_ref,
        count,
        all_rows,
        columns,
        plain_at,
        scaled_at,
        first,
    ) in groups:
        entries = all_rows * columns
        tiles = columns // SEQ
        for matrix in range(count):
            whole = first == 7
            grad = grad_ref if whole else grad_ref.at[matrix]
            old = old_ref if whole else old_ref.at[matrix]
            new = new_ref if whole else new_ref.at[matrix]
            copy = copy_ref if whole else copy_ref.at[matrix]
            at = matrix * tiles
            fresh_cols = []
            total = jnp.zeros((1, SEQ), WIDE)
            for tile, place in tiles_of(columns):
                row = plain_at + at + tile
                plain = flat_ref[row : row + 1] * (1.0 / all_rows) + EPS_STAT
                held = cols_ref[matrix : matrix + 1, place : place + SEQ]
                piece = BETA * held + (1.0 - BETA) * plain
                cols_new_ref[matrix : matrix + 1, place : place + SEQ] = piece
                row = scaled_at + at + tile
                total = total + flat_ref[row : row + 1] / piece
                fresh_cols.append(piece)
            row = FLAT_ROW_SUMS + first + matrix
            row_mean = flat_ref[row : row + 1] * (1.0 / all_rows)
            row = FLAT_WEIGHTS + first + matrix
            spread = jnp.sqrt(flat_ref[row : row + 1] * (1.0 / entries) + EPS_NORM)
            total = jnp.sum(total, axis=1, keepdims=True)
            mean_square = row_mean * total * (1.0 / entries)
            factor = RATE * spread / jnp.maximum(1.0, jnp.sqrt(mean_square) / CLIP)
            rows_scale = lax.rsqrt(rows_ref[matrix])
            for tile, place in tiles_of(columns):
                cols_scale = lax.rsqrt(fresh_cols[tile] / row_mean) * factor
                step = grad[:, place : place + SEQ] * rows_scale * cols_scale
                value = old[:, place : place + SEQ] - step
                new[:, place : place + SEQ] = value
                copy[:, place : place + SEQ] = value.astype(LOW)

    lane_low = lax.broadcasted_iota(jnp.int32, (1, SEQ), 1) < HD
    for start, rows, width, lanes in (
        (0, 12, D, None),
        (12, 12, D, None),
        (24, 1, HD, lane_low),
        (24, 1, HD, jnp.logical_not(lane_low)),
        (25, 1, H, None),
        (26, 288, D * H, None),
    ):
        param = small_ref[start : start + rows]
        grad = flat_ref[FLAT_SMALL + start : FLAT_SMALL + start + rows]
        fresh = BETA * moments_ref[start : start + rows] + (1.0 - BETA) * (grad * grad + EPS_STAT)
        update = grad * lax.rsqrt(fresh)
        if lanes is not None:
            update = jnp.where(lanes, update, 0.0)
        inside = param if lanes is None else jnp.where(lanes, param, 0.0)
        clip_ratio = jnp.sqrt(square_total(update) * (1.0 / width)) / CLIP
        spread = jnp.sqrt(square_total(inside) * (1.0 / width) + EPS_NORM)
        value = param - RATE * spread * (update / jnp.maximum(1.0, clip_ratio))
        if lanes is None:
            small_new_ref[start : start + rows] = value
        elif width == HD:
            held = small_new_ref[start : start + rows]
            small_new_ref[start : start + rows] = jnp.where(lanes, value, held)
        moments_new_ref[start : start + rows] = fresh


def finish(flat, grads, weights, rows, cols, small, moments):
    return pl.pallas_call(
        finish_kernel,
        in_specs=[pl.BlockSpec(memory_space=pltpu.VMEM)]
        + [pl.BlockSpec(memory_space=pltpu.HBM)] * 9
        + [pl.BlockSpec(memory_space=pltpu.VMEM)] * 3
        + [pl.BlockSpec(memory_space=pltpu.HBM)] * 2,
        scratch_shapes=[
            pltpu.VMEM(value.shape, WIDE)
            for value in (*grads, *weights, *rows, small, moments)
        ]
        + [pltpu.SemaphoreType.DMA((11,))],
        out_shape=[
            jax.ShapeDtypeStruct((5, 12, D), WIDE),
            jax.ShapeDtypeStruct((2, 12, FF), WIDE),
            jax.ShapeDtypeStruct((32, D), WIDE),
            jax.ShapeDtypeStruct((5, 12, D), LOW),
            jax.ShapeDtypeStruct((2, 12, FF), LOW),
            jax.ShapeDtypeStruct((32, D), LOW),
            jax.ShapeDtypeStruct((5, D), WIDE),
            jax.ShapeDtypeStruct((2, FF), WIDE),
            jax.ShapeDtypeStruct((1, D), WIDE),
            jax.ShapeDtypeStruct((314, SEQ), WIDE),
            jax.ShapeDtypeStruct((314, SEQ), WIDE),
        ],
        compiler_params=pltpu.CompilerParams(vmem_limit_bytes=40 * 1024 * 1024),
        name="finish",
    )(
        flat,
        *[far(value) for value in (*grads, *weights, *rows)],
        *cols,
        far(small),
        far(moments),
    )


def small_rows(vector, fill):
    bias = vector[2 * D + 2 * HD : 2 * D + 2 * HD + H]
    bias = jnp.concatenate([bias, jnp.full((SEQ - H,), fill, WIDE)])
    return jnp.concatenate(
        [
            vector[: 2 * D].reshape(24, SEQ),
            vector[2 * D : 2 * D + 2 * HD].reshape(1, SEQ),
            bias.reshape(1, SEQ),
            vector[2 * D + 2 * HD + H :].reshape(288, SEQ),
        ]
    )


def small_vector(rows):
    return jnp.concatenate(
        [rows[:25].reshape(-1), rows[25, :H], rows[26:].reshape(-1)]
    )


def spread_sum(flat):
    pieces = flat.reshape(DEVICES, -1, SEQ)
    return jnp.sum(lax.all_to_all(pieces, ALL, 0, 0, tiled=True), axis=0)


def spread_back(mine):
    whole = jnp.broadcast_to(mine[None], (DEVICES, *mine.shape))
    return lax.all_to_all(whole, ALL, 0, 0, tiled=True).reshape(-1, SEQ)


def column_order():
    source = lax.broadcasted_iota(jnp.int32, (1024, 1024), 0)
    target = lax.broadcasted_iota(jnp.int32, (1024, 1024), 1)
    lane = source % 128
    return (target == (lane // 32) * 256 + (source // 128) * 32 + lane % 32).astype(LOW)


def shards(
    tokens,
    cotangent,
    lengths,
    attn_weights,
    attn_rows,
    attn_cols,
    ffn_weights,
    ffn_rows,
    ffn_cols,
    down_weight,
    down_rows,
    down_cols,
    small_params,
    small_moments,
):
    core = lax.axis_index("c")
    deep = lax.axis_index("z")
    inputs = tokens.astype(WIDE)
    slot_ids = jnp.arange(SEQ, dtype=jnp.int32)
    valid_rows = slot_ids < lengths[0]
    gain_one, gain_two, query_gain, key_gain, forget_bias, forget_weight = split_small(small_params)

    device = ((lax.axis_index("x") * 4 + lax.axis_index("y")) * 4 + deep) * 2 + core
    forget_rows = lax.dynamic_slice_in_dim(forget_weight, device * 12, 12, axis=0)
    forget_rows = jnp.pad(forget_rows, ((0, 0), (0, SEQ - H)))
    attn_low = pack(lengths.astype(WIDE), attn_weights, forget_rows)
    attn_low = lax.all_to_all(attn_low, ZC, 0, 0, tiled=True)
    lengths_group = attn_low[:, 0, RAW - 1].astype(WIDE)
    attn_low = attn_low.reshape(96, RAW)
    attn_full = lax.all_gather(attn_low, XY, axis=0, tiled=True)
    order = column_order()
    pair_low = ffn_weights.astype(LOW).reshape(24, 4, 1024).transpose(1, 0, 2).reshape(96, 1024)
    pair_low = dot_right_t(pair_low, order).astype(LOW).reshape(4, 2, 12, GROUP, 128)
    pair_low = pair_low.transpose(3, 2, 1, 0, 4).reshape(GROUP, 12, 2 * FF_PART)
    pair_low = lax.all_to_all(pair_low, ZC, 0, 0, tiled=True).reshape(96, 2 * FF_PART)
    down_low = jnp.concatenate(
        [down_weight[:, at : at + 512].astype(LOW) for at in (0, 512, 1024)], axis=0
    )
    seed_grad = cotangent.astype(WIDE) * valid_rows[:, None].astype(WIDE)
    seed_grad, pair_low, down_low = fence(seed_grad, pair_low, down_low)
    seed_low = lax.all_gather(seed_grad.astype(LOW), ZC, axis=0, tiled=True)
    ffn_full = lax.all_gather(
        jnp.concatenate([pair_low, down_low], axis=1), XY, axis=0, tiled=True
    )

    inverse_one = inverse_rms(inputs)
    normed_one = inputs * inverse_one
    attn_low, attn_weights, ffn_weights, down_weight, small_params = fence(
        attn_low, attn_weights, ffn_weights, down_weight, small_params
    )
    tokens_group = gather_group(tokens)[0]
    inputs_group = tokens_group.astype(WIDE)
    inverse_group = inverse_rms(inputs_group)
    hidden_one = (inputs_group * inverse_group * gain_one).astype(LOW)
    place = 2 * deep + core

    lengths_group = jnp.broadcast_to(lengths_group[:, None, None], (GROUP, 1, SEQ))
    forget_low = lax.dynamic_slice_in_dim(forget_weight, place * OWN_HEADS, OWN_HEADS, axis=1)
    forget_low = forget_low.astype(LOW)
    bias_mine = lax.dynamic_slice_in_dim(forget_bias, place * OWN_HEADS, OWN_HEADS, axis=0)
    bias_tile = jnp.pad(bias_mine[None], ((0, 7), (HD, HD - OWN_HEADS)))
    exact = {"precision": lax.Precision.HIGHEST, "preferred_element_type": WIDE}
    slots = lax.broadcasted_iota(jnp.int32, (SEQ, SEQ), 0)
    later = (slots >= lax.broadcasted_iota(jnp.int32, (SEQ, SEQ), 1)).astype(WIDE)
    gains = jnp.concatenate([query_gain, key_gain])[None]
    gains = jnp.pad(gains, ((0, 7), (0, 0)))
    (
        attn_full,
        hidden_one,
        tokens_group,
        inverse_group,
        lengths_group,
        forget_low,
        bias_tile,
        gains,
        order,
    ) = fence(
        attn_full,
        hidden_one,
        tokens_group,
        inverse_group,
        lengths_group,
        forget_low,
        bias_tile,
        gains,
        order,
    )
    proj_full = attn_full[:, :OWN]
    raw, attn_full = fence(dot_plain(hidden_one, attn_full), attn_full)
    out_rows = attn_full[:, OWN : OWN + 3 * HD].reshape(GROUP, 3 * HD, 3 * HD)
    out_rows = lax.all_to_all(out_rows, ZC, 0, 0, tiled=True)
    gated_out, attended, prob = attend(raw, bias_tile, lengths_group, gains)
    out_rows = move_rows(spread_rows_kernel, out_rows, (WIDE_HEADS, D))
    mixed_part = dot_plain(gated_out, out_rows).astype(LOW).reshape(4, 2, SEQ, D)
    mixed_part = group_reduce_start(mixed_part, core, deep)
    half_one, half_two = fence(*far_halves(mixed_part))
    near_one, near_two, *held = fence(
        *near_blocks(mixed_part, (half_one, half_two)),
        small_params,
        small_moments,
        attn_weights,
        ffn_weights,
        down_weight,
        attn_rows,
        ffn_rows,
        down_rows,
    )
    small_params, small_moments, attn_weights, ffn_weights, down_weight = held[:5]
    attn_rows, ffn_rows, down_rows = held[5:]
    param_rows = small_rows(small_params, 0.0)
    moment_rows = small_rows(small_moments, 1.0)
    old_rows = (attn_rows[:, :, None], ffn_rows[:, :, None], down_rows[None, :, None])
    old_cols = (attn_cols, ffn_cols, down_cols[None])
    weight_sums = jnp.concatenate(
        [square_sum(attn_weights), square_sum(ffn_weights), square_sum(down_weight[None])]
    )
    mixed_sum = inputs + mixed_part[0] + near_one.astype(WIDE) + near_two.astype(WIDE)
    inverse_two = inverse_rms(mixed_sum)
    normed_two = mixed_sum * inverse_two
    hidden_two, ffn_full, seed_low, param_rows, moment_rows, old_rows, weight_sums = gather_group(
        (normed_two * gain_two).astype(LOW),
        ffn_full,
        seed_low,
        param_rows,
        moment_rows,
        old_rows,
        weight_sums,
    )
    pair_full = ffn_full[:, : 2 * FF_PART]
    down_full = ffn_full[:, 2 * FF_PART :].reshape(PLANE, 3, 32, 512)
    down_full = jnp.concatenate(
        [down_full[:, part].reshape(FF_PART, 512) for part in range(3)], axis=1
    )

    gate_full = pair_full[:, :FF_PART]
    up_full = pair_full[:, FF_PART:]
    gate_part = dot_plain(hidden_two, gate_full)
    up_part = dot_plain(hidden_two, up_full)
    gate_sig = lax.logistic(gate_part)
    activated = (gate_part * gate_sig * up_part).astype(LOW)
    activated_grad = dot_right_t(seed_low, down_full)
    silu_grad = activated_grad * up_part
    gate_part_grad = silu_grad * gate_sig + silu_grad * gate_part * gate_sig * (1.0 - gate_sig)
    gate_part_grad = gate_part_grad.astype(LOW)
    up_part_grad = (activated_grad * (gate_part * gate_sig)).astype(LOW)
    token_part = dot_right_t(gate_part_grad, gate_full) + dot_right_t(up_part_grad, up_full)
    token_part = token_part.astype(LOW).reshape(4, 2, SEQ, D)
    token_part, hidden_two, gate_part_grad, up_part_grad, activated, seed_low, down_full = fence(
        token_part, hidden_two, gate_part_grad, up_part_grad, activated, seed_low, down_full
    )
    token_got, gate_terms, hidden_two, up_part_grad, activated, seed_low = fence(
        swap_core(lax.dynamic_index_in_dim(token_part, 1 - core, 1, keepdims=False)),
        dot_left_t(hidden_two, gate_part_grad).astype(LOW),
        hidden_two,
        up_part_grad,
        activated,
        seed_low,
    )
    token_part = lax.dynamic_index_in_dim(token_part, core, 1, keepdims=False)
    token_part = token_part.astype(WIDE) + token_got.astype(WIDE)
    token_part, hidden_two, up_part_grad = fence(token_part, hidden_two, up_part_grad)
    token_part = [
        lax.dynamic_index_in_dim(token_part, (deep + step) % 4, 0, keepdims=False)
        for step in (0, 3, 1, 2)
    ]
    half_one, half_two, up_terms, down_terms, activated = fence(
        *far_halves(token_part),
        dot_left_t(hidden_two, up_part_grad).astype(LOW),
        dot_left_t(activated, seed_low).astype(LOW),
        activated,
    )
    down_terms = down_terms.reshape(PLANE, 32, D)
    ffn_terms = jnp.concatenate(
        [
            gate_terms.reshape(PLANE, 96, FF_PART),
            up_terms.reshape(PLANE, 96, FF_PART),
            down_terms[:, :, :512],
            down_terms[:, :, 512:1024],
            down_terms[:, :, 1024:],
        ],
        axis=1,
    )
    out_part = dot_plain(activated, down_full).astype(LOW).reshape(GROUP, SEQ, D)
    near_one, near_two, ffn_terms, out_part = fence(
        *near_blocks(token_part, (half_one, half_two)), ffn_terms, out_part
    )
    ffn_got = lax.all_to_all(ffn_terms, XY, 0, 0, tiled=True)
    hidden_two_grad = token_part[0] + near_one.astype(WIDE) + near_two.astype(WIDE)

    gain_two_grad = jnp.sum(normed_two * hidden_two_grad, axis=0)
    mixed_grad = seed_grad + norm_back(normed_two, inverse_two, hidden_two_grad * gain_two)
    mixed_low, out_part = gather_group(mixed_grad.astype(LOW), out_part)
    gated_grad = dot_right_t(mixed_low, out_rows)
    out_terms = dot_left_t(gated_out, mixed_low)
    out_terms = move_rows(collect_rows_kernel, out_terms, (PLANE, 24, OWN))
    gated_grad, out_terms = fence(gated_grad, out_terms)
    raw_grad, forget_sums, gain_sums = attend_back(raw, gated_grad, attended, prob, gains)
    out_terms, raw_grad, forget_sums, gain_sums = fence(
        out_terms, raw_grad, forget_sums, gain_sums
    )
    terms = jnp.concatenate(
        [
            dot_left_t(hidden_one, raw_grad).astype(LOW).reshape(PLANE, 96, OWN),
            out_terms,
        ],
        axis=1,
    )
    forget_arg = raw[:, OWN + 3 * HD : OWN + 3 * HD + OWN_HEADS] + bias_mine
    log_forget_grad = jnp.einsum(
        "bhu,ut->bth",
        forget_sums[:, :OWN_HEADS],
        later,
        **exact,
    ).reshape(GROUP * SEQ, OWN_HEADS)
    forget_arg_grad = log_forget_grad * (1.0 - lax.logistic(forget_arg))
    forget_low_grad = forget_arg_grad.astype(LOW)
    head_ids = lax.broadcasted_iota(jnp.int32, (OWN_HEADS, H), 0) + OWN_HEADS * place
    own_heads = head_ids == lax.broadcasted_iota(jnp.int32, (OWN_HEADS, H), 1)
    forget_wide = dot_plain(forget_low_grad, own_heads.astype(LOW)).astype(LOW)
    forget_w_grad = dot_left_t(hidden_one, forget_wide).reshape(288, SEQ)
    terms, raw_grad, ffn_got, forget_low_grad, forget_arg_grad, forget_w_grad = fence(
        terms, raw_grad, ffn_got, forget_low_grad, forget_arg_grad, forget_w_grad
    )
    terms = lax.all_to_all(terms, XY, 0, 0, tiled=True)
    pair_sum = jnp.sum(ffn_got[:, :192].astype(WIDE), axis=0).astype(LOW)

    raw_grad, token_weights, pair_sum = fence(raw_grad, proj_full, pair_sum)
    pair_back = lax.all_gather(pair_sum, ZC, axis=0, tiled=False)
    raw_grad, forget_low_grad, pair_back, ffn_got = fence(
        raw_grad, forget_low_grad, pair_back, ffn_got
    )
    down_sum = jnp.sum(ffn_got[:, 192:].astype(WIDE), axis=0).astype(LOW)
    token_part = dot_right_t(raw_grad, token_weights) + dot_right_t(
        forget_low_grad, forget_low
    )
    normed_group = tokens_group.astype(WIDE) * inverse_group
    gain_one_grad = jnp.sum(normed_group * token_part, axis=0)
    token_part = token_part.astype(LOW).reshape(GROUP, SEQ, D)
    forget_bias_grad = jnp.sum(
        jnp.where(own_heads, jnp.sum(forget_arg_grad, axis=0)[:, None], 0.0), axis=0
    )
    out_part, down_sum = fence(out_part, down_sum)
    hidden_one_grad = lax.psum_scatter(token_part, ZC, scatter_dimension=0, tiled=False)
    pair_back = pair_back.reshape(GROUP, 2, GROUP, 12, FF_PART)
    pair_back = lax.dynamic_index_in_dim(pair_back, place, 2, keepdims=False)
    pair_back = pair_back.reshape(GROUP, 2, 12, 4, 128).transpose(3, 1, 2, 0, 4).reshape(96, 1024)
    pair_back = dot_plain(pair_back, order)
    out_sum = lax.psum_scatter(out_part, ZC, scatter_dimension=0, tiled=False)
    hidden_one_grad = hidden_one_grad.astype(WIDE)
    forget_bias_grad = jnp.pad(forget_bias_grad, (0, SEQ - H))
    small_grads = jnp.concatenate([gain_one_grad, gain_two_grad, gain_sums[0], forget_bias_grad])
    small_grads = small_grads.reshape(26, SEQ)
    terms, pair_back, small_grads, forget_w_grad = fence(
        terms, pair_back, small_grads, forget_w_grad
    )
    attn_part = jnp.sum(terms.astype(WIDE), axis=0)
    out_part = jnp.concatenate([attn_part[96:108], attn_part[108:]], axis=1)
    out_part = lax.ppermute(
        out_part,
        ALL,
        [(GROUP * row + col, PLANE * col + row) for row in range(PLANE) for col in range(GROUP)],
    )
    attn_part = attn_part[:96].reshape(GROUP, 12, OWN)
    attn_part = lax.all_to_all(attn_part, ZC, 0, 0, tiled=True)
    *measured, flat = measure(
        weight_sums, attn_part, out_part, pair_back, down_sum, *old_rows, small_grads, forget_w_grad
    )
    grads, rows_new = measured[:3], measured[3:]
    block_out = (mixed_sum + out_sum.astype(WIDE)).astype(LOW)
    mine, block_out = fence(spread_sum(flat), block_out)
    flat = spread_back(mine)
    input_grad = mixed_grad + norm_back(normed_one, inverse_one, hidden_one_grad * gain_one)
    fresh = finish(
        flat,
        grads,
        (attn_weights, ffn_weights, down_weight),
        rows_new,
        old_cols,
        param_rows,
        moment_rows,
    )
    attn_new, ffn_new, down_new, attn_copy, ffn_copy, down_copy = fresh[:6]
    attn_cols_new, ffn_cols_new, down_cols_new, small_new, moments_new = fresh[6:]
    return (
        block_out,
        input_grad,
        grads[0],
        attn_new,
        attn_copy,
        rows_new[0].reshape(5, 12),
        attn_cols_new,
        grads[1],
        ffn_new,
        ffn_copy,
        rows_new[1].reshape(2, 12),
        ffn_cols_new,
        grads[2],
        down_new,
        down_copy,
        rows_new[2].reshape(32),
        down_cols_new.reshape(D),
        small_vector(flat[FLAT_SMALL : FLAT_SMALL + 314]),
        small_vector(small_new),
        small_vector(moments_new),
    )


def solution(mesh):
    chips = Mesh(mesh.devices.reshape(4, 4, 4, 2), ALL)
    rows_first = P(ALL, None)
    rows_second = P(None, ALL, None)
    stat_rows = P(None, ALL)
    flat = P(ALL)
    whole = P()
    return jax.shard_map(
        shards,
        mesh=chips,
        in_specs=(
            rows_first,
            rows_first,
            flat,
            rows_second,
            stat_rows,
            whole,
            rows_second,
            stat_rows,
            whole,
            rows_first,
            flat,
            whole,
            whole,
            whole,
        ),
        out_specs=(
            rows_first,
            rows_first,
            rows_second,
            rows_second,
            rows_second,
            stat_rows,
            whole,
            rows_second,
            rows_second,
            rows_second,
            stat_rows,
            whole,
            rows_first,
            rows_first,
            rows_first,
            flat,
            whole,
            whole,
            whole,
            whole,
        ),
        check_vma=False,
    )
```

```python
import jax
import jax.numpy as jnp
from jax import lax
from jax.experimental import pallas as pl
from jax.experimental.pallas import tpu as pltpu
from jax.sharding import Mesh
from jax.sharding import PartitionSpec as P

D = 1536
H = 24
HD = 64
FF = 4096
SEQ = 128
HALF = D // 2
HEADS = H // 2
GROUP = 8
PLANE = 16
CHIPS = 64
DEVICES = 128
FF_PART = FF // GROUP
OWN_HEADS = H // GROUP
FLAT_ROWS = 640
FLAT_ROW_SUMS = 120
FLAT_SMALL = 280
FLAT_FORGET = 306
FLAT_WEIGHTS = 594
FLAT_END = 602
OWN = 4 * OWN_HEADS * HD
RAW = OWN + 2 * SEQ
WIDE_HEADS = OWN_HEADS * 2 * HD

BETA = 0.5
CLIP = 0.1
RATE = 3.0
EPS_NORM = 1e-06
EPS_STAT = 1e-30
NEG_FILL = -1e30
LOW = jnp.bfloat16
WIDE = jnp.float32

ALL = ("x", "y", "z", "c")
XYZ = ("x", "y", "z")
XY = ("x", "y")
ZC = ("z", "c")


def dot_plain(left_side, right_side):
    return jnp.dot(left_side, right_side, preferred_element_type=WIDE)


def dot_right_t(left_side, right_side):
    return lax.dot_general(
        left_side, right_side, (((1,), (1,)), ((), ())), preferred_element_type=WIDE
    )


def dot_left_t(left_side, right_side):
    return lax.dot_general(
        left_side, right_side, (((0,), (0,)), ((), ())), preferred_element_type=WIDE
    )


def inverse_rms(values):
    return lax.rsqrt(jnp.mean(values * values, axis=-1, keepdims=True) + EPS_NORM)


def norm_back(normed, inverse, grad_out):
    return inverse * (grad_out - normed * jnp.mean(grad_out * normed, axis=-1, keepdims=True))


def split_small(vector):
    widths = [D, D, HD, HD, H]
    pieces = []
    offset = 0
    for piece_width in widths:
        pieces.append(vector[offset : offset + piece_width])
        offset = offset + piece_width
    pieces.append(vector[offset:].reshape(D, H))
    return pieces


SMALL_WIDTHS = (D, D, HD, HD, H, D * H)


def square_sum(weight):
    return jnp.sum(weight * weight, axis=(1, 2))


def fence(*values):
    return lax.optimization_barrier(values)


def swap_core(value):
    return lax.ppermute(value, "c", [(0, 1), (1, 0)])


def reduce_core(part, core):
    keep = lax.dynamic_index_in_dim(part, core, 0, keepdims=False)
    send = lax.dynamic_index_in_dim(part, 1 - core, 0, keepdims=False)
    return keep + swap_core(send)


def hop(value, axis, step):
    return lax.ppermute(value, axis, [(i, (i + step) % 4) for i in range(4)])


def assemble_kernel(
    place_ref, own, near, far_one, far_two, other, near_other, far_other, whole_ref
):
    deep = place_ref[0]
    core = place_ref[1]
    rows = own.shape[0]
    half = rows // 2

    def put(step, side, start, value):
        at = lax.rem(deep + step, 4)
        whole_ref[at, side, start : start + value.shape[0], :] = value

    put(0, core, 0, own[...])
    put(0, 1 - core, 0, other[...])
    put(3, core, 0, near[:rows])
    put(1, core, 0, near[rows:])
    put(3, 1 - core, 0, near_other[:rows])
    put(1, 1 - core, 0, near_other[rows:])
    put(2, core, 0, far_one[...])
    put(2, core, half, far_two[...])
    put(2, 1 - core, 0, far_other[...])


def assemble(*pieces):
    place = jnp.stack([lax.axis_index("z"), lax.axis_index("c")]).astype(jnp.int32)
    rows, columns = pieces[0].shape
    whole = pl.pallas_call(
        assemble_kernel,
        in_specs=[pl.BlockSpec(memory_space=pltpu.SMEM)]
        + [pl.BlockSpec(memory_space=pltpu.VMEM)] * len(pieces),
        out_shape=jax.ShapeDtypeStruct((4, 2, rows, columns), pieces[0].dtype),
        compiler_params=pltpu.CompilerParams(vmem_limit_bytes=40 * 1024 * 1024),
        name="assemble",
    )(place, *pieces)
    return whole.reshape(GROUP * rows, columns)


def gather_group(value, *others):
    rows = value.shape[0] // 2
    before = hop(value, "z", 1)
    after = hop(value, "z", -1)
    other = swap_core(value)
    before, after, other = fence(before, after, other)
    near = jnp.concatenate([before, after])
    far_one = hop(before[:rows], "z", 1)
    far_two = hop(after[rows:], "z", -1)
    near_other = swap_core(near)
    far_one, far_two, near_other, *others = fence(far_one, far_two, near_other, *others)
    far_other = swap_core(jnp.concatenate([far_one, far_two]))
    whole = assemble(value, near, far_one, far_two, other, near_other, far_other)
    return (whole, *others)


def far_halves(part):
    rows = SEQ // 2
    far = part[3].astype(LOW)
    return (hop(far[:rows], "z", 1), hop(far[rows:], "z", -1))


def near_blocks(part, halves):
    rows = SEQ // 2
    to_after = jnp.concatenate([part[2][:rows] + halves[0].astype(WIDE), part[2][rows:]])
    to_before = jnp.concatenate([part[1][:rows], part[1][rows:] + halves[1].astype(WIDE)])
    return (hop(to_after.astype(LOW), "z", 1), hop(to_before.astype(LOW), "z", -1))


def group_reduce_start(part, core, deep):
    got = swap_core(lax.dynamic_index_in_dim(part, 1 - core, 1, keepdims=False))
    part = lax.dynamic_index_in_dim(part, core, 1, keepdims=False)
    part = part.astype(WIDE) + got.astype(WIDE)
    return [
        lax.dynamic_index_in_dim(part, (deep + step) % 4, 0, keepdims=False)
        for step in (0, 3, 1, 2)
    ]


def direct_sum(blocks, axis, dim):
    here = lax.axis_index(axis)
    total = lax.dynamic_index_in_dim(blocks, here, dim, keepdims=False).astype(WIDE)
    for step in (1, 2, 3):
        block = lax.dynamic_index_in_dim(blocks, (here + step) % 4, dim, keepdims=False)
        total = total + hop(block, axis, step).astype(WIDE)
    return total


def split_far(blocks, axis):
    far = lax.dynamic_index_in_dim(blocks, (lax.axis_index(axis) + 2) % 4, 0, keepdims=False)
    half = far.shape[0] // 2
    return (hop(far[:half], axis, 1), hop(far[half:], axis, -1))


def split_near(blocks, axis, halves):
    here = lax.axis_index(axis)
    after = lax.dynamic_index_in_dim(blocks, (here + 1) % 4, 0, keepdims=False)
    before = lax.dynamic_index_in_dim(blocks, (here + 3) % 4, 0, keepdims=False)
    half = after.shape[0] // 2
    to_after = jnp.concatenate([after[:half] + halves[0], after[half:]])
    to_before = jnp.concatenate([before[:half], before[half:] + halves[1]])
    return (hop(to_after, axis, 1), hop(to_before, axis, -1))


def split_sum(blocks, axis, near):
    own = lax.dynamic_index_in_dim(blocks, lax.axis_index(axis), 0, keepdims=False)
    return (own.astype(WIDE) + near[0].astype(WIDE) + near[1].astype(WIDE)).astype(LOW)


def direct_exchange(blocks, axis):
    here = lax.axis_index(axis)
    pieces = [lax.dynamic_index_in_dim(blocks, here, 0, keepdims=False)]
    for step in (1, 2, 3):
        block = lax.dynamic_index_in_dim(blocks, (here + step) % 4, 0, keepdims=False)
        pieces.append(hop(block, axis, step))
    return pieces


def head_stat(values, lane_low):
    low = jnp.sum(jnp.where(lane_low, values, 0.0), axis=-1, keepdims=True) * (1.0 / HD)
    high = jnp.sum(jnp.where(lane_low, 0.0, values), axis=-1, keepdims=True) * (1.0 / HD)
    return jnp.where(lane_low, low, high)


def head_normed(values, lane_low):
    inverse = lax.rsqrt(head_stat(values * values, lane_low) + EPS_NORM)
    return (values * inverse, inverse)


def far(value):
    return pltpu.with_memory_space_constraint(value, pltpu.HBM)


def attend_kernel(
    raw_ref, bias_ref, length_ref, gains_ref, gated_ref, attended_ref, prob_ref
):
    lane = lax.broadcasted_iota(jnp.int32, (SEQ, SEQ), 1)
    lane_low = lane < HD
    slot = lax.broadcasted_iota(jnp.int32, (SEQ, SEQ), 0)
    allowed = (lane <= slot) & (lane.astype(WIDE) < length_ref[0])
    forget = raw_ref[:, RAW - SEQ :] + bias_ref[0:1]
    mine = (lane >= HD) & (lane < HD + OWN_HEADS)
    log_forget = -jnp.log1p(jnp.exp(jnp.where(mine, -forget, 0.0)))
    cols = lax.dot_general(
        (lane <= slot).astype(WIDE),
        log_forget,
        (((1,), (0,)), ((), ())),
        precision=lax.Precision.HIGHEST,
        preferred_element_type=WIDE,
    )
    rows = cols.T
    for head in range(OWN_HEADS):
        at = 2 * head * SEQ
        normed, _ = head_normed(raw_ref[:, at : at + SEQ], lane_low)
        scaled = normed * gains_ref[0:1]
        query = jnp.where(lane_low, scaled, 0.0).astype(LOW)
        key = pltpu.roll(scaled, HD, 1).astype(LOW)
        value_gate = raw_ref[:, at + SEQ : at + 2 * SEQ]
        score = dot_right_t(query, key) * (HD**-0.5)
        score = score + cols[:, HD + head : HD + head + 1]
        score = score - rows[HD + head : HD + head + 1]
        score = jnp.where(allowed, score, NEG_FILL)
        weight = jnp.exp(score - jnp.max(score, axis=-1, keepdims=True))
        prob = weight / jnp.sum(weight, axis=-1, keepdims=True)
        prob_ref[0, head] = prob
        attended = dot_plain(prob.astype(LOW), value_gate.astype(LOW))
        gate = lax.logistic(pltpu.roll(value_gate, HD, 1))
        attended_ref[:, head * SEQ : (head + 1) * SEQ] = attended
        gated = jnp.where(lane_low, attended * gate, 0.0)
        gated_ref[:, head * SEQ : (head + 1) * SEQ] = gated.astype(LOW)


def attend(raw, bias, lengths, gains):
    return pl.pallas_call(
        attend_kernel,
        grid=(GROUP,),
        in_specs=[
            pl.BlockSpec((SEQ, RAW), lambda i: (i, 0)),
            pl.BlockSpec((8, SEQ), lambda i: (0, 0)),
            pl.BlockSpec((1, 1, SEQ), lambda i: (i, 0, 0)),
            pl.BlockSpec((8, SEQ), lambda i: (0, 0)),
        ],
        out_specs=[
            pl.BlockSpec((SEQ, WIDE_HEADS), lambda i: (i, 0)),
            pl.BlockSpec((SEQ, WIDE_HEADS), lambda i: (i, 0)),
            pl.BlockSpec((1, OWN_HEADS, SEQ, SEQ), lambda i: (i, 0, 0, 0)),
        ],
        out_shape=[
            jax.ShapeDtypeStruct((GROUP * SEQ, WIDE_HEADS), LOW),
            jax.ShapeDtypeStruct((GROUP * SEQ, WIDE_HEADS), WIDE),
            jax.ShapeDtypeStruct((GROUP, OWN_HEADS, SEQ, SEQ), WIDE),
        ],
        compiler_params=pltpu.CompilerParams(vmem_limit_bytes=40 * 1024 * 1024),
        cost_estimate=pl.CostEstimate(
            flops=24 * 4 * SEQ**3, bytes_accessed=6_000_000, transcendentals=24 * SEQ * SEQ
        ),
        name="attend",
    )(far(raw), bias, lengths, gains)


def attend_back_kernel(
    raw_ref, gated_grad_ref, attended_ref, prob_ref, gains_ref, grad_ref, forget_ref, gain_ref
):
    lane_low = lax.broadcasted_iota(jnp.int32, (SEQ, SEQ), 1) < HD
    ones = jnp.ones((8, SEQ), LOW)
    gains = gains_ref[0:1]
    forget_ref[...] = jnp.zeros_like(forget_ref)

    @pl.when(pl.program_id(0) == 0)
    def _():
        gain_ref[...] = jnp.zeros_like(gain_ref)

    for head in range(OWN_HEADS):
        at = 2 * head * SEQ
        normed, inverse = head_normed(raw_ref[:, at : at + SEQ], lane_low)
        swapped = pltpu.roll(normed * gains, HD, 1).astype(LOW)
        value_gate = raw_ref[:, at + SEQ : at + 2 * SEQ]
        gate = lax.logistic(pltpu.roll(value_gate, HD, 1))
        gated_grad = gated_grad_ref[:, head * SEQ : (head + 1) * SEQ]
        gated_grad = jnp.where(lane_low, gated_grad, 0.0)
        out_grad = (gated_grad * gate).astype(LOW)
        attended = attended_ref[:, head * SEQ : (head + 1) * SEQ]
        gate_grad = gated_grad * attended * gate * (1.0 - gate)
        prob = prob_ref[0, head]
        prob_grad = dot_right_t(out_grad, value_gate.astype(LOW))
        delta = jnp.sum(prob * prob_grad, axis=-1, keepdims=True)
        score_grad = (prob * (prob_grad - delta)).astype(LOW)
        value_grad = dot_left_t(prob.astype(LOW), out_grad)
        value_gate_grad = jnp.where(lane_low, value_grad, pltpu.roll(gate_grad, HD, 1))
        grad_ref[:, at + SEQ : at + 2 * SEQ] = value_gate_grad.astype(LOW)
        sums = dot_right_t(ones, score_grad) - dot_plain(ones, score_grad)
        forget_ref[0, head : head + 1] = sums[0:1]
        grad = jnp.where(
            lane_low, dot_plain(score_grad, swapped), dot_left_t(score_grad, swapped)
        ) * (HD**-0.5)
        product = grad * normed
        gain_ref[0:1] += jnp.sum(product, axis=0, keepdims=True)
        mean = head_stat(product * gains, lane_low)
        grad_ref[:, at : at + SEQ] = (inverse * (grad * gains - normed * mean)).astype(LOW)


def attend_back(raw, gated_grad, attended, prob, gains):
    return pl.pallas_call(
        attend_back_kernel,
        grid=(GROUP,),
        in_specs=[
            pl.BlockSpec((SEQ, RAW), lambda i: (i, 0)),
            pl.BlockSpec((SEQ, WIDE_HEADS), lambda i: (i, 0)),
            pl.BlockSpec((SEQ, WIDE_HEADS), lambda i: (i, 0)),
            pl.BlockSpec((1, OWN_HEADS, SEQ, SEQ), lambda i: (i, 0, 0, 0)),
            pl.BlockSpec((8, SEQ), lambda i: (0, 0)),
        ],
        out_specs=[
            pl.BlockSpec((SEQ, OWN), lambda i: (i, 0)),
            pl.BlockSpec((1, 8, SEQ), lambda i: (i, 0, 0)),
            pl.BlockSpec((8, SEQ), lambda i: (0, 0)),
        ],
        out_shape=[
            jax.ShapeDtypeStruct((GROUP * SEQ, OWN), LOW),
            jax.ShapeDtypeStruct((GROUP, 8, SEQ), WIDE),
            jax.ShapeDtypeStruct((8, SEQ), WIDE),
        ],
        compiler_params=pltpu.CompilerParams(vmem_limit_bytes=40 * 1024 * 1024),
        cost_estimate=pl.CostEstimate(
            flops=24 * 10 * SEQ**3, bytes_accessed=8_000_000, transcendentals=2 * SEQ * HALF
        ),
        name="attend_back",
    )(far(raw), far(gated_grad), far(attended), far(prob), gains)


def half_tile(ref, matrix, head):
    tile = ref[matrix, :, SEQ * (head // 2) : SEQ * (head // 2) + SEQ]
    return (tile, pltpu.roll(tile, HD, 1))[:: 1 if head % 2 == 0 else -1]


def pack_kernel(length_ref, weight_ref, forget_ref, packed_ref):
    lane = lax.broadcasted_iota(jnp.int32, (12, SEQ), 1)
    lane_low = lane < HD
    forget = forget_ref[...]
    length = jnp.where(lane == SEQ - 1, length_ref[0], 0.0)
    for place in range(GROUP):
        for slot in range(OWN_HEADS):
            head = OWN_HEADS * place + slot
            for pair in range(2):
                left, _ = half_tile(weight_ref, 2 * pair, head)
                _, right = half_tile(weight_ref, 2 * pair + 1, head)
                at = (2 * slot + pair) * SEQ
                tile = jnp.where(lane_low, left, right)
                packed_ref[place, :, at : at + SEQ] = tile.astype(LOW)
        first, _ = half_tile(weight_ref, 4, OWN_HEADS * place)
        _, second = half_tile(weight_ref, 4, OWN_HEADS * place + 1)
        third, _ = half_tile(weight_ref, 4, OWN_HEADS * place + 2)
        packed_ref[place, :, OWN : OWN + SEQ] = jnp.where(lane_low, first, second).astype(LOW)
        rest = pltpu.roll(forget, (HD - OWN_HEADS * place) % SEQ, 1)
        rest = jnp.where(lane < HD + OWN_HEADS, rest, length)
        packed_ref[place, :, OWN + SEQ :] = jnp.where(lane_low, third, rest).astype(LOW)


def pack(length, weights, forget):
    return pl.pallas_call(
        pack_kernel,
        in_specs=[
            pl.BlockSpec(memory_space=pltpu.SMEM),
            pl.BlockSpec(memory_space=pltpu.VMEM),
            pl.BlockSpec(memory_space=pltpu.VMEM),
        ],
        out_shape=jax.ShapeDtypeStruct((GROUP, 12, RAW), LOW),
        compiler_params=pltpu.CompilerParams(vmem_limit_bytes=40 * 1024 * 1024),
        name="pack",
    )(length, weights, forget)


def spread_rows_kernel(blocks_ref, rows_ref):
    for head in range(OWN_HEADS):
        at = head * SEQ
        for pair in range(GROUP // 2):
            left = blocks_ref[2 * pair, head * HD : head * HD + HD, :]
            right = blocks_ref[2 * pair + 1, head * HD : head * HD + HD, :]
            both = jnp.concatenate([left, right], axis=1)
            rows_ref[at : at + HD, 384 * pair : 384 * pair + 384] = both
        rows_ref[at + HD : at + SEQ, :] = jnp.zeros((HD, D), LOW)


def collect_rows_kernel(rows_ref, blocks_ref):
    pieces = [rows_ref[head * SEQ : head * SEQ + HD] for head in range(OWN_HEADS)]
    rows = jnp.concatenate(pieces, axis=0).astype(LOW)
    for block in range(PLANE):
        mine = rows[12 * block : 12 * block + 12]
        blocks_ref[block, :12, :] = mine[:, :OWN]
        blocks_ref[block, 12:, :] = mine[:, OWN:]


def move_rows(kernel, value, shape):
    return pl.pallas_call(
        kernel,
        out_shape=jax.ShapeDtypeStruct(shape, LOW),
        compiler_params=pltpu.CompilerParams(vmem_limit_bytes=40 * 1024 * 1024),
        name="move_rows",
    )(value)


def unpack_kernel(packed_ref, grad_ref):
    lane_low = lax.broadcasted_iota(jnp.int32, (12, SEQ), 1) < HD

    def tile_of(place, at):
        tile = packed_ref[place, :, at : at + SEQ]
        return (tile, pltpu.roll(tile, HD, 1))

    for left in range(0, H, 2):
        places = [(head // OWN_HEADS, head % OWN_HEADS) for head in (left, left + 1)]
        at = SEQ * (left // 2)
        for pair in range(2):
            tiles = [tile_of(place, (2 * slot + pair) * SEQ) for place, slot in places]
            grad_ref[2 * pair, :, at : at + SEQ] = jnp.where(lane_low, tiles[0][0], tiles[1][1])
            grad_ref[2 * pair + 1, :, at : at + SEQ] = jnp.where(lane_low, tiles[0][1], tiles[1][0])


def tiles_of(columns):
    return [(tile, tile * SEQ) for tile in range(columns // SEQ)]


def row_stats(grad_ref, rows_old, columns):
    total = jnp.zeros((grad_ref.shape[0], SEQ), WIDE)
    for _, at in tiles_of(columns):
        part = grad_ref[:, at : at + SEQ]
        total = total + part * part
    mean = jnp.sum(total, axis=1, keepdims=True) * (1.0 / columns)
    return BETA * rows_old + (1.0 - BETA) * (mean + EPS_STAT)


def column_stats(grad_ref, rows_new, columns, flat_ref, plain_at, scaled_at):
    for tile, at in tiles_of(columns):
        part = grad_ref[:, at : at + SEQ]
        part = part * part
        plain = jnp.sum(part, axis=0, keepdims=True)
        scaled = jnp.sum(part / rows_new, axis=0, keepdims=True)
        flat_ref[plain_at + tile : plain_at + tile + 1] = plain
        flat_ref[scaled_at + tile : scaled_at + tile + 1] = scaled


def measure_kernel(
    sums_ref,
    packed_ref,
    out_ref,
    pair_ref,
    ffn_ref,
    attn_rows_ref,
    ffn_rows_ref,
    down_rows_ref,
    small_ref,
    forget_ref,
    attn_grad_ref,
    ffn_grad_ref,
    down_grad_ref,
    attn_rows_new_ref,
    ffn_rows_new_ref,
    down_rows_new_ref,
    flat_ref,
):
    unpack_kernel(packed_ref, attn_grad_ref)
    attn_grad_ref[4] = out_ref[...]
    for block in range(4):
        for matrix in range(2):
            row = 24 * block + 12 * matrix
            ffn_grad_ref[matrix, :, 1024 * block : 1024 * block + 1024] = pair_ref[row : row + 12]
    for part in range(3):
        rows = ffn_ref[192 + 32 * part : 224 + 32 * part]
        down_grad_ref[:, 512 * part : 512 * part + 512] = rows.astype(WIDE)
    flat_ref[FLAT_END:] = jnp.zeros((FLAT_ROWS - FLAT_END, SEQ), WIDE)
    for matrix in range(8):
        value = jnp.full((1, SEQ), sums_ref[matrix], WIDE)
        flat_ref[FLAT_WEIGHTS + matrix : FLAT_WEIGHTS + matrix + 1] = value
    flat_ref[FLAT_SMALL : FLAT_SMALL + 26] = small_ref[...]
    flat_ref[FLAT_FORGET : FLAT_FORGET + 288] = forget_ref[...]
    groups = (
        (attn_grad_ref, attn_rows_ref, attn_rows_new_ref, 5, D, 0, 60, 0),
        (ffn_grad_ref, ffn_rows_ref, ffn_rows_new_ref, 2, FF, 128, 192, 5),
        (down_grad_ref, down_rows_ref, down_rows_new_ref, 1, D, 256, 268, 7),
    )
    for grad_ref, old_ref, new_ref, count, columns, plain_at, scaled_at, first in groups:
        for matrix in range(count):
            mine = grad_ref if first == 7 else grad_ref.at[matrix]
            rows_new = row_stats(mine, old_ref[matrix], columns)
            new_ref[matrix] = rows_new
            at = matrix * (columns // SEQ)
            column_stats(mine, rows_new, columns, flat_ref, plain_at + at, scaled_at + at)
            value = jnp.broadcast_to(jnp.sum(rows_new, axis=0, keepdims=True), (1, SEQ))
            flat_ref[FLAT_ROW_SUMS + first + matrix : FLAT_ROW_SUMS + first + matrix + 1] = value


def measure(sums, packed, out, pair, ffn, attn_rows, ffn_rows, down_rows, small, forget):
    return pl.pallas_call(
        measure_kernel,
        in_specs=[pl.BlockSpec(memory_space=pltpu.SMEM)]
        + [pl.BlockSpec(memory_space=pltpu.VMEM)] * 9,
        out_shape=[
            jax.ShapeDtypeStruct((5, 12, D), WIDE),
            jax.ShapeDtypeStruct((2, 12, FF), WIDE),
            jax.ShapeDtypeStruct((32, D), WIDE),
            jax.ShapeDtypeStruct((5, 12, 1), WIDE),
            jax.ShapeDtypeStruct((2, 12, 1), WIDE),
            jax.ShapeDtypeStruct((1, 32, 1), WIDE),
            jax.ShapeDtypeStruct((FLAT_ROWS, SEQ), WIDE),
        ],
        compiler_params=pltpu.CompilerParams(vmem_limit_bytes=40 * 1024 * 1024),
        name="measure",
    )(sums, packed, out, pair, ffn, attn_rows, ffn_rows, down_rows, small, forget)


def square_total(values):
    return jnp.sum(jnp.sum(values * values, axis=0, keepdims=True), axis=1, keepdims=True)


def finish_kernel(
    flat_ref,
    attn_grad_ref,
    ffn_grad_ref,
    down_grad_ref,
    attn_ref,
    ffn_ref,
    down_ref,
    attn_rows_ref,
    ffn_rows_ref,
    down_rows_ref,
    attn_cols_ref,
    ffn_cols_ref,
    down_cols_ref,
    small_ref,
    moments_ref,
    attn_new_ref,
    ffn_new_ref,
    down_new_ref,
    attn_copy_ref,
    ffn_copy_ref,
    down_copy_ref,
    attn_cols_new_ref,
    ffn_cols_new_ref,
    down_cols_new_ref,
    small_new_ref,
    moments_new_ref,
    *scratch,
):
    *held, arrivals = scratch
    sources = (
        (attn_grad_ref, ffn_grad_ref, down_grad_ref, attn_ref, ffn_ref, down_ref)
        + (attn_rows_ref, ffn_rows_ref, down_rows_ref, small_ref, moments_ref)
    )
    copies = [
        pltpu.make_async_copy(source, target, arrivals.at[place])
        for place, (source, target) in enumerate(zip(sources, held))
    ]
    for copy in copies:
        copy.start()
    for copy in copies:
        copy.wait()
    attn_grad_ref, ffn_grad_ref, down_grad_ref, attn_ref, ffn_ref, down_ref = held[:6]
    attn_rows_ref, ffn_rows_ref, down_rows_ref, small_ref, moments_ref = held[6:]
    groups = (
        (attn_grad_ref, attn_ref, attn_rows_ref, attn_cols_ref)
        + (attn_new_ref, attn_copy_ref, attn_cols_new_ref, 5, D, D, 0, 60, 0),
        (ffn_grad_ref, ffn_ref, ffn_rows_ref, ffn_cols_ref)
        + (ffn_new_ref, ffn_copy_ref, ffn_cols_new_ref, 2, D, FF, 128, 192, 5),
        (down_grad_ref, down_ref, down_rows_ref, down_cols_ref)
        + (down_new_ref, down_copy_ref, down_cols_new_ref, 1, FF, D, 256, 268, 7),
    )
    for (
        grad_ref,
        old_ref,
        rows_ref,
        cols_ref,
        new_ref,
        copy_ref,
        cols_new_ref,
        count,
        all_rows,
        columns,
        plain_at,
        scaled_at,
        first,
    ) in groups:
        entries = all_rows * columns
        tiles = columns // SEQ
        for matrix in range(count):
            whole = first == 7
            grad = grad_ref if whole else grad_ref.at[matrix]
            old = old_ref if whole else old_ref.at[matrix]
            new = new_ref if whole else new_ref.at[matrix]
            copy = copy_ref if whole else copy_ref.at[matrix]
            at = matrix * tiles
            fresh_cols = []
            total = jnp.zeros((1, SEQ), WIDE)
            for tile, place in tiles_of(columns):
                row = plain_at + at + tile
                plain = flat_ref[row : row + 1] * (1.0 / all_rows) + EPS_STAT
                held = cols_ref[matrix : matrix + 1, place : place + SEQ]
                piece = BETA * held + (1.0 - BETA) * plain
                cols_new_ref[matrix : matrix + 1, place : place + SEQ] = piece
                row = scaled_at + at + tile
                total = total + flat_ref[row : row + 1] / piece
                fresh_cols.append(piece)
            row = FLAT_ROW_SUMS + first + matrix
            row_mean = flat_ref[row : row + 1] * (1.0 / all_rows)
            row = FLAT_WEIGHTS + first + matrix
            spread = jnp.sqrt(flat_ref[row : row + 1] * (1.0 / entries) + EPS_NORM)
            total = jnp.sum(total, axis=1, keepdims=True)
            mean_square = row_mean * total * (1.0 / entries)
            factor = RATE * spread / jnp.maximum(1.0, jnp.sqrt(mean_square) / CLIP)
            rows_scale = lax.rsqrt(rows_ref[matrix])
            for tile, place in tiles_of(columns):
                cols_scale = lax.rsqrt(fresh_cols[tile] / row_mean) * factor
                step = grad[:, place : place + SEQ] * rows_scale * cols_scale
                value = old[:, place : place + SEQ] - step
                new[:, place : place + SEQ] = value
                copy[:, place : place + SEQ] = value.astype(LOW)

    lane_low = lax.broadcasted_iota(jnp.int32, (1, SEQ), 1) < HD
    for start, rows, width, lanes in (
        (0, 12, D, None),
        (12, 12, D, None),
        (24, 1, HD, lane_low),
        (24, 1, HD, jnp.logical_not(lane_low)),
        (25, 1, H, None),
        (26, 288, D * H, None),
    ):
        param = small_ref[start : start + rows]
        grad = flat_ref[FLAT_SMALL + start : FLAT_SMALL + start + rows]
        fresh = BETA * moments_ref[start : start + rows] + (1.0 - BETA) * (grad * grad + EPS_STAT)
        update = grad * lax.rsqrt(fresh)
        if lanes is not None:
            update = jnp.where(lanes, update, 0.0)
        inside = param if lanes is None else jnp.where(lanes, param, 0.0)
        clip_ratio = jnp.sqrt(square_total(update) * (1.0 / width)) / CLIP
        spread = jnp.sqrt(square_total(inside) * (1.0 / width) + EPS_NORM)
        value = param - RATE * spread * (update / jnp.maximum(1.0, clip_ratio))
        if lanes is None:
            small_new_ref[start : start + rows] = value
        elif width == HD:
            held = small_new_ref[start : start + rows]
            small_new_ref[start : start + rows] = jnp.where(lanes, value, held)
        moments_new_ref[start : start + rows] = fresh


def finish(flat, grads, weights, rows, cols, small, moments):
    return pl.pallas_call(
        finish_kernel,
        in_specs=[pl.BlockSpec(memory_space=pltpu.VMEM)]
        + [pl.BlockSpec(memory_space=pltpu.HBM)] * 9
        + [pl.BlockSpec(memory_space=pltpu.VMEM)] * 3
        + [pl.BlockSpec(memory_space=pltpu.HBM)] * 2,
        scratch_shapes=[
            pltpu.VMEM(value.shape, WIDE)
            for value in (*grads, *weights, *rows, small, moments)
        ]
        + [pltpu.SemaphoreType.DMA((11,))],
        out_shape=[
            jax.ShapeDtypeStruct((5, 12, D), WIDE),
            jax.ShapeDtypeStruct((2, 12, FF), WIDE),
            jax.ShapeDtypeStruct((32, D), WIDE),
            jax.ShapeDtypeStruct((5, 12, D), LOW),
            jax.ShapeDtypeStruct((2, 12, FF), LOW),
            jax.ShapeDtypeStruct((32, D), LOW),
            jax.ShapeDtypeStruct((5, D), WIDE),
            jax.ShapeDtypeStruct((2, FF), WIDE),
            jax.ShapeDtypeStruct((1, D), WIDE),
            jax.ShapeDtypeStruct((314, SEQ), WIDE),
            jax.ShapeDtypeStruct((314, SEQ), WIDE),
        ],
        compiler_params=pltpu.CompilerParams(vmem_limit_bytes=40 * 1024 * 1024),
        name="finish",
    )(
        flat,
        *[far(value) for value in (*grads, *weights, *rows)],
        *cols,
        far(small),
        far(moments),
    )


def small_rows(vector, fill):
    bias = vector[2 * D + 2 * HD : 2 * D + 2 * HD + H]
    bias = jnp.concatenate([bias, jnp.full((SEQ - H,), fill, WIDE)])
    return jnp.concatenate(
        [
            vector[: 2 * D].reshape(24, SEQ),
            vector[2 * D : 2 * D + 2 * HD].reshape(1, SEQ),
            bias.reshape(1, SEQ),
            vector[2 * D + 2 * HD + H :].reshape(288, SEQ),
        ]
    )


def small_vector(rows):
    return jnp.concatenate(
        [rows[:25].reshape(-1), rows[25, :H], rows[26:].reshape(-1)]
    )


def spread_sum(flat):
    pieces = flat.reshape(DEVICES, -1, SEQ)
    return jnp.sum(lax.all_to_all(pieces, ALL, 0, 0, tiled=True), axis=0)


def spread_back(mine):
    whole = jnp.broadcast_to(mine[None], (DEVICES, *mine.shape))
    return lax.all_to_all(whole, ALL, 0, 0, tiled=True).reshape(-1, SEQ)


def column_order():
    source = lax.broadcasted_iota(jnp.int32, (1024, 1024), 0)
    target = lax.broadcasted_iota(jnp.int32, (1024, 1024), 1)
    lane = source % 128
    return (target == (lane // 32) * 256 + (source // 128) * 32 + lane % 32).astype(LOW)


def shards(
    tokens,
    cotangent,
    lengths,
    attn_weights,
    attn_rows,
    attn_cols,
    ffn_weights,
    ffn_rows,
    ffn_cols,
    down_weight,
    down_rows,
    down_cols,
    small_params,
    small_moments,
):
    core = lax.axis_index("c")
    deep = lax.axis_index("z")
    inputs = tokens.astype(WIDE)
    slot_ids = jnp.arange(SEQ, dtype=jnp.int32)
    valid_rows = slot_ids < lengths[0]
    gain_one, gain_two, query_gain, key_gain, forget_bias, forget_weight = split_small(small_params)

    device = ((lax.axis_index("x") * 4 + lax.axis_index("y")) * 4 + deep) * 2 + core
    forget_rows = lax.dynamic_slice_in_dim(forget_weight, device * 12, 12, axis=0)
    forget_rows = jnp.pad(forget_rows, ((0, 0), (0, SEQ - H)))
    attn_low = pack(lengths.astype(WIDE), attn_weights, forget_rows)
    attn_low = lax.all_to_all(attn_low, ZC, 0, 0, tiled=True)
    lengths_group = attn_low[:, 0, RAW - 1].astype(WIDE)
    attn_low = attn_low.reshape(96, RAW)
    attn_full = lax.all_gather(attn_low, XY, axis=0, tiled=True)
    order = column_order()
    pair_low = ffn_weights.astype(LOW).reshape(24, 4, 1024).transpose(1, 0, 2).reshape(96, 1024)
    pair_low = dot_right_t(pair_low, order).astype(LOW).reshape(4, 2, 12, GROUP, 128)
    pair_low = pair_low.transpose(3, 2, 1, 0, 4).reshape(GROUP, 12, 2 * FF_PART)
    pair_low = lax.all_to_all(pair_low, ZC, 0, 0, tiled=True).reshape(96, 2 * FF_PART)
    down_low = jnp.concatenate(
        [down_weight[:, at : at + 512].astype(LOW) for at in (0, 512, 1024)], axis=0
    )
    seed_grad = cotangent.astype(WIDE) * valid_rows[:, None].astype(WIDE)
    seed_grad, pair_low, down_low = fence(seed_grad, pair_low, down_low)
    seed_low = lax.all_gather(seed_grad.astype(LOW), ZC, axis=0, tiled=True)
    ffn_full = lax.all_gather(
        jnp.concatenate([pair_low, down_low], axis=1), XY, axis=0, tiled=True
    )

    inverse_one = inverse_rms(inputs)
    normed_one = inputs * inverse_one
    attn_low, attn_weights, ffn_weights, down_weight, small_params = fence(
        attn_low, attn_weights, ffn_weights, down_weight, small_params
    )
    tokens_group = gather_group(tokens)[0]
    inputs_group = tokens_group.astype(WIDE)
    inverse_group = inverse_rms(inputs_group)
    hidden_one = (inputs_group * inverse_group * gain_one).astype(LOW)
    place = 2 * deep + core

    lengths_group = jnp.broadcast_to(lengths_group[:, None, None], (GROUP, 1, SEQ))
    forget_low = lax.dynamic_slice_in_dim(forget_weight, place * OWN_HEADS, OWN_HEADS, axis=1)
    forget_low = forget_low.astype(LOW)
    bias_mine = lax.dynamic_slice_in_dim(forget_bias, place * OWN_HEADS, OWN_HEADS, axis=0)
    bias_tile = jnp.pad(bias_mine[None], ((0, 7), (HD, HD - OWN_HEADS)))
    exact = {"precision": lax.Precision.HIGHEST, "preferred_element_type": WIDE}
    slots = lax.broadcasted_iota(jnp.int32, (SEQ, SEQ), 0)
    later = (slots >= lax.broadcasted_iota(jnp.int32, (SEQ, SEQ), 1)).astype(WIDE)
    gains = jnp.concatenate([query_gain, key_gain])[None]
    gains = jnp.pad(gains, ((0, 7), (0, 0)))
    (
        attn_full,
        hidden_one,
        tokens_group,
        inverse_group,
        lengths_group,
        forget_low,
        bias_tile,
        gains,
        order,
    ) = fence(
        attn_full,
        hidden_one,
        tokens_group,
        inverse_group,
        lengths_group,
        forget_low,
        bias_tile,
        gains,
        order,
    )
    proj_full = attn_full[:, :OWN]
    raw, attn_full = fence(dot_plain(hidden_one, attn_full), attn_full)
    out_rows = attn_full[:, OWN : OWN + 3 * HD].reshape(GROUP, 3 * HD, 3 * HD)
    out_rows = lax.all_to_all(out_rows, ZC, 0, 0, tiled=True)
    gated_out, attended, prob = attend(raw, bias_tile, lengths_group, gains)
    out_rows = move_rows(spread_rows_kernel, out_rows, (WIDE_HEADS, D))
    mixed_part = dot_plain(gated_out, out_rows).astype(LOW).reshape(4, 2, SEQ, D)
    mixed_part = group_reduce_start(mixed_part, core, deep)
    half_one, half_two = fence(*far_halves(mixed_part))
    near_one, near_two, *held = fence(
        *near_blocks(mixed_part, (half_one, half_two)),
        small_params,
        small_moments,
        attn_weights,
        ffn_weights,
        down_weight,
        attn_rows,
        ffn_rows,
        down_rows,
    )
    small_params, small_moments, attn_weights, ffn_weights, down_weight = held[:5]
    attn_rows, ffn_rows, down_rows = held[5:]
    param_rows = small_rows(small_params, 0.0)
    moment_rows = small_rows(small_moments, 1.0)
    old_rows = (attn_rows[:, :, None], ffn_rows[:, :, None], down_rows[None, :, None])
    old_cols = (attn_cols, ffn_cols, down_cols[None])
    weight_sums = jnp.concatenate(
        [square_sum(attn_weights), square_sum(ffn_weights), square_sum(down_weight[None])]
    )
    mixed_sum = inputs + mixed_part[0] + near_one.astype(WIDE) + near_two.astype(WIDE)
    inverse_two = inverse_rms(mixed_sum)
    normed_two = mixed_sum * inverse_two
    hidden_two, ffn_full, seed_low, param_rows, moment_rows, old_rows, weight_sums = gather_group(
        (normed_two * gain_two).astype(LOW),
        ffn_full,
        seed_low,
        param_rows,
        moment_rows,
        old_rows,
        weight_sums,
    )
    pair_full = ffn_full[:, : 2 * FF_PART]
    down_full = ffn_full[:, 2 * FF_PART :].reshape(PLANE, 3, 32, 512)
    down_full = jnp.concatenate(
        [down_full[:, part].reshape(FF_PART, 512) for part in range(3)], axis=1
    )

    gate_full = pair_full[:, :FF_PART]
    up_full = pair_full[:, FF_PART:]
    gate_part = dot_plain(hidden_two, gate_full)
    up_part = dot_plain(hidden_two, up_full)
    gate_sig = lax.logistic(gate_part)
    activated = (gate_part * gate_sig * up_part).astype(LOW)
    activated_grad = dot_right_t(seed_low, down_full)
    silu_grad = activated_grad * up_part
    gate_part_grad = silu_grad * gate_sig + silu_grad * gate_part * gate_sig * (1.0 - gate_sig)
    gate_part_grad = gate_part_grad.astype(LOW)
    up_part_grad = (activated_grad * (gate_part * gate_sig)).astype(LOW)
    token_part = dot_right_t(gate_part_grad, gate_full) + dot_right_t(up_part_grad, up_full)
    token_part = token_part.astype(LOW).reshape(4, 2, SEQ, D)
    token_part, hidden_two, gate_part_grad, up_part_grad, activated, seed_low, down_full = fence(
        token_part, hidden_two, gate_part_grad, up_part_grad, activated, seed_low, down_full
    )
    token_got, gate_terms, hidden_two, up_part_grad, activated, seed_low = fence(
        swap_core(lax.dynamic_index_in_dim(token_part, 1 - core, 1, keepdims=False)),
        dot_left_t(hidden_two, gate_part_grad).astype(LOW),
        hidden_two,
        up_part_grad,
        activated,
        seed_low,
    )
    token_part = lax.dynamic_index_in_dim(token_part, core, 1, keepdims=False)
    token_part = token_part.astype(WIDE) + token_got.astype(WIDE)
    token_part, hidden_two, up_part_grad = fence(token_part, hidden_two, up_part_grad)
    token_part = [
        lax.dynamic_index_in_dim(token_part, (deep + step) % 4, 0, keepdims=False)
        for step in (0, 3, 1, 2)
    ]
    half_one, half_two, up_terms, down_terms, activated = fence(
        *far_halves(token_part),
        dot_left_t(hidden_two, up_part_grad).astype(LOW),
        dot_left_t(activated, seed_low).astype(LOW),
        activated,
    )
    down_terms = down_terms.reshape(PLANE, 32, D)
    ffn_terms = jnp.concatenate(
        [
            gate_terms.reshape(PLANE, 96, FF_PART),
            up_terms.reshape(PLANE, 96, FF_PART),
            down_terms[:, :, :512],
            down_terms[:, :, 512:1024],
            down_terms[:, :, 1024:],
        ],
        axis=1,
    )
    out_part = dot_plain(activated, down_full).astype(LOW).reshape(GROUP, SEQ, D)
    near_one, near_two, ffn_terms, out_part = fence(
        *near_blocks(token_part, (half_one, half_two)), ffn_terms, out_part
    )
    ffn_got = lax.all_to_all(ffn_terms, XY, 0, 0, tiled=True)
    hidden_two_grad = token_part[0] + near_one.astype(WIDE) + near_two.astype(WIDE)

    gain_two_grad = jnp.sum(normed_two * hidden_two_grad, axis=0)
    mixed_grad = seed_grad + norm_back(normed_two, inverse_two, hidden_two_grad * gain_two)
    mixed_low, out_part = gather_group(mixed_grad.astype(LOW), out_part)
    gated_grad = dot_right_t(mixed_low, out_rows)
    out_terms = dot_left_t(gated_out, mixed_low)
    out_terms = move_rows(collect_rows_kernel, out_terms, (PLANE, 24, OWN))
    gated_grad, out_terms = fence(gated_grad, out_terms)
    raw_grad, forget_sums, gain_sums = attend_back(raw, gated_grad, attended, prob, gains)
    out_terms, raw_grad, forget_sums, gain_sums = fence(
        out_terms, raw_grad, forget_sums, gain_sums
    )
    terms = jnp.concatenate(
        [
            dot_left_t(hidden_one, raw_grad).astype(LOW).reshape(PLANE, 96, OWN),
            out_terms,
        ],
        axis=1,
    )
    forget_arg = raw[:, OWN + 3 * HD : OWN + 3 * HD + OWN_HEADS] + bias_mine
    log_forget_grad = jnp.einsum(
        "bhu,ut->bth",
        forget_sums[:, :OWN_HEADS],
        later,
        **exact,
    ).reshape(GROUP * SEQ, OWN_HEADS)
    forget_arg_grad = log_forget_grad * (1.0 - lax.logistic(forget_arg))
    forget_low_grad = forget_arg_grad.astype(LOW)
    terms, raw_grad, ffn_got, forget_low_grad, forget_arg_grad = fence(
        terms, raw_grad, ffn_got, forget_low_grad, forget_arg_grad
    )
    terms = lax.all_to_all(terms, XY, 0, 0, tiled=True)
    ffn_sum = jnp.sum(ffn_got.astype(WIDE), axis=0).astype(LOW)

    raw_grad, token_weights, ffn_sum = fence(raw_grad, proj_full, ffn_sum)
    pair_back = lax.all_gather(ffn_sum[:192], ZC, axis=0, tiled=False)
    raw_grad, forget_low_grad, pair_back = fence(raw_grad, forget_low_grad, pair_back)
    token_part = dot_right_t(raw_grad, token_weights) + dot_right_t(
        forget_low_grad, forget_low
    )
    normed_group = tokens_group.astype(WIDE) * inverse_group
    gain_one_grad = jnp.sum(normed_group * token_part, axis=0)
    token_part = token_part.astype(LOW).reshape(GROUP, SEQ, D)
    head_ids = lax.broadcasted_iota(jnp.int32, (OWN_HEADS, H), 0) + OWN_HEADS * place
    own_heads = head_ids == lax.broadcasted_iota(jnp.int32, (OWN_HEADS, H), 1)
    forget_wide = dot_plain(forget_low_grad, own_heads.astype(LOW)).astype(LOW)
    forget_w_grad = dot_left_t(hidden_one, forget_wide).reshape(288, SEQ)
    forget_bias_grad = jnp.sum(
        jnp.where(own_heads, jnp.sum(forget_arg_grad, axis=0)[:, None], 0.0), axis=0
    )
    out_part, ffn_sum = fence(out_part, ffn_sum)
    hidden_one_grad = lax.psum_scatter(token_part, ZC, scatter_dimension=0, tiled=False)
    pair_back = pair_back.reshape(GROUP, 2, GROUP, 12, FF_PART)
    pair_back = lax.dynamic_index_in_dim(pair_back, place, 2, keepdims=False)
    pair_back = pair_back.reshape(GROUP, 2, 12, 4, 128).transpose(3, 1, 2, 0, 4).reshape(96, 1024)
    pair_back = dot_plain(pair_back, order)
    out_sum = lax.psum_scatter(out_part, ZC, scatter_dimension=0, tiled=False)
    hidden_one_grad = hidden_one_grad.astype(WIDE)
    forget_bias_grad = jnp.pad(forget_bias_grad, (0, SEQ - H))
    small_grads = jnp.concatenate([gain_one_grad, gain_two_grad, gain_sums[0], forget_bias_grad])
    small_grads = small_grads.reshape(26, SEQ)
    terms, pair_back, small_grads, forget_w_grad = fence(
        terms, pair_back, small_grads, forget_w_grad
    )
    attn_part = jnp.sum(terms.astype(WIDE), axis=0)
    out_part = jnp.concatenate([attn_part[96:108], attn_part[108:]], axis=1)
    out_part = lax.ppermute(
        out_part,
        ALL,
        [(GROUP * row + col, PLANE * col + row) for row in range(PLANE) for col in range(GROUP)],
    )
    attn_part = attn_part[:96].reshape(GROUP, 12, OWN)
    attn_part = lax.all_to_all(attn_part, ZC, 0, 0, tiled=True)
    *measured, flat = measure(
        weight_sums, attn_part, out_part, pair_back, ffn_sum, *old_rows, small_grads, forget_w_grad
    )
    grads, rows_new = measured[:3], measured[3:]
    flat = spread_back(spread_sum(flat))
    input_grad = mixed_grad + norm_back(normed_one, inverse_one, hidden_one_grad * gain_one)
    block_out = (mixed_sum + out_sum.astype(WIDE)).astype(LOW)
    fresh = finish(
        flat,
        grads,
        (attn_weights, ffn_weights, down_weight),
        rows_new,
        old_cols,
        param_rows,
        moment_rows,
    )
    attn_new, ffn_new, down_new, attn_copy, ffn_copy, down_copy = fresh[:6]
    attn_cols_new, ffn_cols_new, down_cols_new, small_new, moments_new = fresh[6:]
    return (
        block_out,
        input_grad,
        grads[0],
        attn_new,
        attn_copy,
        rows_new[0].reshape(5, 12),
        attn_cols_new,
        grads[1],
        ffn_new,
        ffn_copy,
        rows_new[1].reshape(2, 12),
        ffn_cols_new,
        grads[2],
        down_new,
        down_copy,
        rows_new[2].reshape(32),
        down_cols_new.reshape(D),
        small_vector(flat[FLAT_SMALL : FLAT_SMALL + 314]),
        small_vector(small_new),
        small_vector(moments_new),
    )


def solution(mesh):
    chips = Mesh(mesh.devices.reshape(4, 4, 4, 2), ALL)
    rows_first = P(ALL, None)
    rows_second = P(None, ALL, None)
    stat_rows = P(None, ALL)
    flat = P(ALL)
    whole = P()
    return jax.shard_map(
        shards,
        mesh=chips,
        in_specs=(
            rows_first,
            rows_first,
            flat,
            rows_second,
            stat_rows,
            whole,
            rows_second,
            stat_rows,
            whole,
            rows_first,
            flat,
            whole,
            whole,
            whole,
        ),
        out_specs=(
            rows_first,
            rows_first,
            rows_second,
            rows_second,
            rows_second,
            stat_rows,
            whole,
            rows_second,
            rows_second,
            rows_second,
            stat_rows,
            whole,
            rows_first,
            rows_first,
            rows_first,
            flat,
            whole,
            whole,
            whole,
            whole,
        ),
        check_vma=False,
    )
```
